128 devices in a mesh: pts: 128 (over x, y, z, core).
Axes of the slice: x: 4, y: 4, z: 4, core: 2. Of those that a mesh axis runs over, the one named last changes fastest.
Arguments:
- points: bfloat16 [49152, 128], P('pts'), may hold values from -5 to 5
- noise_var: float32 [49152], P('pts'), may hold values from 0.5 to 4
- right_side: float32 [49152, 32], P('pts'), may hold values from -8 to 8
Outputs:
- solution_field: float32 [49152, 32], P('pts')
- residual: float32 [49152, 32], P('pts')
The draws below stay inside these ranges and needn't reach their ends.
All inputs are finite; a program needn't handle non-finite values.
Results may differ from the reference program's by a relative error of at most 0.0075.
Values may be sent and summed in bfloat16 or wider, within the bound.
No kernel may reach another device: no remote copies, remote signals or barrier semaphores. Data moves between devices by JAX's collectives and lax.ppermute only.
A program may use at most 128 MiB of HBM per device.

```python
import math
import jax
import jax.numpy as jnp
from jax import lax

PTS_DEV = 384
FEAT = 128
COLS = 32
ITERS = 2
NPTS = 49152
N_PTS = 128


def draw_points(key, part):
    key = jax.random.fold_in(key, 11)
    freq_key = jax.random.fold_in(key, 0)
    phase_key = jax.random.fold_in(key, 1)
    place_key = jax.random.fold_in(key, 2)
    noise_key = jax.random.fold_in(key, 4)
    freq = 12.0 * jnp.clip(jax.random.normal(freq_key, (2, FEAT), jnp.float32), -4.0, 4.0)
    phase = jax.random.uniform(phase_key, (FEAT,), jnp.float32, -jnp.pi, jnp.pi)
    latent = jax.random.uniform(place_key, (NPTS, 2), jnp.float32)
    noise = 0.5 * jnp.clip(jax.random.normal(noise_key, (NPTS, FEAT), jnp.float32), -6.0, 6.0)
    angle = latent[:, 0:1] * freq[0][None, :] + latent[:, 1:2] * freq[1][None, :] + phase[None, :]
    return (2.0 * jnp.cos(angle) + noise).astype(jnp.bfloat16)


def draw_right_side(key, part):
    key = jax.random.fold_in(key, 7)
    place = jnp.arange(NPTS, dtype=jnp.float32)[:, None] / (NPTS - 1)
    base = jnp.clip(jax.random.normal(key, (NPTS, COLS), jnp.float32), -6.0, 6.0)
    scale = 1.0 + 0.75 * place
    return (0.75 * base * scale).astype(jnp.float32)


def block_levels(key, dims, shards, smallest, high):
    loudness = 1.0
    for dim, blocks in shards:
        heights = jax.random.uniform(jax.random.fold_in(jax.random.fold_in(key, 6), dim), (blocks,), jnp.float32, smallest / len(shards), high / len(shards))
        loudness = loudness * jnp.repeat(jnp.exp(heights), dims[dim] // blocks).reshape((-1,) + (1,) * (len(dims) - 1 - dim))
    return loudness


def setup_inputs(seed: int = 0) -> dict:
    keys = jax.random.split(jax.random.key(seed), 4)
    points = draw_points(jax.random.fold_in(keys[3], 71), 0)
    noise_var = jnp.clip(jnp.exp(math.log(4.0) - 2.0794415 * jax.random.uniform(keys[1], (NPTS,), jnp.float32) ** block_levels(keys[1], (NPTS,), ((0, 128),), -0.2, 0.2)), 0.5, 4.0)
    right_side = draw_right_side(jax.random.fold_in(keys[3], 71), 0)
    return {"points": points, "noise_var": noise_var, "right_side": right_side}


def kernel_rows(block, sq_block, points_f, sq_all):
    cross = jnp.dot(block, points_f.T, precision=lax.Precision.HIGHEST)
    dist = sq_block[:, None] + sq_all[None, :] - 2.0 * cross
    return jnp.exp(-dist / FEAT)


def apply_kernel(points_f, sq_all, noise_var, direction):
    dir_half = direction.astype(jnp.bfloat16)
    dir_full = lax.optimization_barrier(dir_half).astype(jnp.float32)
    blocks = points_f.reshape(N_PTS, PTS_DEV, FEAT)
    sq_blocks = sq_all.reshape(N_PTS, PTS_DEV)

    def one_block(items):
        block, sq_block = items
        kern = kernel_rows(block, sq_block, points_f, sq_all).astype(jnp.bfloat16)
        kern = lax.optimization_barrier(kern).astype(jnp.float32)
        return jnp.dot(kern, dir_full, precision=lax.Precision.HIGHEST)

    product = lax.map(one_block, (blocks, sq_blocks)).reshape(NPTS, COLS)
    return product + noise_var[:, None] * direction


def reference(points, noise_var, right_side):
    points_f = points.astype(jnp.float32)
    sq_all = jnp.sum(points_f * points_f, axis=1)
    solution_field = jnp.zeros_like(right_side)
    residual = right_side
    direction = right_side
    norm_now = jnp.sum(residual * residual, axis=0)
    for step in range(ITERS):
        image = apply_kernel(points_f, sq_all, noise_var, direction)
        alpha = norm_now / jnp.sum(direction * image, axis=0)
        solution_field = solution_field + alpha * direction
        residual = residual - alpha * image
        norm_next = jnp.sum(residual * residual, axis=0)
        direction = residual + (norm_next / norm_now) * direction
        norm_now = norm_next
    return solution_field, residual
```

```python
import functools
import math

import jax
import jax.numpy as jnp
from jax import lax
from jax.experimental import pallas as pl
from jax.experimental.pallas import tpu as pltpu
from jax.sharding import PartitionSpec as P

DEVICES = 128
NEAR_MASKS = (2, 8)
SIDE_MASKS = (6, 24)
LINE_MASKS = (32, 64)
CORE_MASK = 1
NEAR = 1 << len(NEAR_MASKS)
SIDE = 1 << len(SIDE_MASKS)
EVEN_LINES = (0, 1, 3, 2)
ODD_LINES = (0, 1, 2, 3)
TURNS = 4
CHIPS = SIDE * TURNS
PAIR = 2
UNROLL = 2
LANES = 128
CHUNK = 512
UNIT = 256
SPLITS = 3
LIMIT = 6 * 1024 * 1024
SMALL = 8 * 1024 * 1024
INSIDE = pl.BlockSpec(memory_space=pltpu.VMEM)


def scale_of(feats):
    return 2.0 / feats * math.log2(math.e)


def reach(masks, k):
    mask = 0
    for bit, step in enumerate(masks):
        if (k >> bit) & 1:
            mask ^= step
    return mask


def chip_groups():
    groups, seen = [], set()
    for base in range(DEVICES):
        if base not in seen:
            group = [base ^ reach(SIDE_MASKS + LINE_MASKS, k) for k in range(CHIPS)]
            groups.append(group)
            seen.update(group)
    return groups


def place_in_group(index):
    place = 0
    for bit, mask in enumerate(SIDE_MASKS + LINE_MASKS):
        place += lax.rem(lax.div(index, 1 << (mask.bit_length() - 1)), 2) << bit
    return place


def partner(value, even, odd=None):
    odd = even if odd is None else odd
    pairs = [(k, k ^ (odd if k & CORE_MASK else even)) for k in range(DEVICES)]
    return lax.ppermute(value, "pts", pairs)


def exchange(items, masks):
    return [items[0]] + [partner(items[k], reach(masks, k)) for k in range(1, len(items))]


def line_masks(turn):
    return reach(LINE_MASKS, EVEN_LINES[turn]), reach(SIDE_MASKS, ODD_LINES[turn])


def share(copies):
    return lax.all_to_all(copies, "pts", 0, 0, axis_index_groups=chip_groups())


def small_call(body, shapes, *args):
    return pl.pallas_call(
        body,
        in_specs=[INSIDE] * len(args),
        out_specs=[INSIDE] * len(shapes),
        out_shape=[jax.ShapeDtypeStruct(*shape) for shape in shapes],
        compiler_params=pltpu.CompilerParams(vmem_limit_bytes=SMALL),
    )(*args)


def half_norms(scale, block):
    ones = jnp.ones((8, block.shape[1]), jnp.bfloat16)
    dims = (((1,), (1,)), ((), ()))
    square = jnp.square(block.astype(jnp.float32))
    high = square.astype(jnp.bfloat16)
    low = (square - high.astype(jnp.float32)).astype(jnp.bfloat16)
    total = lax.dot_general(ones, high, dims, preferred_element_type=jnp.float32)
    total += lax.dot_general(ones, low, dims, preferred_element_type=jnp.float32)
    return total * (-0.5 * scale)


def first_product(scale, rows, turn, *refs):
    far_refs = refs[:2]
    near_ref, half_ref = refs[2:4]
    kern_ref, sum_ref, far_ref = refs[-3:]
    sum_ref[...] = jnp.zeros_like(sum_ref) if turn == 0 else refs[4][...]
    cols = sum_ref.shape[0]
    width = near_ref.shape[1]
    chunks = width // UNIT
    tall = rows + cols * (rows // near_ref.shape[0])
    for k, ref in enumerate(far_refs):
        far_ref[pl.ds(k * SIDE, SIDE)] = ref[...]
        for j in range(SIDE):
            sum_ref[:, width:] += ref[j, pl.ds(tall, cols), :].astype(jnp.float32)

    @pl.loop(0, far_ref.shape[0] // (PAIR * UNROLL))
    def _(step):
        units, far, vec, far_half, here = [], [], [], [], []
        for u in range(UNROLL):
            first = PAIR * (UNROLL * step + u)
            block = jnp.concatenate([far_ref[first + k, :rows, :] for k in range(PAIR)], axis=0)
            pieces = [
                far_ref[first + k, pl.ds(at, cols), :]
                for k in range(PAIR)
                for at in range(rows, tall, cols)
            ]
            block_f = block.astype(jnp.float32)
            far.append(block)
            vec.append(jnp.concatenate(pieces, axis=1))
            far_half.append(jnp.sum(block_f * block_f, axis=1, keepdims=True) * (-0.5 * scale))
            here.append(pl.ds(pl.multiple_of(first * rows, PAIR * rows), PAIR * rows))
            units += [(u, pl.ds(c * UNIT, UNIT)) for c in range(chunks)]
        cross, tile = {}, {}
        for c in range(len(units) + 2):
            if c < len(units):
                u, part = units[c]
                cross[c] = jnp.dot(far[u], near_ref[:, part], preferred_element_type=jnp.float32)
            if 0 <= c - 1 < len(units):
                u, part = units[c - 1]
                tile[c - 1] = jnp.exp2(
                    cross.pop(c - 1) * scale + far_half[u] + half_ref[0:1, part]
                ).astype(jnp.bfloat16)
                kern_ref[here[u], part] = tile[c - 1]
            if 0 <= c - 2 < len(units):
                u, part = units[c - 2]
                sum_ref[:, part] += jnp.dot(
                    vec[u], tile.pop(c - 2), preferred_element_type=jnp.float32
                )


def split_product(rows, sum_ref, *outs):
    for k, ref in enumerate(outs):
        ref[:, :rows] = sum_ref[:, pl.ds(k * rows, rows)]
        ref[:, rows:] = sum_ref[:, pl.ds(len(outs) * rows, LANES)]


def second_product(rows, core, *refs):
    kerns = refs[:TURNS]
    blocks_ref = refs[TURNS]
    vec_ref, total_ref = refs[-2:]
    index = lax.axis_index("pts")
    place = place_in_group(index)
    odd = lax.rem(index, 2)
    for n in range(TURNS):
        for side in range(SIDE):
            even_slot = side + SIDE * EVEN_LINES[n]
            odd_slot = SIDE * side + ODD_LINES[n]
            slot = jnp.bitwise_xor(place, jnp.where(odd == core, even_slot, odd_slot))
            vec_ref[n, :, pl.ds(side * rows, rows)] = blocks_ref[slot, :, pl.ds(0, rows)]
    half = pl.ds(core * SIDE * rows, SIDE * rows)
    for c in range(total_ref.shape[1] // CHUNK):
        part = pl.ds(c * CHUNK, CHUNK)
        value = jnp.zeros((total_ref.shape[0], CHUNK), jnp.float32)
        if core == 1:
            value = refs[TURNS + 1][:, part]
        for n, ref in enumerate(kerns):
            value += jnp.dot(vec_ref[n], ref[half, part], preferred_element_type=jnp.float32)
        total_ref[:, part] = value
    if core == 0:
        refs[-3][...] = total_ref[...]
    else:
        other_ref = refs[TURNS + 2]
        lanes = jnp.zeros((total_ref.shape[0], LANES), jnp.float32)
        for k in range(CHIPS):
            lanes += blocks_ref[k, :, rows:].astype(jnp.float32)
            lanes += other_ref[k, :, rows:].astype(jnp.float32)
        for k, ref in enumerate(refs[TURNS + 3 : TURNS + 3 + NEAR]):
            ref[:, :rows] = total_ref[:, pl.ds(k * rows, rows)]
            ref[:, rows:] = lanes


def run_first(turn, far, near, half, last, rows, cols):
    feats, width = near.shape
    inputs = list(far) + [near, half] + ([last] if turn > 0 else [])
    count = 2 * SIDE * rows
    return pl.pallas_call(
        functools.partial(first_product, scale_of(feats), rows, turn),
        in_specs=[INSIDE] * len(inputs),
        out_specs=[INSIDE, INSIDE],
        out_shape=[
            pltpu.VMEM((count, width), jnp.bfloat16),
            jax.ShapeDtypeStruct((cols, width + LANES), jnp.float32),
        ],
        scratch_shapes=[pltpu.VMEM((2 * SIDE,) + far[0].shape[1:], jnp.bfloat16)],
        compiler_params=pltpu.CompilerParams(vmem_limit_bytes=LIMIT),
        cost_estimate=pl.CostEstimate(
            flops=2 * count * width * 2 * feats,
            bytes_accessed=2 * count * width,
            transcendentals=count * width,
        ),
    )(*inputs)


def run_second(core, kerns, blocks, rows, *others):
    width = kerns[0].shape[1]
    cols = blocks.shape[1]
    kerns = [pltpu.with_memory_space_constraint(kern, pltpu.VMEM) for kern in kerns]
    inputs = kerns + [blocks] + list(others)
    if core == 0:
        outs = [jax.ShapeDtypeStruct((cols, width), jnp.float32)]
    else:
        outs = [jax.ShapeDtypeStruct((cols, rows + LANES), jnp.float32)] * NEAR
    return pl.pallas_call(
        functools.partial(second_product, rows, core),
        in_specs=[INSIDE] * len(inputs),
        out_specs=[INSIDE] * len(outs),
        out_shape=outs,
        scratch_shapes=[
            pltpu.VMEM((TURNS, cols, SIDE * rows), jnp.bfloat16),
            pltpu.VMEM((cols, width), jnp.float32),
        ],
        compiler_params=pltpu.CompilerParams(vmem_limit_bytes=LIMIT),
        cost_estimate=pl.CostEstimate(
            flops=2 * TURNS * SIDE * rows * width * 8 * cols,
            bytes_accessed=2 * TURNS * SIDE * rows * width,
            transcendentals=0,
        ),
    )(*inputs)


def spread_lanes(items, shape):
    lane = lax.broadcasted_iota(jnp.int32, shape, 1)
    lanes = jnp.zeros(shape, jnp.float32)
    for k, rest in enumerate(items):
        for j in range(SPLITS):
            piece = rest.astype(jnp.bfloat16).astype(jnp.float32)
            lanes = jnp.where(lane == SPLITS * k + j, piece, lanes)
            rest = rest - piece
    return lanes.astype(jnp.bfloat16)


def collect_lanes(lanes, count):
    lane = lax.broadcasted_iota(jnp.int32, lanes.shape, 1)
    items = []
    for k in range(count):
        inside = (lane >= SPLITS * k) & (lane < SPLITS * (k + 1))
        items.append(jnp.sum(jnp.where(inside, lanes, 0.0), axis=1, keepdims=True))
    return items


def row_sum(value):
    return jnp.sum(value, axis=1, keepdims=True)


def pack(points_ref, rhs_ref, noise_ref, out_ref, keep_ref, noisy_ref, sems):
    rows, feats = points_ref.shape
    cols = rhs_ref.shape[0]
    first = pltpu.make_async_copy(points_ref, out_ref.at[pl.ds(0, rows), :], sems.at[0])
    second = pltpu.make_async_copy(rhs_ref, keep_ref, sems.at[1])
    first.start()
    second.start()
    second.wait()
    for k in range(rows // feats):
        part = keep_ref[:, pl.ds(k * feats, feats)]
        out_ref[pl.ds(rows + k * cols, cols), :] = part.astype(jnp.bfloat16)
    rhs = keep_ref[...]
    noisy = noise_ref[...] * rhs
    noisy_ref[...] = noisy
    lanes = spread_lanes((row_sum(rhs * rhs), row_sum(rhs * noisy)), (cols, LANES))
    out_ref[pl.ds(rows + cols * (rows // feats), cols), :] = lanes
    first.wait()


def run_pack(points, rhs, noise):
    rows, feats = points.shape
    cols = rhs.shape[0]
    tall = rows + cols * (rows // feats) + cols
    place = pl.BlockSpec(memory_space=pl.ANY)
    return pl.pallas_call(
        pack,
        in_specs=[place, place, INSIDE],
        out_specs=[INSIDE] * 3,
        out_shape=[
            jax.ShapeDtypeStruct((tall, feats), points.dtype),
            jax.ShapeDtypeStruct(rhs.shape, rhs.dtype),
            jax.ShapeDtypeStruct(rhs.shape, rhs.dtype),
        ],
        scratch_shapes=[pltpu.SemaphoreType.DMA((2,))],
        compiler_params=pltpu.CompilerParams(vmem_limit_bytes=SMALL),
    )(points, rhs, noise)


def run_bundle(side, near):
    place = pl.BlockSpec(memory_space=pl.ANY)
    return pl.pallas_call(
        bundle,
        in_specs=[INSIDE] * len(side) + [place] * len(near),
        out_specs=INSIDE,
        out_shape=jax.ShapeDtypeStruct((len(side),) + side[0].shape, side[0].dtype),
        compiler_params=pltpu.CompilerParams(vmem_limit_bytes=SMALL),
    )(*side, *near)


def bundle(*refs):
    for k, ref in enumerate(refs[:SIDE]):
        refs[-1][k] = ref[...]


def prepare(scale, *refs):
    near_ref, half_ref = refs[NEAR:]
    rows = refs[0].shape[0]
    for k, ref in enumerate(refs[:NEAR]):
        block = ref[...]
        part = pl.ds(k * rows, rows)
        near_ref[:, part] = block.astype(jnp.float32).T.astype(jnp.bfloat16)
        half_ref[:, part] = half_norms(scale, block)


def middle(*refs):
    noisy_ref, rhs_ref, image_ref, rest_ref, known_ref, copies_ref = refs[NEAR:]
    rhs = rhs_ref[...]
    rows = rhs.shape[1]
    total = refs[0][...]
    for ref in refs[1:NEAR]:
        total += ref[...]
    norm, noisy_norm = collect_lanes(total[:, rows:], 2)
    shift = 1.0 + noisy_norm / norm
    image = total[:, :rows] + noisy_ref[...]
    rest = image - shift * rhs
    image_ref[...] = image
    rest_ref[...] = rest
    lane = lax.broadcasted_iota(jnp.int32, known_ref.shape, 1)
    known_ref[...] = jnp.where(lane == 0, norm, shift)
    lanes = spread_lanes((row_sum(rhs * rest), row_sum(rest * rest)), known_ref.shape)
    packed = jnp.concatenate([rest.astype(jnp.bfloat16), lanes], axis=1)
    for k in range(copies_ref.shape[0]):
        copies_ref[k] = packed


def closing(*refs):
    noise_ref, rhs_ref, image_ref, rest_ref, known_ref = refs[NEAR : NEAR + 5]
    field_ref, residual_ref, direction_ref, image_dir_ref, norm_ref, curve_ref = refs[NEAR + 5 :]
    rhs = rhs_ref[...]
    image = image_ref[...]
    rows = rhs.shape[1]
    total = refs[0][...]
    for ref in refs[1:NEAR]:
        total += ref[...]
    rest_image = total[:, :rows] + noise_ref[...] * rest_ref[...]
    cross, square = collect_lanes(total[:, rows:], 2)
    norm, shift = known_ref[:, 0:1], known_ref[:, 1:2]
    extra = cross / norm
    alpha = 1.0 / (shift + extra)
    norm_next = alpha * alpha * jnp.maximum(square - extra * cross, 0.0)
    beta = norm_next / norm
    residual = rhs - alpha * image
    direction = residual + beta * rhs
    image_dir = (alpha * extra + beta) * image - alpha * rest_image
    curve_two = row_sum(direction * image_dir)
    field_ref[...] = alpha * rhs
    residual_ref[...] = residual
    direction_ref[...] = direction
    image_dir_ref[...] = image_dir
    norm_ref[...] = jnp.broadcast_to(norm_next, norm_ref.shape)
    curve_ref[...] = jnp.broadcast_to(curve_two, norm_ref.shape).T


def finish(curve_ref, norm_ref, field_ref, residual_ref, direction_ref, image_dir_ref, *outs):
    cols = curve_ref.shape[1]
    curve = jnp.sum(curve_ref[...], axis=0, keepdims=True)
    curve = jnp.concatenate([curve, jnp.ones((1, LANES - cols), jnp.float32)], axis=1)
    curve = jnp.broadcast_to(curve, (LANES, LANES)).T[:cols, 0:1]
    alpha = norm_ref[:, 0:1] / curve
    outs[0][...] = field_ref[...] + alpha * direction_ref[...]
    outs[1][...] = residual_ref[...] - alpha * image_dir_ref[...]


def per_device(points, noise_var, right_side):
    rows, feats = points.shape
    noise = noise_var[None, :]
    packed, rhs, noisy = run_pack(points, right_side.T, noise)
    cols = rhs.shape[0]
    field_shape = ((cols, rows), jnp.float32)
    lanes_shape = ((cols, LANES), jnp.float32)
    side = [packed]
    for k in range(1, SIDE):
        side.append(partner(packed, reach(SIDE_MASKS, k), reach(LINE_MASKS, k)))
    near = exchange([points] * NEAR, NEAR_MASKS)
    own = run_bundle(side, near)
    first, second = [partner(own, *line_masks(turn)) for turn in (1, 2)]
    near, half = small_call(
        functools.partial(prepare, scale_of(feats)),
        [((feats, NEAR * rows), points.dtype), ((8, NEAR * rows), jnp.float32)],
        *near,
    )

    kerns = []
    kern, total = run_first(0, (own, partner(own, CORE_MASK)), near, half, None, rows, cols)
    kerns.append(kern)
    first, second, total = lax.optimization_barrier((first, second, total))
    third = partner(second, *line_masks(1))
    across = [partner(item, CORE_MASK) for item in (first, second)]
    kern, total = run_first(1, (first, across[0]), near, half, total, rows, cols)
    kerns.append(kern)
    kern, total = run_first(2, (second, across[1]), near, half, total, rows, cols)
    kerns.append(kern)
    third, total = lax.optimization_barrier((third, total))
    kern, total = run_first(3, (third, partner(third, CORE_MASK)), near, half, total, rows, cols)
    kerns.append(kern)
    wide_shape = ((cols, rows + LANES), jnp.float32)
    parts = small_call(functools.partial(split_product, rows), [wide_shape] * NEAR, total)
    image, rest, known, copies = small_call(
        middle,
        [field_shape, field_shape, lanes_shape, ((CHIPS, cols, rows + LANES), jnp.bfloat16)],
        *exchange(parts, NEAR_MASKS),
        noisy,
        rhs,
    )
    copies = share(copies)
    other = partner(copies, CORE_MASK)
    half_total = run_second(0, kerns, copies, rows)[0]
    parts = run_second(1, kerns, other, rows, half_total, copies)
    field, residual, direction, image_dir, norm_next, curve = small_call(
        closing,
        [field_shape] * 4 + [lanes_shape, ((DEVICES, cols), jnp.float32)],
        *exchange(parts, NEAR_MASKS),
        noise,
        rhs,
        image,
        rest,
        known,
    )
    curve = lax.all_to_all(curve[:, None, :], "pts", 0, 0).reshape(DEVICES, cols)
    field, residual = small_call(
        finish, [field_shape] * 2, curve, norm_next, field, residual, direction, image_dir
    )
    return (field.T, residual.T)


def solution(mesh):
    return jax.shard_map(
        per_device,
        mesh=mesh,
        in_specs=(P("pts", None), P("pts"), P("pts", None)),
        out_specs=(P("pts", None), P("pts", None)),
        check_vma=False,
    )
```

```python
import functools
import math

import jax
import jax.numpy as jnp
from jax import lax
from jax.experimental import pallas as pl
from jax.experimental.pallas import tpu as pltpu
from jax.sharding import PartitionSpec as P

DEVICES = 128
NEAR_MASKS = (2, 8)
SIDE_MASKS = (6, 24)
LINE_MASKS = (32, 64)
CORE_MASK = 1
NEAR = 1 << len(NEAR_MASKS)
SIDE = 1 << len(SIDE_MASKS)
EVEN_LINES = (0, 1, 3, 2)
ODD_LINES = (0, 1, 2, 3)
TURNS = 4
CHIPS = SIDE * TURNS
PAIR = 2
UNROLL = 2
LANES = 128
CHUNK = 512
UNIT = 256
SPLITS = 3
LIMIT = 6 * 1024 * 1024
SMALL = 8 * 1024 * 1024
INSIDE = pl.BlockSpec(memory_space=pltpu.VMEM)


def scale_of(feats):
    return 2.0 / feats * math.log2(math.e)


def reach(masks, k):
    mask = 0
    for bit, step in enumerate(masks):
        if (k >> bit) & 1:
            mask ^= step
    return mask


def chip_groups():
    groups, seen = [], set()
    for base in range(DEVICES):
        if base not in seen:
            group = [base ^ reach(SIDE_MASKS + LINE_MASKS, k) for k in range(CHIPS)]
            groups.append(group)
            seen.update(group)
    return groups


def place_in_group(index):
    place = 0
    for bit, mask in enumerate(SIDE_MASKS + LINE_MASKS):
        place += lax.rem(lax.div(index, 1 << (mask.bit_length() - 1)), 2) << bit
    return place


def partner(value, even, odd=None):
    odd = even if odd is None else odd
    pairs = [(k, k ^ (odd if k & CORE_MASK else even)) for k in range(DEVICES)]
    return lax.ppermute(value, "pts", pairs)


def exchange(items, masks):
    return [items[0]] + [partner(items[k], reach(masks, k)) for k in range(1, len(items))]


def line_masks(turn):
    return reach(LINE_MASKS, EVEN_LINES[turn]), reach(SIDE_MASKS, ODD_LINES[turn])


def share(copies):
    return lax.all_to_all(copies, "pts", 0, 0, axis_index_groups=chip_groups())


def small_call(body, shapes, *args):
    return pl.pallas_call(
        body,
        in_specs=[INSIDE] * len(args),
        out_specs=[INSIDE] * len(shapes),
        out_shape=[jax.ShapeDtypeStruct(*shape) for shape in shapes],
        compiler_params=pltpu.CompilerParams(vmem_limit_bytes=SMALL),
    )(*args)


def half_norms(scale, block):
    ones = jnp.ones((8, block.shape[1]), jnp.bfloat16)
    dims = (((1,), (1,)), ((), ()))
    square = jnp.square(block.astype(jnp.float32))
    high = square.astype(jnp.bfloat16)
    low = (square - high.astype(jnp.float32)).astype(jnp.bfloat16)
    total = lax.dot_general(ones, high, dims, preferred_element_type=jnp.float32)
    total += lax.dot_general(ones, low, dims, preferred_element_type=jnp.float32)
    return total * (-0.5 * scale)


def first_product(scale, rows, count, opening, ending, *refs):
    far_refs = refs[:count]
    near_ref, half_ref = refs[count : count + 2]
    kern_ref, sum_ref, far_ref = refs[count + 2 + (0 if opening else 1) :][:1] + refs[-2:]
    sum_ref[...] = jnp.zeros_like(sum_ref) if opening else refs[count + 2][...]
    cols = sum_ref.shape[0]
    width = near_ref.shape[1]
    chunks = width // UNIT
    tall = rows + cols * (rows // near_ref.shape[0])
    for k, ref in enumerate(far_refs):
        far_ref[pl.ds(k * SIDE, SIDE)] = ref[...]
        for j in range(SIDE):
            sum_ref[:, width:] += ref[j, pl.ds(tall, cols), :].astype(jnp.float32)

    @pl.loop(0, far_ref.shape[0] // (PAIR * UNROLL))
    def _(step):
        units, far, vec, far_half, here = [], [], [], [], []
        for u in range(UNROLL):
            first = PAIR * (UNROLL * step + u)
            block = jnp.concatenate([far_ref[first + k, :rows, :] for k in range(PAIR)], axis=0)
            pieces = [
                far_ref[first + k, pl.ds(at, cols), :]
                for k in range(PAIR)
                for at in range(rows, tall, cols)
            ]
            block_f = block.astype(jnp.float32)
            far.append(block)
            vec.append(jnp.concatenate(pieces, axis=1))
            far_half.append(jnp.sum(block_f * block_f, axis=1, keepdims=True) * (-0.5 * scale))
            here.append(pl.ds(pl.multiple_of(first * rows, PAIR * rows), PAIR * rows))
            units += [(u, pl.ds(c * UNIT, UNIT)) for c in range(chunks)]
        cross, tile = {}, {}
        for c in range(len(units) + 2):
            if c < len(units):
                u, part = units[c]
                cross[c] = jnp.dot(far[u], near_ref[:, part], preferred_element_type=jnp.float32)
            if 0 <= c - 1 < len(units):
                u, part = units[c - 1]
                tile[c - 1] = jnp.exp2(
                    cross.pop(c - 1) * scale + far_half[u] + half_ref[0:1, part]
                ).astype(jnp.bfloat16)
                kern_ref[here[u], part] = tile[c - 1]
            if 0 <= c - 2 < len(units):
                u, part = units[c - 2]
                sum_ref[:, part] += jnp.dot(
                    vec[u], tile.pop(c - 2), preferred_element_type=jnp.float32
                )

    if ending:
        for k, ref in enumerate(refs[-2 - NEAR : -2]):
            ref[:, :rows] = sum_ref[:, pl.ds(k * rows, rows)]
            ref[:, rows:] = sum_ref[:, width:]


def second_product(rows, core, starts, *refs):
    kerns = refs[:TURNS]
    blocks_ref = refs[TURNS]
    vec_ref, total_ref = refs[-2:]
    index = lax.axis_index("pts")
    place = place_in_group(index)
    odd = lax.rem(index, 2)
    for n in range(TURNS):
        for side in range(SIDE):
            even_slot = side + SIDE * EVEN_LINES[n]
            odd_slot = SIDE * side + ODD_LINES[n]
            slot = jnp.bitwise_xor(place, jnp.where(odd == core, even_slot, odd_slot))
            vec_ref[n, :, pl.ds(side * rows, rows)] = blocks_ref[slot, :, pl.ds(0, rows)]
    for c in range(total_ref.shape[1] // CHUNK):
        part = pl.ds(c * CHUNK, CHUNK)
        value = jnp.zeros((total_ref.shape[0], CHUNK), jnp.float32)
        if core == 1:
            value = refs[TURNS + 1][:, part]
        for n, ref in enumerate(kerns):
            tile = ref[pl.ds(starts[n], SIDE * rows), part]
            value += jnp.dot(vec_ref[n], tile, preferred_element_type=jnp.float32)
        total_ref[:, part] = value
    if core == 0:
        refs[-3][...] = total_ref[...]
    else:
        other_ref = refs[TURNS + 2]
        lanes = jnp.zeros((total_ref.shape[0], LANES), jnp.float32)
        for k in range(CHIPS):
            lanes += blocks_ref[k, :, rows:].astype(jnp.float32)
            lanes += other_ref[k, :, rows:].astype(jnp.float32)
        for k, ref in enumerate(refs[TURNS + 3 : TURNS + 3 + NEAR]):
            ref[:, :rows] = total_ref[:, pl.ds(k * rows, rows)]
            ref[:, rows:] = lanes


def run_first(far, near, half, last, rows, cols, ending=False):
    feats, width = near.shape
    opening = last is None
    inputs = list(far) + [near, half] + ([] if opening else [last])
    count = len(far) * SIDE * rows
    running = (cols, width + LANES)
    if ending:
        outs = [jax.ShapeDtypeStruct((cols, rows + LANES), jnp.float32)] * NEAR
        scratch = [pltpu.VMEM(running, jnp.float32)]
    else:
        outs = [jax.ShapeDtypeStruct(running, jnp.float32)]
        scratch = []
    return pl.pallas_call(
        functools.partial(first_product, scale_of(feats), rows, len(far), opening, ending),
        in_specs=[INSIDE] * len(inputs),
        out_specs=[INSIDE] * (1 + len(outs)),
        out_shape=[pltpu.VMEM((count, width), jnp.bfloat16)] + outs,
        scratch_shapes=scratch + [pltpu.VMEM((len(far) * SIDE,) + far[0].shape[1:], jnp.bfloat16)],
        compiler_params=pltpu.CompilerParams(vmem_limit_bytes=LIMIT),
        cost_estimate=pl.CostEstimate(
            flops=4 * count * width * feats,
            bytes_accessed=2 * count * width,
            transcendentals=count * width,
        ),
    )(*inputs)


def run_second(core, pieces, blocks, rows, *others):
    width = pieces[0][0].shape[1]
    cols = blocks.shape[1]
    starts = [start for _, start in pieces]
    kerns = [pltpu.with_memory_space_constraint(kern, pltpu.VMEM) for kern, _ in pieces]
    inputs = kerns + [blocks] + list(others)
    if core == 0:
        outs = [jax.ShapeDtypeStruct((cols, width), jnp.float32)]
    else:
        outs = [jax.ShapeDtypeStruct((cols, rows + LANES), jnp.float32)] * NEAR
    return pl.pallas_call(
        functools.partial(second_product, rows, core, starts),
        in_specs=[INSIDE] * len(inputs),
        out_specs=[INSIDE] * len(outs),
        out_shape=outs,
        scratch_shapes=[
            pltpu.VMEM((TURNS, cols, SIDE * rows), jnp.bfloat16),
            pltpu.VMEM((cols, width), jnp.float32),
        ],
        compiler_params=pltpu.CompilerParams(vmem_limit_bytes=LIMIT),
        cost_estimate=pl.CostEstimate(
            flops=2 * TURNS * SIDE * rows * width * 8 * cols,
            bytes_accessed=2 * TURNS * SIDE * rows * width,
            transcendentals=0,
        ),
    )(*inputs)


def spread_lanes(items, shape):
    lane = lax.broadcasted_iota(jnp.int32, shape, 1)
    lanes = jnp.zeros(shape, jnp.float32)
    for k, rest in enumerate(items):
        for j in range(SPLITS):
            piece = rest.astype(jnp.bfloat16).astype(jnp.float32)
            lanes = jnp.where(lane == SPLITS * k + j, piece, lanes)
            rest = rest - piece
    return lanes.astype(jnp.bfloat16)


def collect_lanes(lanes, count):
    lane = lax.broadcasted_iota(jnp.int32, lanes.shape, 1)
    items = []
    for k in range(count):
        inside = (lane >= SPLITS * k) & (lane < SPLITS * (k + 1))
        items.append(jnp.sum(jnp.where(inside, lanes, 0.0), axis=1, keepdims=True))
    return items


def row_sum(value):
    return jnp.sum(value, axis=1, keepdims=True)


def pack(points_ref, rhs_ref, noise_ref, out_ref, keep_ref, noisy_ref, sems):
    rows, feats = points_ref.shape
    cols = rhs_ref.shape[0]
    first = pltpu.make_async_copy(points_ref, out_ref.at[pl.ds(0, rows), :], sems.at[0])
    second = pltpu.make_async_copy(rhs_ref, keep_ref, sems.at[1])
    first.start()
    second.start()
    second.wait()
    for k in range(rows // feats):
        part = keep_ref[:, pl.ds(k * feats, feats)]
        out_ref[pl.ds(rows + k * cols, cols), :] = part.astype(jnp.bfloat16)
    rhs = keep_ref[...]
    noisy = noise_ref[...] * rhs
    noisy_ref[...] = noisy
    lanes = spread_lanes((row_sum(rhs * rhs), row_sum(rhs * noisy)), (cols, LANES))
    out_ref[pl.ds(rows + cols * (rows // feats), cols), :] = lanes
    first.wait()


def outside(value):
    return pltpu.with_memory_space_constraint(value, pltpu.HBM)


def run_pack(points, rhs, noise):
    rows, feats = points.shape
    cols = rhs.shape[0]
    tall = rows + cols * (rows // feats) + cols
    place = pl.BlockSpec(memory_space=pltpu.HBM)
    return pl.pallas_call(
        pack,
        in_specs=[place, place, INSIDE],
        out_specs=[INSIDE] * 3,
        out_shape=[
            jax.ShapeDtypeStruct((tall, feats), points.dtype),
            jax.ShapeDtypeStruct(rhs.shape, rhs.dtype),
            jax.ShapeDtypeStruct(rhs.shape, rhs.dtype),
        ],
        scratch_shapes=[pltpu.SemaphoreType.DMA((2,))],
        compiler_params=pltpu.CompilerParams(vmem_limit_bytes=SMALL),
    )(outside(points), outside(rhs), noise)


def run_bundle(side, near):
    place = pl.BlockSpec(memory_space=pl.ANY)
    return pl.pallas_call(
        bundle,
        in_specs=[INSIDE] * len(side) + [place] * len(near),
        out_specs=INSIDE,
        out_shape=jax.ShapeDtypeStruct((len(side),) + side[0].shape, side[0].dtype),
        compiler_params=pltpu.CompilerParams(vmem_limit_bytes=SMALL),
    )(*side, *near)


def bundle(*refs):
    for k, ref in enumerate(refs[:SIDE]):
        refs[-1][k] = ref[...]


def prepare(scale, *refs):
    near_ref, half_ref = refs[NEAR:]
    rows = refs[1].shape[0]
    for k, ref in enumerate(refs[:NEAR]):
        block = ref[:rows, :]
        part = pl.ds(k * rows, rows)
        near_ref[:, part] = block.astype(jnp.float32).T.astype(jnp.bfloat16)
        half_ref[:, part] = half_norms(scale, block)


def middle(*refs):
    noisy_ref, rhs_ref, image_ref, rest_ref, known_ref, copies_ref = refs[NEAR:]
    rhs = rhs_ref[...]
    rows = rhs.shape[1]
    total = refs[0][...]
    for ref in refs[1:NEAR]:
        total += ref[...]
    norm, noisy_norm = collect_lanes(total[:, rows:], 2)
    shift = 1.0 + noisy_norm / norm
    image = total[:, :rows] + noisy_ref[...]
    rest = image - shift * rhs
    image_ref[...] = image
    rest_ref[...] = rest
    lane = lax.broadcasted_iota(jnp.int32, known_ref.shape, 1)
    known_ref[...] = jnp.where(lane == 0, norm, shift)
    lanes = spread_lanes((row_sum(rhs * rest), row_sum(rest * rest)), known_ref.shape)
    packed = jnp.concatenate([rest.astype(jnp.bfloat16), lanes], axis=1)
    for k in range(copies_ref.shape[0]):
        copies_ref[k] = packed


def closing(*refs):
    noise_ref, rhs_ref, image_ref, rest_ref, known_ref = refs[NEAR : NEAR + 5]
    field_ref, residual_ref, direction_ref, image_dir_ref, norm_ref, curve_ref = refs[NEAR + 5 :]
    rhs = rhs_ref[...]
    image = image_ref[...]
    rows = rhs.shape[1]
    total = refs[0][...]
    for ref in refs[1:NEAR]:
        total += ref[...]
    rest_image = total[:, :rows] + noise_ref[...] * rest_ref[...]
    cross, square = collect_lanes(total[:, rows:], 2)
    norm, shift = known_ref[:, 0:1], known_ref[:, 1:2]
    extra = cross / norm
    alpha = 1.0 / (shift + extra)
    norm_next = alpha * alpha * jnp.maximum(square - extra * cross, 0.0)
    beta = norm_next / norm
    residual = rhs - alpha * image
    direction = residual + beta * rhs
    image_dir = (alpha * extra + beta) * image - alpha * rest_image
    curve_two = row_sum(direction * image_dir)
    field_ref[...] = alpha * rhs
    residual_ref[...] = residual
    direction_ref[...] = direction
    image_dir_ref[...] = image_dir
    norm_ref[...] = jnp.broadcast_to(norm_next, norm_ref.shape)
    curve_ref[...] = jnp.broadcast_to(curve_two, norm_ref.shape).T


def finish(curve_ref, norm_ref, field_ref, residual_ref, direction_ref, image_dir_ref, *outs):
    cols = curve_ref.shape[1]
    curve = jnp.sum(curve_ref[...], axis=0, keepdims=True)
    curve = jnp.concatenate([curve, jnp.ones((1, LANES - cols), jnp.float32)], axis=1)
    curve = jnp.broadcast_to(curve, (LANES, LANES)).T[:cols, 0:1]
    alpha = norm_ref[:, 0:1] / curve
    outs[0][...] = field_ref[...] + alpha * direction_ref[...]
    outs[1][...] = residual_ref[...] - alpha * image_dir_ref[...]


def per_device(points, noise_var, right_side):
    rows, feats = points.shape
    noise = noise_var[None, :]
    packed, rhs, noisy = run_pack(points, right_side.T, noise)
    cols = rhs.shape[0]
    field_shape = ((cols, rows), jnp.float32)
    lanes_shape = ((cols, LANES), jnp.float32)
    side = [packed]
    for k in range(1, SIDE):
        side.append(partner(packed, reach(SIDE_MASKS, k), reach(LINE_MASKS, k)))
    near = exchange([points] * NEAR, NEAR_MASKS)
    own = run_bundle(side, near[1:])
    own_across = partner(own, CORE_MASK)
    first, second = [partner(own, *line_masks(turn)) for turn in (1, 2)]
    near, half = small_call(
        functools.partial(prepare, scale_of(feats)),
        [((feats, NEAR * rows), points.dtype), ((8, NEAR * rows), jnp.float32)],
        packed,
        *near[1:],
    )

    def first_call(far, last, ending=False):
        return run_first(far, near, half, last, rows, cols, ending)

    across = own_across
    half_a, total = first_call([own], None)
    half_b, total = first_call([across], total)
    first, second, total = lax.optimization_barrier((first, second, total))
    third = partner(second, *line_masks(1))
    across = [partner(item, CORE_MASK) for item in (first, second)]
    pair_a, total = first_call([first, across[0]], total)
    pair_b, total = first_call([second, across[1]], total)
    third, total = lax.optimization_barrier((third, total))
    across = partner(third, CORE_MASK)
    half_c, total = first_call([third], total)
    half_d, *parts = first_call([across], total, True)
    skip = SIDE * rows
    own_pieces = [(half_a, 0), (pair_a, 0), (pair_b, 0), (half_c, 0)]
    other_pieces = [(half_b, 0), (pair_a, skip), (pair_b, skip), (half_d, 0)]

    image, rest, known, copies = small_call(
        middle,
        [field_shape, field_shape, lanes_shape, ((CHIPS, cols, rows + LANES), jnp.bfloat16)],
        *exchange(parts, NEAR_MASKS),
        noisy,
        rhs,
    )
    copies = share(copies)
    other = partner(copies, CORE_MASK)
    half_total = run_second(0, own_pieces, copies, rows)[0]
    parts = run_second(1, other_pieces, other, rows, half_total, copies)
    field, residual, direction, image_dir, norm_next, curve = small_call(
        closing,
        [field_shape] * 4 + [lanes_shape, ((DEVICES, cols), jnp.float32)],
        *exchange(parts, NEAR_MASKS),
        noise,
        rhs,
        image,
        rest,
        known,
    )
    curve = lax.all_to_all(curve[:, None, :], "pts", 0, 0).reshape(DEVICES, cols)
    field, residual = small_call(
        finish, [field_shape] * 2, curve, norm_next, field, residual, direction, image_dir
    )
    return (field.T, residual.T)


def solution(mesh):
    return jax.shard_map(
        per_device,
        mesh=mesh,
        in_specs=(P("pts", None), P("pts"), P("pts", None)),
        out_specs=(P("pts", None), P("pts", None)),
        check_vma=False,
    )
```

```python
import functools
import math

import jax
import jax.numpy as jnp
from jax import lax
from jax.experimental import pallas as pl
from jax.experimental.pallas import tpu as pltpu
from jax.sharding import PartitionSpec as P

DEVICES = 128
NEAR_MASKS = (10, 2)
SIDE_MASKS = (6, 24)
LINE_MASKS = (32, 64)
CORE_MASK = 1
NEAR = 1 << len(NEAR_MASKS)
SIDE = 1 << len(SIDE_MASKS)
EVEN_LINES = (0, 1, 3, 2)
ODD_LINES = (0, 1, 2, 3)
TURNS = 4
CHIPS = SIDE * TURNS
PAIR = 2
UNROLL = 2
LANES = 128
CHUNK = 512
UNIT = 256
SPLITS = 3
LIMIT = 6 * 1024 * 1024
SMALL = 8 * 1024 * 1024
INSIDE = pl.BlockSpec(memory_space=pltpu.VMEM)


def scale_of(feats):
    return 2.0 / feats * math.log2(math.e)


def reach(masks, k):
    mask = 0
    for bit, step in enumerate(masks):
        if (k >> bit) & 1:
            mask ^= step
    return mask


def chip_groups():
    groups, seen = [], set()
    for base in range(DEVICES):
        if base not in seen:
            group = [base ^ reach(SIDE_MASKS + LINE_MASKS, k) for k in range(CHIPS)]
            groups.append(group)
            seen.update(group)
    return groups


def place_in_group(index):
    place = 0
    for bit, mask in enumerate(SIDE_MASKS + LINE_MASKS):
        place += lax.rem(lax.div(index, 1 << (mask.bit_length() - 1)), 2) << bit
    return place


def partner(value, even, odd=None):
    odd = even if odd is None else odd
    pairs = [(k, k ^ (odd if k & CORE_MASK else even)) for k in range(DEVICES)]
    return lax.ppermute(value, "pts", pairs)


def exchange(items, masks):
    return [items[0]] + [partner(items[k], reach(masks, k)) for k in range(1, len(items))]


def line_masks(turn):
    return reach(LINE_MASKS, EVEN_LINES[turn]), reach(SIDE_MASKS, ODD_LINES[turn])


def share(copies):
    return lax.all_to_all(copies, "pts", 0, 0, axis_index_groups=chip_groups())


def small_call(body, shapes, *args):
    return pl.pallas_call(
        body,
        in_specs=[INSIDE] * len(args),
        out_specs=[INSIDE] * len(shapes),
        out_shape=[jax.ShapeDtypeStruct(*shape) for shape in shapes],
        compiler_params=pltpu.CompilerParams(vmem_limit_bytes=SMALL),
    )(*args)


def half_norms(scale, block):
    ones = jnp.ones((8, block.shape[1]), jnp.bfloat16)
    dims = (((1,), (1,)), ((), ()))
    square = jnp.square(block.astype(jnp.float32))
    high = square.astype(jnp.bfloat16)
    low = (square - high.astype(jnp.float32)).astype(jnp.bfloat16)
    total = lax.dot_general(ones, high, dims, preferred_element_type=jnp.float32)
    total += lax.dot_general(ones, low, dims, preferred_element_type=jnp.float32)
    return total * (-0.5 * scale)


def first_product(scale, rows, count, opening, ending, *refs):
    far_refs = refs[:count]
    near_ref, half_ref = refs[count : count + 2]
    kern_ref, sum_ref, far_ref = refs[count + 2 + (0 if opening else 1) :][:1] + refs[-2:]
    sum_ref[...] = jnp.zeros_like(sum_ref) if opening else refs[count + 2][...]
    cols = sum_ref.shape[0]
    width = near_ref.shape[1]
    chunks = width // UNIT
    tall = rows + cols * (rows // near_ref.shape[0])
    for k, ref in enumerate(far_refs):
        far_ref[pl.ds(k * SIDE, SIDE)] = ref[...]
        for j in range(SIDE):
            sum_ref[:, width:] += ref[j, pl.ds(tall, cols), :].astype(jnp.float32)

    @pl.loop(0, far_ref.shape[0] // (PAIR * UNROLL))
    def _(step):
        units, far, vec, far_half, here = [], [], [], [], []
        for u in range(UNROLL):
            first = PAIR * (UNROLL * step + u)
            block = jnp.concatenate([far_ref[first + k, :rows, :] for k in range(PAIR)], axis=0)
            pieces = [
                far_ref[first + k, pl.ds(at, cols), :]
                for k in range(PAIR)
                for at in range(rows, tall, cols)
            ]
            block_f = block.astype(jnp.float32)
            far.append(block)
            vec.append(jnp.concatenate(pieces, axis=1))
            far_half.append(jnp.sum(block_f * block_f, axis=1, keepdims=True) * (-0.5 * scale))
            here.append(pl.ds(pl.multiple_of(first * rows, PAIR * rows), PAIR * rows))
            units += [(u, pl.ds(c * UNIT, UNIT)) for c in range(chunks)]
        cross, tile = {}, {}
        for c in range(len(units) + 2):
            if c < len(units):
                u, part = units[c]
                cross[c] = jnp.dot(far[u], near_ref[:, part], preferred_element_type=jnp.float32)
            if 0 <= c - 1 < len(units):
                u, part = units[c - 1]
                tile[c - 1] = jnp.exp2(
                    cross.pop(c - 1) * scale + far_half[u] + half_ref[0:1, part]
                ).astype(jnp.bfloat16)
                kern_ref[here[u], part] = tile[c - 1]
            if 0 <= c - 2 < len(units):
                u, part = units[c - 2]
                sum_ref[:, part] += jnp.dot(
                    vec[u], tile.pop(c - 2), preferred_element_type=jnp.float32
                )

    if ending:
        for k, ref in enumerate(refs[-2 - NEAR : -2]):
            ref[:, :rows] = sum_ref[:, pl.ds(k * rows, rows)]
            ref[:, rows:] = sum_ref[:, width:]


def second_product(rows, core, starts, *refs):
    kerns = refs[:TURNS]
    blocks_ref = refs[TURNS]
    vec_ref, total_ref = refs[-2:]
    index = lax.axis_index("pts")
    place = place_in_group(index)
    odd = lax.rem(index, 2)
    for n in range(TURNS):
        for side in range(SIDE):
            even_slot = side + SIDE * EVEN_LINES[n]
            odd_slot = SIDE * side + ODD_LINES[n]
            slot = jnp.bitwise_xor(place, jnp.where(odd == core, even_slot, odd_slot))
            vec_ref[n, :, pl.ds(side * rows, rows)] = blocks_ref[slot, :, pl.ds(0, rows)]
    for c in range(total_ref.shape[1] // CHUNK):
        part = pl.ds(c * CHUNK, CHUNK)
        value = jnp.zeros((total_ref.shape[0], CHUNK), jnp.float32)
        if core == 1:
            value = refs[TURNS + 1][:, part]
        for n, ref in enumerate(kerns):
            tile = ref[pl.ds(starts[n], SIDE * rows), part]
            value += jnp.dot(vec_ref[n], tile, preferred_element_type=jnp.float32)
        total_ref[:, part] = value
    if core == 0:
        refs[-3][...] = total_ref[...]
    else:
        other_ref = refs[TURNS + 2]
        lanes = jnp.zeros((total_ref.shape[0], LANES), jnp.float32)
        for k in range(CHIPS):
            lanes += blocks_ref[k, :, rows:].astype(jnp.float32)
            lanes += other_ref[k, :, rows:].astype(jnp.float32)
        for k, ref in enumerate(refs[TURNS + 3 : TURNS + 3 + NEAR]):
            ref[:, :rows] = total_ref[:, pl.ds(k * rows, rows)]
            ref[:, rows:] = lanes


def run_first(far, near, half, last, rows, cols, ending=False):
    feats, width = near.shape
    opening = last is None
    inputs = list(far) + [near, half] + ([] if opening else [last])
    count = len(far) * SIDE * rows
    running = (cols, width + LANES)
    if ending:
        outs = [jax.ShapeDtypeStruct((cols, rows + LANES), jnp.float32)] * NEAR
        scratch = [pltpu.VMEM(running, jnp.float32)]
    else:
        outs = [jax.ShapeDtypeStruct(running, jnp.float32)]
        scratch = []
    return pl.pallas_call(
        functools.partial(first_product, scale_of(feats), rows, len(far), opening, ending),
        in_specs=[INSIDE] * len(inputs),
        out_specs=[INSIDE] * (1 + len(outs)),
        out_shape=[pltpu.VMEM((count, width), jnp.bfloat16)] + outs,
        scratch_shapes=scratch + [pltpu.VMEM((len(far) * SIDE,) + far[0].shape[1:], jnp.bfloat16)],
        compiler_params=pltpu.CompilerParams(vmem_limit_bytes=LIMIT),
        cost_estimate=pl.CostEstimate(
            flops=4 * count * width * feats,
            bytes_accessed=2 * count * width,
            transcendentals=count * width,
        ),
    )(*inputs)


def run_second(core, pieces, blocks, rows, *others):
    width = pieces[0][0].shape[1]
    cols = blocks.shape[1]
    starts = [start for _, start in pieces]
    kerns = [pltpu.with_memory_space_constraint(kern, pltpu.VMEM) for kern, _ in pieces]
    inputs = kerns + [blocks] + list(others)
    if core == 0:
        outs = [jax.ShapeDtypeStruct((cols, width), jnp.float32)]
    else:
        outs = [jax.ShapeDtypeStruct((cols, rows + LANES), jnp.float32)] * NEAR
    return pl.pallas_call(
        functools.partial(second_product, rows, core, starts),
        in_specs=[INSIDE] * len(inputs),
        out_specs=[INSIDE] * len(outs),
        out_shape=outs,
        scratch_shapes=[
            pltpu.VMEM((TURNS, cols, SIDE * rows), jnp.bfloat16),
            pltpu.VMEM((cols, width), jnp.float32),
        ],
        compiler_params=pltpu.CompilerParams(vmem_limit_bytes=LIMIT),
        cost_estimate=pl.CostEstimate(
            flops=2 * TURNS * SIDE * rows * width * 8 * cols,
            bytes_accessed=2 * TURNS * SIDE * rows * width,
            transcendentals=0,
        ),
    )(*inputs)


def spread_lanes(items, shape):
    lane = lax.broadcasted_iota(jnp.int32, shape, 1)
    lanes = jnp.zeros(shape, jnp.float32)
    for k, rest in enumerate(items):
        for j in range(SPLITS):
            piece = rest.astype(jnp.bfloat16).astype(jnp.float32)
            lanes = jnp.where(lane == SPLITS * k + j, piece, lanes)
            rest = rest - piece
    return lanes.astype(jnp.bfloat16)


def collect_lanes(lanes, count):
    lane = lax.broadcasted_iota(jnp.int32, lanes.shape, 1)
    items = []
    for k in range(count):
        inside = (lane >= SPLITS * k) & (lane < SPLITS * (k + 1))
        items.append(jnp.sum(jnp.where(inside, lanes, 0.0), axis=1, keepdims=True))
    return items


def row_sum(value):
    return jnp.sum(value, axis=1, keepdims=True)


def pack(points_ref, rhs_ref, noise_ref, out_ref, keep_ref, noisy_ref, row_ref, line_ref, sems):
    rows, feats = points_ref.shape
    cols = rhs_ref.shape[0]
    first = pltpu.make_async_copy(points_ref, out_ref.at[pl.ds(0, rows), :], sems.at[0])
    second = pltpu.make_async_copy(rhs_ref, keep_ref, sems.at[1])
    third = pltpu.make_async_copy(noise_ref, line_ref, sems.at[2])
    second.start()
    third.start()
    first.start()
    second.wait()
    for k in range(rows // feats):
        part = keep_ref[:, pl.ds(k * feats, feats)]
        out_ref[pl.ds(rows + k * cols, cols), :] = part.astype(jnp.bfloat16)
    rhs = keep_ref[...]
    third.wait()
    noise = line_ref[...].reshape(1, rows)
    row_ref[...] = noise
    noisy = noise * rhs
    noisy_ref[...] = noisy
    lanes = spread_lanes((row_sum(rhs * rhs), row_sum(rhs * noisy)), (cols, LANES))
    out_ref[pl.ds(rows + cols * (rows // feats), cols), :] = lanes
    first.wait()


def outside(value):
    return pltpu.with_memory_space_constraint(value, pltpu.HBM)


def run_pack(points, rhs, noise):
    rows, feats = points.shape
    cols = rhs.shape[0]
    tall = rows + cols * (rows // feats) + cols
    place = pl.BlockSpec(memory_space=pltpu.HBM)
    return pl.pallas_call(
        pack,
        in_specs=[place] * 3,
        out_specs=[INSIDE] * 4,
        out_shape=[
            jax.ShapeDtypeStruct((tall, feats), points.dtype),
            jax.ShapeDtypeStruct(rhs.shape, rhs.dtype),
            jax.ShapeDtypeStruct(rhs.shape, rhs.dtype),
            jax.ShapeDtypeStruct((1, rows), noise.dtype),
        ],
        scratch_shapes=[pltpu.VMEM((rows,), noise.dtype), pltpu.SemaphoreType.DMA((3,))],
        compiler_params=pltpu.CompilerParams(vmem_limit_bytes=SMALL),
    )(outside(points), outside(rhs), outside(noise))


def run_bundle(side, near):
    place = pl.BlockSpec(memory_space=pl.ANY)
    return pl.pallas_call(
        bundle,
        in_specs=[INSIDE] * len(side) + [place] * len(near),
        out_specs=INSIDE,
        out_shape=jax.ShapeDtypeStruct((len(side),) + side[0].shape, side[0].dtype),
        compiler_params=pltpu.CompilerParams(vmem_limit_bytes=SMALL),
    )(*side, *near)


def bundle(*refs):
    for k, ref in enumerate(refs[:SIDE]):
        refs[-1][k] = ref[...]


def prepare(scale, *refs):
    near_ref, half_ref = refs[NEAR:]
    rows = refs[1].shape[0]
    for k, ref in enumerate(refs[:NEAR]):
        block = ref[:rows, :]
        part = pl.ds(k * rows, rows)
        near_ref[:, part] = block.astype(jnp.float32).T.astype(jnp.bfloat16)
        half_ref[:, part] = half_norms(scale, block)


def middle(*refs):
    noisy_ref, rhs_ref, image_ref, rest_ref, known_ref, copies_ref = refs[NEAR:]
    rhs = rhs_ref[...]
    rows = rhs.shape[1]
    total = refs[0][...]
    for ref in refs[1:NEAR]:
        total += ref[...]
    norm, noisy_norm = collect_lanes(total[:, rows:], 2)
    shift = 1.0 + noisy_norm / norm
    image = total[:, :rows] + noisy_ref[...]
    rest = image - shift * rhs
    image_ref[...] = image
    rest_ref[...] = rest
    lane = lax.broadcasted_iota(jnp.int32, known_ref.shape, 1)
    known_ref[...] = jnp.where(lane == 0, norm, shift)
    lanes = spread_lanes((row_sum(rhs * rest), row_sum(rest * rest)), known_ref.shape)
    packed = jnp.concatenate([rest.astype(jnp.bfloat16), lanes], axis=1)
    for k in range(copies_ref.shape[0]):
        copies_ref[k] = packed


def closing(*refs):
    noise_ref, rhs_ref, image_ref, rest_ref, known_ref = refs[NEAR : NEAR + 5]
    field_ref, residual_ref, direction_ref, image_dir_ref, norm_ref, curve_ref = refs[NEAR + 5 :]
    rhs = rhs_ref[...]
    image = image_ref[...]
    rows = rhs.shape[1]
    total = refs[0][...]
    for ref in refs[1:NEAR]:
        total += ref[...]
    rest_image = total[:, :rows] + noise_ref[...] * rest_ref[...]
    cross, square = collect_lanes(total[:, rows:], 2)
    norm, shift = known_ref[:, 0:1], known_ref[:, 1:2]
    extra = cross / norm
    alpha = 1.0 / (shift + extra)
    norm_next = alpha * alpha * jnp.maximum(square - extra * cross, 0.0)
    beta = norm_next / norm
    residual = rhs - alpha * image
    direction = residual + beta * rhs
    image_dir = (alpha * extra + beta) * image - alpha * rest_image
    curve_two = row_sum(direction * image_dir)
    field_ref[...] = alpha * rhs
    residual_ref[...] = residual
    direction_ref[...] = direction
    image_dir_ref[...] = image_dir
    norm_ref[...] = jnp.broadcast_to(norm_next, norm_ref.shape)
    curve_ref[...] = jnp.broadcast_to(curve_two, norm_ref.shape).T


def finish(curve_ref, norm_ref, field_ref, residual_ref, direction_ref, image_dir_ref, *outs):
    cols = curve_ref.shape[1]
    curve = jnp.sum(curve_ref[...], axis=0, keepdims=True)
    curve = jnp.concatenate([curve, jnp.ones((1, LANES - cols), jnp.float32)], axis=1)
    curve = jnp.broadcast_to(curve, (LANES, LANES)).T[:cols, 0:1]
    alpha = norm_ref[:, 0:1] / curve
    outs[0][...] = field_ref[...] + alpha * direction_ref[...]
    outs[1][...] = residual_ref[...] - alpha * image_dir_ref[...]


def per_device(points, noise_var, right_side):
    rows, feats = points.shape
    packed, rhs, noisy, noise = run_pack(points, right_side.T, noise_var)
    cols = rhs.shape[0]
    field_shape = ((cols, rows), jnp.float32)
    lanes_shape = ((cols, LANES), jnp.float32)
    side = [packed]
    for k in range(1, SIDE):
        side.append(partner(packed, reach(SIDE_MASKS, k), reach(LINE_MASKS, k)))
    near = exchange([points] * NEAR, NEAR_MASKS)
    own = run_bundle(side, near[1:])
    own_across = partner(own, CORE_MASK)
    first, second = [partner(own, *line_masks(turn)) for turn in (1, 2)]
    near, half = small_call(
        functools.partial(prepare, scale_of(feats)),
        [((feats, NEAR * rows), points.dtype), ((8, NEAR * rows), jnp.float32)],
        packed,
        *near[1:],
    )

    def first_call(far, last, ending=False):
        return run_first(far, near, half, last, rows, cols, ending)

    across = own_across
    half_a, total = first_call([own], None)
    half_b, total = first_call([across], total)
    first, second, total = lax.optimization_barrier((first, second, total))
    third = partner(second, *line_masks(1))
    across = [partner(item, CORE_MASK) for item in (first, second)]
    pair_a, total = first_call([first, across[0]], total)
    pair_b, total = first_call([second, across[1]], total)
    third, total = lax.optimization_barrier((third, total))
    across = partner(third, CORE_MASK)
    half_c, total = first_call([third], total)
    half_d, *parts = first_call([across], total, True)
    skip = SIDE * rows
    own_pieces = [(half_a, 0), (pair_a, 0), (pair_b, 0), (half_c, 0)]
    other_pieces = [(half_b, 0), (pair_a, skip), (pair_b, skip), (half_d, 0)]

    image, rest, known, copies = small_call(
        middle,
        [field_shape, field_shape, lanes_shape, ((CHIPS, cols, rows + LANES), jnp.bfloat16)],
        *exchange(parts, NEAR_MASKS),
        noisy,
        rhs,
    )
    copies = share(copies)
    other = partner(copies, CORE_MASK)
    half_total = run_second(0, own_pieces, copies, rows)[0]
    parts = run_second(1, other_pieces, other, rows, half_total, copies)
    field, residual, direction, image_dir, norm_next, curve = small_call(
        closing,
        [field_shape] * 4 + [lanes_shape, ((DEVICES, cols), jnp.float32)],
        *exchange(parts, NEAR_MASKS),
        noise,
        rhs,
        image,
        rest,
        known,
    )
    curve = lax.all_to_all(curve[:, None, :], "pts", 0, 0).reshape(DEVICES, cols)
    field, residual = small_call(
        finish, [field_shape] * 2, curve, norm_next, field, residual, direction, image_dir
    )
    return (field.T, residual.T)


def solution(mesh):
    return jax.shard_map(
        per_device,
        mesh=mesh,
        in_specs=(P("pts", None), P("pts"), P("pts", None)),
        out_specs=(P("pts", None), P("pts", None)),
        check_vma=False,
    )
```

```python
import functools
import math

import jax
import jax.numpy as jnp
from jax import lax
from jax.experimental import pallas as pl
from jax.experimental.pallas import tpu as pltpu
from jax.sharding import PartitionSpec as P

DEVICES = 128
NEAR_MASKS = (10, 2)
SIDE_MASKS = (6, 24)
LINE_MASKS = (32, 64)
CORE_MASK = 1
NEAR = 1 << len(NEAR_MASKS)
SIDE = 1 << len(SIDE_MASKS)
EVEN_LINES = (0, 1, 3, 2)
ODD_LINES = (0, 1, 2, 3)
TURNS = 4
CHIPS = SIDE * TURNS
PAIR = 2
UNROLL = 2
LANES = 128
CHUNK = 512
UNIT = 256
SPLITS = 3
LIMIT = 6 * 1024 * 1024
SMALL = 8 * 1024 * 1024
INSIDE = pl.BlockSpec(memory_space=pltpu.VMEM)


def scale_of(feats):
    return 2.0 / feats * math.log2(math.e)


def reach(masks, k):
    mask = 0
    for bit, step in enumerate(masks):
        if (k >> bit) & 1:
            mask ^= step
    return mask


def chip_groups():
    groups, seen = [], set()
    for base in range(DEVICES):
        if base not in seen:
            group = [base ^ reach(SIDE_MASKS + LINE_MASKS, k) for k in range(CHIPS)]
            groups.append(group)
            seen.update(group)
    return groups


def place_in_group(index):
    place = 0
    for bit, mask in enumerate(SIDE_MASKS + LINE_MASKS):
        place += lax.rem(lax.div(index, 1 << (mask.bit_length() - 1)), 2) << bit
    return place


def partner(value, even, odd=None):
    odd = even if odd is None else odd
    pairs = [(k, k ^ (odd if k & CORE_MASK else even)) for k in range(DEVICES)]
    return lax.ppermute(value, "pts", pairs)


def exchange(items, masks):
    return [items[0]] + [partner(items[k], reach(masks, k)) for k in range(1, len(items))]


def line_masks(turn):
    return reach(LINE_MASKS, EVEN_LINES[turn]), reach(SIDE_MASKS, ODD_LINES[turn])


def share(copies):
    return lax.all_to_all(copies, "pts", 0, 0, axis_index_groups=chip_groups())


def small_call(body, shapes, *args):
    return pl.pallas_call(
        body,
        in_specs=[INSIDE] * len(args),
        out_specs=[INSIDE] * len(shapes),
        out_shape=[jax.ShapeDtypeStruct(*shape) for shape in shapes],
        compiler_params=pltpu.CompilerParams(vmem_limit_bytes=SMALL),
    )(*args)


def half_norms(scale, block):
    ones = jnp.ones((8, block.shape[1]), jnp.bfloat16)
    dims = (((1,), (1,)), ((), ()))
    square = jnp.square(block.astype(jnp.float32))
    high = square.astype(jnp.bfloat16)
    low = (square - high.astype(jnp.float32)).astype(jnp.bfloat16)
    total = lax.dot_general(ones, high, dims, preferred_element_type=jnp.float32)
    total += lax.dot_general(ones, low, dims, preferred_element_type=jnp.float32)
    return total * (-0.5 * scale)


def first_product(scale, rows, count, opening, ending, *refs):
    far_refs = refs[:count]
    near_ref, half_ref = refs[count : count + 2]
    kern_ref, sum_ref, far_ref = refs[count + 2 + (0 if opening else 1) :][:1] + refs[-2:]
    sum_ref[...] = jnp.zeros_like(sum_ref) if opening else refs[count + 2][...]
    cols = sum_ref.shape[0]
    width = near_ref.shape[1]
    chunks = width // UNIT
    tall = rows + cols * (rows // near_ref.shape[0])
    for k, ref in enumerate(far_refs):
        far_ref[pl.ds(k * SIDE, SIDE)] = ref[...]
        for j in range(SIDE):
            sum_ref[:, width:] += ref[j, pl.ds(tall, cols), :].astype(jnp.float32)

    @pl.loop(0, far_ref.shape[0] // (PAIR * UNROLL))
    def _(step):
        units, far, vec, far_half, here = [], [], [], [], []
        for u in range(UNROLL):
            first = PAIR * (UNROLL * step + u)
            block = jnp.concatenate([far_ref[first + k, :rows, :] for k in range(PAIR)], axis=0)
            pieces = [
                far_ref[first + k, pl.ds(at, cols), :]
                for k in range(PAIR)
                for at in range(rows, tall, cols)
            ]
            block_f = block.astype(jnp.float32)
            far.append(block)
            vec.append(jnp.concatenate(pieces, axis=1))
            far_half.append(jnp.sum(block_f * block_f, axis=1, keepdims=True) * (-0.5 * scale))
            here.append(pl.ds(pl.multiple_of(first * rows, PAIR * rows), PAIR * rows))
            units += [(u, pl.ds(c * UNIT, UNIT)) for c in range(chunks)]
        cross, tile = {}, {}
        for c in range(len(units) + 2):
            if c < len(units):
                u, part = units[c]
                cross[c] = jnp.dot(far[u], near_ref[:, part], preferred_element_type=jnp.float32)
            if 0 <= c - 1 < len(units):
                u, part = units[c - 1]
                tile[c - 1] = jnp.exp2(
                    cross.pop(c - 1) * scale + far_half[u] + half_ref[0:1, part]
                ).astype(jnp.bfloat16)
                kern_ref[here[u], part] = tile[c - 1]
            if 0 <= c - 2 < len(units):
                u, part = units[c - 2]
                sum_ref[:, part] += jnp.dot(
                    vec[u], tile.pop(c - 2), preferred_element_type=jnp.float32
                )

    if ending:
        for k, ref in enumerate(refs[-2 - NEAR : -2]):
            ref[:, :rows] = sum_ref[:, pl.ds(k * rows, rows)]
            ref[:, rows:] = sum_ref[:, width:]


def second_product(rows, core, starts, *refs):
    kerns = refs[:TURNS]
    blocks_ref = refs[TURNS]
    vec_ref, total_ref = refs[-2:]
    cols = total_ref.shape[0]
    index = lax.axis_index("pts")
    place = place_in_group(index)
    odd = lax.rem(index, 2)
    for n in range(TURNS):
        for side in range(SIDE):
            even_slot = side + SIDE * EVEN_LINES[n]
            odd_slot = SIDE * side + ODD_LINES[n]
            slot = jnp.bitwise_xor(place, jnp.where(odd == core, even_slot, odd_slot))
            part = pl.ds(side * rows, rows)
            vec_ref[n, :cols, part] = blocks_ref[slot, :, pl.ds(0, rows)]
            vec_ref[n, cols:, part] = blocks_ref[slot, :, pl.ds(rows, rows)]
    for c in range(total_ref.shape[1] // CHUNK):
        part = pl.ds(c * CHUNK, CHUNK)
        value = jnp.zeros((2 * cols, CHUNK), jnp.float32)
        for n, ref in enumerate(kerns):
            tile = ref[pl.ds(starts[n], SIDE * rows), part]
            value += jnp.dot(vec_ref[n], tile, preferred_element_type=jnp.float32)
        value = value[:cols] + value[cols:]
        if core == 1:
            value += refs[TURNS + 1][:, part]
        total_ref[:, part] = value
    if core == 0:
        refs[-3][...] = total_ref[...]
    else:
        other_ref = refs[TURNS + 2]
        lanes = jnp.zeros((total_ref.shape[0], LANES), jnp.float32)
        for k in range(CHIPS):
            lanes += blocks_ref[k, :, 2 * rows :].astype(jnp.float32)
            lanes += other_ref[k, :, 2 * rows :].astype(jnp.float32)
        for k, ref in enumerate(refs[TURNS + 3 : TURNS + 3 + NEAR]):
            ref[:, :rows] = total_ref[:, pl.ds(k * rows, rows)]
            ref[:, rows:] = lanes


def run_first(far, near, half, last, rows, cols, ending=False):
    feats, width = near.shape
    opening = last is None
    inputs = list(far) + [near, half] + ([] if opening else [last])
    count = len(far) * SIDE * rows
    running = (cols, width + LANES)
    if ending:
        outs = [jax.ShapeDtypeStruct((cols, rows + LANES), jnp.float32)] * NEAR
        scratch = [pltpu.VMEM(running, jnp.float32)]
    else:
        outs = [jax.ShapeDtypeStruct(running, jnp.float32)]
        scratch = []
    return pl.pallas_call(
        functools.partial(first_product, scale_of(feats), rows, len(far), opening, ending),
        in_specs=[INSIDE] * len(inputs),
        out_specs=[INSIDE] * (1 + len(outs)),
        out_shape=[pltpu.VMEM((count, width), jnp.bfloat16)] + outs,
        scratch_shapes=scratch + [pltpu.VMEM((len(far) * SIDE,) + far[0].shape[1:], jnp.bfloat16)],
        compiler_params=pltpu.CompilerParams(vmem_limit_bytes=LIMIT),
        cost_estimate=pl.CostEstimate(
            flops=4 * count * width * feats,
            bytes_accessed=2 * count * width,
            transcendentals=count * width,
        ),
    )(*inputs)


def run_second(core, pieces, blocks, rows, *others):
    width = pieces[0][0].shape[1]
    cols = blocks.shape[1]
    starts = [start for _, start in pieces]
    kerns = [pltpu.with_memory_space_constraint(kern, pltpu.VMEM) for kern, _ in pieces]
    inputs = kerns + [blocks] + list(others)
    if core == 0:
        outs = [jax.ShapeDtypeStruct((cols, width), jnp.float32)]
    else:
        outs = [jax.ShapeDtypeStruct((cols, rows + LANES), jnp.float32)] * NEAR
    return pl.pallas_call(
        functools.partial(second_product, rows, core, starts),
        in_specs=[INSIDE] * len(inputs),
        out_specs=[INSIDE] * len(outs),
        out_shape=outs,
        scratch_shapes=[
            pltpu.VMEM((TURNS, 2 * cols, SIDE * rows), jnp.bfloat16),
            pltpu.VMEM((cols, width), jnp.float32),
        ],
        compiler_params=pltpu.CompilerParams(vmem_limit_bytes=LIMIT),
        cost_estimate=pl.CostEstimate(
            flops=2 * TURNS * SIDE * rows * width * 8 * cols,
            bytes_accessed=2 * TURNS * SIDE * rows * width,
            transcendentals=0,
        ),
    )(*inputs)


def spread_lanes(items, shape):
    lane = lax.broadcasted_iota(jnp.int32, shape, 1)
    lanes = jnp.zeros(shape, jnp.float32)
    for k, rest in enumerate(items):
        for j in range(SPLITS):
            piece = rest.astype(jnp.bfloat16).astype(jnp.float32)
            lanes = jnp.where(lane == SPLITS * k + j, piece, lanes)
            rest = rest - piece
    return lanes.astype(jnp.bfloat16)


def collect_lanes(lanes, count):
    lane = lax.broadcasted_iota(jnp.int32, lanes.shape, 1)
    items = []
    for k in range(count):
        inside = (lane >= SPLITS * k) & (lane < SPLITS * (k + 1))
        items.append(jnp.sum(jnp.where(inside, lanes, 0.0), axis=1, keepdims=True))
    return items


def row_sum(value):
    return jnp.sum(value, axis=1, keepdims=True)


def pack(points_ref, rhs_ref, noise_ref, out_ref, keep_ref, noisy_ref, row_ref, line_ref, sems):
    rows, feats = points_ref.shape
    cols = rhs_ref.shape[0]
    first = pltpu.make_async_copy(points_ref, out_ref.at[pl.ds(0, rows), :], sems.at[0])
    second = pltpu.make_async_copy(rhs_ref, keep_ref, sems.at[1])
    third = pltpu.make_async_copy(noise_ref, line_ref, sems.at[2])
    second.start()
    third.start()
    first.start()
    second.wait()
    for k in range(rows // feats):
        part = keep_ref[:, pl.ds(k * feats, feats)]
        out_ref[pl.ds(rows + k * cols, cols), :] = part.astype(jnp.bfloat16)
    rhs = keep_ref[...]
    third.wait()
    noise = line_ref[...].reshape(1, rows)
    row_ref[...] = noise
    noisy = noise * rhs
    noisy_ref[...] = noisy
    lanes = spread_lanes((row_sum(rhs * rhs), row_sum(rhs * noisy)), (cols, LANES))
    out_ref[pl.ds(rows + cols * (rows // feats), cols), :] = lanes
    first.wait()


def outside(value):
    return pltpu.with_memory_space_constraint(value, pltpu.HBM)


def run_pack(points, rhs, noise):
    rows, feats = points.shape
    cols = rhs.shape[0]
    tall = rows + cols * (rows // feats) + cols
    place = pl.BlockSpec(memory_space=pltpu.HBM)
    return pl.pallas_call(
        pack,
        in_specs=[place] * 3,
        out_specs=[INSIDE] * 4,
        out_shape=[
            jax.ShapeDtypeStruct((tall, feats), points.dtype),
            jax.ShapeDtypeStruct(rhs.shape, rhs.dtype),
            jax.ShapeDtypeStruct(rhs.shape, rhs.dtype),
            jax.ShapeDtypeStruct((1, rows), noise.dtype),
        ],
        scratch_shapes=[pltpu.VMEM((rows,), noise.dtype), pltpu.SemaphoreType.DMA((3,))],
        compiler_params=pltpu.CompilerParams(vmem_limit_bytes=SMALL),
    )(outside(points), outside(rhs), outside(noise))


def run_bundle(side, near):
    place = pl.BlockSpec(memory_space=pl.ANY)
    return pl.pallas_call(
        bundle,
        in_specs=[INSIDE] * len(side) + [place] * len(near),
        out_specs=INSIDE,
        out_shape=jax.ShapeDtypeStruct((len(side),) + side[0].shape, side[0].dtype),
        compiler_params=pltpu.CompilerParams(vmem_limit_bytes=SMALL),
    )(*side, *near)


def bundle(*refs):
    for k, ref in enumerate(refs[:SIDE]):
        refs[-1][k] = ref[...]


def prepare(scale, *refs):
    near_ref, half_ref = refs[NEAR:]
    rows = refs[1].shape[0]
    for k, ref in enumerate(refs[:NEAR]):
        block = ref[:rows, :]
        part = pl.ds(k * rows, rows)
        near_ref[:, part] = block.astype(jnp.float32).T.astype(jnp.bfloat16)
        half_ref[:, part] = half_norms(scale, block)


def middle(*refs):
    noisy_ref, rhs_ref, image_ref, rest_ref, known_ref, copies_ref = refs[NEAR:]
    rhs = rhs_ref[...]
    rows = rhs.shape[1]
    total = refs[0][...]
    for ref in refs[1:NEAR]:
        total += ref[...]
    norm, noisy_norm = collect_lanes(total[:, rows:], 2)
    shift = 1.0 + noisy_norm / norm
    image = total[:, :rows] + noisy_ref[...]
    rest = image - shift * rhs
    image_ref[...] = image
    rest_ref[...] = rest
    lane = lax.broadcasted_iota(jnp.int32, known_ref.shape, 1)
    known_ref[...] = jnp.where(lane == 0, norm, shift)
    lanes = spread_lanes((row_sum(rhs * rest), row_sum(rest * rest)), known_ref.shape)
    high = rest.astype(jnp.bfloat16)
    low = (rest - high.astype(jnp.float32)).astype(jnp.bfloat16)
    packed = jnp.concatenate([high, low, lanes], axis=1)
    for k in range(copies_ref.shape[0]):
        copies_ref[k] = packed


def closing(*refs):
    noise_ref, rhs_ref, image_ref, rest_ref, known_ref = refs[NEAR : NEAR + 5]
    field_ref, residual_ref, direction_ref, image_dir_ref, norm_ref, curve_ref = refs[NEAR + 5 :]
    rhs = rhs_ref[...]
    image = image_ref[...]
    rows = rhs.shape[1]
    total = refs[0][...]
    for ref in refs[1:NEAR]:
        total += ref[...]
    rest_image = total[:, :rows] + noise_ref[...] * rest_ref[...]
    cross, square = collect_lanes(total[:, rows:], 2)
    norm, shift = known_ref[:, 0:1], known_ref[:, 1:2]
    extra = cross / norm
    alpha = 1.0 / (shift + extra)
    norm_next = alpha * alpha * jnp.maximum(square - extra * cross, 0.0)
    beta = norm_next / norm
    residual = rhs - alpha * image
    direction = residual + beta * rhs
    image_dir = (alpha * extra + beta) * image - alpha * rest_image
    curve_two = row_sum(direction * image_dir)
    field_ref[...] = alpha * rhs
    residual_ref[...] = residual
    direction_ref[...] = direction
    image_dir_ref[...] = image_dir
    norm_ref[...] = jnp.broadcast_to(norm_next, norm_ref.shape)
    curve_ref[...] = jnp.broadcast_to(curve_two, norm_ref.shape).T


def finish(curve_ref, norm_ref, field_ref, residual_ref, direction_ref, image_dir_ref, *outs):
    cols = curve_ref.shape[1]
    curve = jnp.sum(curve_ref[...], axis=0, keepdims=True)
    curve = jnp.concatenate([curve, jnp.ones((1, LANES - cols), jnp.float32)], axis=1)
    curve = jnp.broadcast_to(curve, (LANES, LANES)).T[:cols, 0:1]
    alpha = norm_ref[:, 0:1] / curve
    outs[0][...] = field_ref[...] + alpha * direction_ref[...]
    outs[1][...] = residual_ref[...] - alpha * image_dir_ref[...]


def per_device(points, noise_var, right_side):
    rows, feats = points.shape
    packed, rhs, noisy, noise = run_pack(points, right_side.T, noise_var)
    cols = rhs.shape[0]
    field_shape = ((cols, rows), jnp.float32)
    lanes_shape = ((cols, LANES), jnp.float32)
    side = [packed]
    for k in range(1, SIDE):
        side.append(partner(packed, reach(SIDE_MASKS, k), reach(LINE_MASKS, k)))
    near = exchange([points] * NEAR, NEAR_MASKS)
    own = run_bundle(side, near[1:])
    own_across = partner(own, CORE_MASK)
    first, second = [partner(own, *line_masks(turn)) for turn in (1, 2)]
    near, half = small_call(
        functools.partial(prepare, scale_of(feats)),
        [((feats, NEAR * rows), points.dtype), ((8, NEAR * rows), jnp.float32)],
        packed,
        *near[1:],
    )

    def first_call(far, last, ending=False):
        return run_first(far, near, half, last, rows, cols, ending)

    across = own_across
    half_a, total = first_call([own], None)
    half_b, total = first_call([across], total)
    first, second, total = lax.optimization_barrier((first, second, total))
    third = partner(second, *line_masks(1))
    across = [partner(item, CORE_MASK) for item in (first, second)]
    pair_a, total = first_call([first, across[0]], total)
    pair_b, total = first_call([second, across[1]], total)
    third, total = lax.optimization_barrier((third, total))
    across = partner(third, CORE_MASK)
    half_c, total = first_call([third], total)
    half_d, *parts = first_call([across], total, True)
    skip = SIDE * rows
    own_pieces = [(half_a, 0), (pair_a, 0), (pair_b, 0), (half_c, 0)]
    other_pieces = [(half_b, 0), (pair_a, skip), (pair_b, skip), (half_d, 0)]

    image, rest, known, copies = small_call(
        middle,
        [field_shape, field_shape, lanes_shape, ((CHIPS, cols, 2 * rows + LANES), jnp.bfloat16)],
        *exchange(parts, NEAR_MASKS),
        noisy,
        rhs,
    )
    copies = share(copies)
    other = partner(copies, CORE_MASK)
    half_total = run_second(0, own_pieces, copies, rows)[0]
    parts = run_second(1, other_pieces, other, rows, half_total, copies)
    field, residual, direction, image_dir, norm_next, curve = small_call(
        closing,
        [field_shape] * 4 + [lanes_shape, ((DEVICES, cols), jnp.float32)],
        *exchange(parts, NEAR_MASKS),
        noise,
        rhs,
        image,
        rest,
        known,
    )
    curve = lax.all_to_all(curve[:, None, :], "pts", 0, 0).reshape(DEVICES, cols)
    field, residual = small_call(
        finish, [field_shape] * 2, curve, norm_next, field, residual, direction, image_dir
    )
    return (field.T, residual.T)


def solution(mesh):
    return jax.shard_map(
        per_device,
        mesh=mesh,
        in_specs=(P("pts", None), P("pts"), P("pts", None)),
        out_specs=(P("pts", None), P("pts", None)),
        check_vma=False,
    )
```

```python
import functools
import math

import jax
import jax.numpy as jnp
from jax import lax
from jax.experimental import pallas as pl
from jax.experimental.pallas import tpu as pltpu
from jax.sharding import PartitionSpec as P

DEVICES = 128
NEAR_MASKS = (10, 2)
SIDE_MASKS = (6, 24)
LINE_MASKS = (32, 64)
CORE_MASK = 1
NEAR = 1 << len(NEAR_MASKS)
SIDE = 1 << len(SIDE_MASKS)
EVEN_LINES = (0, 1, 3, 2)
ODD_LINES = (0, 1, 2, 3)
PAIR = 2
UNROLL = 2
LANES = 128
CHUNK = 512
UNIT = 256
SPLITS = 3
LIMIT = 6 * 1024 * 1024
SMALL = 8 * 1024 * 1024
INSIDE = pl.BlockSpec(memory_space=pltpu.VMEM)


def scale_of(feats):
    return 2.0 / feats * math.log2(math.e)


def reach(masks, k):
    mask = 0
    for bit, step in enumerate(masks):
        if (k >> bit) & 1:
            mask ^= step
    return mask


def partner(value, even, odd=None):
    odd = even if odd is None else odd
    pairs = [(k, k ^ (odd if k & CORE_MASK else even)) for k in range(DEVICES)]
    return lax.ppermute(value, "pts", pairs)


def exchange(items, masks):
    return [items[0]] + [partner(items[k], reach(masks, k)) for k in range(1, len(items))]


def line_masks(turn):
    return reach(LINE_MASKS, EVEN_LINES[turn]), reach(SIDE_MASKS, ODD_LINES[turn])


def small_call(body, shapes, *args):
    return pl.pallas_call(
        body,
        in_specs=[INSIDE] * len(args),
        out_specs=[INSIDE] * len(shapes),
        out_shape=[jax.ShapeDtypeStruct(*shape) for shape in shapes],
        compiler_params=pltpu.CompilerParams(vmem_limit_bytes=SMALL),
    )(*args)


def half_norms(scale, block):
    ones = jnp.ones((8, block.shape[1]), jnp.bfloat16)
    dims = (((1,), (1,)), ((), ()))
    square = jnp.square(block.astype(jnp.float32))
    high = square.astype(jnp.bfloat16)
    low = (square - high.astype(jnp.float32)).astype(jnp.bfloat16)
    total = lax.dot_general(ones, high, dims, preferred_element_type=jnp.float32)
    total += lax.dot_general(ones, low, dims, preferred_element_type=jnp.float32)
    return total * (-0.5 * scale)


def first_product(scale, rows, count, opening, ending, *refs):
    far_refs = refs[:count]
    near_ref, half_ref = refs[count : count + 2]
    kern_ref, sum_ref, far_ref = refs[count + 2 + (0 if opening else 1) :][:1] + refs[-2:]
    sum_ref[...] = jnp.zeros_like(sum_ref) if opening else refs[count + 2][...]
    cols = sum_ref.shape[0]
    width = near_ref.shape[1]
    chunks = width // UNIT
    tall = rows + cols * (rows // near_ref.shape[0])
    for k, ref in enumerate(far_refs):
        far_ref[pl.ds(k * SIDE, SIDE)] = ref[...]
        for j in range(SIDE):
            sum_ref[:, width:] += ref[j, pl.ds(tall, cols), :].astype(jnp.float32)

    @pl.loop(0, far_ref.shape[0] // (PAIR * UNROLL))
    def _(step):
        units, far, vec, far_half, here = [], [], [], [], []
        for u in range(UNROLL):
            first = PAIR * (UNROLL * step + u)
            block = jnp.concatenate([far_ref[first + k, :rows, :] for k in range(PAIR)], axis=0)
            pieces = [
                far_ref[first + k, pl.ds(at, cols), :]
                for k in range(PAIR)
                for at in range(rows, tall, cols)
            ]
            block_f = block.astype(jnp.float32)
            far.append(block)
            vec.append(jnp.concatenate(pieces, axis=1))
            far_half.append(jnp.sum(block_f * block_f, axis=1, keepdims=True) * (-0.5 * scale))
            here.append(pl.ds(pl.multiple_of(first * rows, PAIR * rows), PAIR * rows))
            units += [(u, pl.ds(c * UNIT, UNIT)) for c in range(chunks)]
        cross, tile = {}, {}
        for c in range(len(units) + 2):
            if c < len(units):
                u, part = units[c]
                cross[c] = jnp.dot(far[u], near_ref[:, part], preferred_element_type=jnp.float32)
            if 0 <= c - 1 < len(units):
                u, part = units[c - 1]
                tile[c - 1] = jnp.exp2(
                    cross.pop(c - 1) * scale + far_half[u] + half_ref[0:1, part]
                ).astype(jnp.bfloat16)
                kern_ref[here[u], part] = tile[c - 1]
            if 0 <= c - 2 < len(units):
                u, part = units[c - 2]
                sum_ref[:, part] += jnp.dot(
                    vec[u], tile.pop(c - 2), preferred_element_type=jnp.float32
                )

    if ending:
        write_parts(rows, width, sum_ref, refs[-2 - NEAR : -2])


def write_parts(rows, width, sum_ref, outs):
    for k, ref in enumerate(outs):
        ref[:, :rows] = sum_ref[:, pl.ds(k * rows, rows)]
        ref[:, rows:] = sum_ref[:, width:]


def second_product(rows, starts, ending, *refs):
    count = len(starts)
    blocks, pieces = refs[:count], refs[count : 2 * count]
    vec_ref = refs[-1]
    sum_ref = refs[-2]
    cols = sum_ref.shape[0]
    width = pieces[0].shape[1]
    last_ref = None if len(refs) == 2 * count + 2 else refs[2 * count]
    lanes = jnp.zeros((cols, LANES), jnp.float32) if last_ref is None else last_ref[:, width:]
    for n, ref in enumerate(blocks):
        for side in range(SIDE):
            part = pl.ds(side * rows, rows)
            vec_ref[n, :cols, part] = ref[side, :, pl.ds(0, rows)]
            vec_ref[n, cols:, part] = ref[side, :, pl.ds(rows, rows)]
            lanes += ref[side, :, 2 * rows :].astype(jnp.float32)
    sum_ref[:, width:] = lanes
    for c in range(width // CHUNK):
        part = pl.ds(c * CHUNK, CHUNK)
        value = jnp.zeros((2 * cols, CHUNK), jnp.float32)
        for n, ref in enumerate(pieces):
            tile = ref[pl.ds(starts[n], SIDE * rows), part]
            value += jnp.dot(vec_ref[n], tile, preferred_element_type=jnp.float32)
        value = value[:cols] + value[cols:]
        if last_ref is not None:
            value += last_ref[:, part]
        sum_ref[:, part] = value
    if ending:
        write_parts(rows, width, sum_ref, refs[-2 - NEAR : -2])


def run_first(far, near, half, last, rows, cols, ending=False):
    feats, width = near.shape
    opening = last is None
    inputs = list(far) + [near, half] + ([] if opening else [last])
    count = len(far) * SIDE * rows
    running = (cols, width + LANES)
    if ending:
        outs = [jax.ShapeDtypeStruct((cols, rows + LANES), jnp.float32)] * NEAR
        scratch = [pltpu.VMEM(running, jnp.float32)]
    else:
        outs = [jax.ShapeDtypeStruct(running, jnp.float32)]
        scratch = []
    return pl.pallas_call(
        functools.partial(first_product, scale_of(feats), rows, len(far), opening, ending),
        in_specs=[INSIDE] * len(inputs),
        out_specs=[INSIDE] * (1 + len(outs)),
        out_shape=[pltpu.VMEM((count, width), jnp.bfloat16)] + outs,
        scratch_shapes=scratch + [pltpu.VMEM((len(far) * SIDE,) + far[0].shape[1:], jnp.bfloat16)],
        compiler_params=pltpu.CompilerParams(vmem_limit_bytes=LIMIT),
        cost_estimate=pl.CostEstimate(
            flops=4 * count * width * feats,
            bytes_accessed=2 * count * width,
            transcendentals=count * width,
        ),
    )(*inputs)


def run_second(blocks, pieces, last, rows, ending=False):
    width = pieces[0][0].shape[1]
    cols = blocks[0].shape[1]
    starts = [start for _, start in pieces]
    kerns = [pltpu.with_memory_space_constraint(kern, pltpu.VMEM) for kern, _ in pieces]
    inputs = list(blocks) + kerns + ([] if last is None else [last])
    running = (cols, width + LANES)
    if ending:
        outs = [jax.ShapeDtypeStruct((cols, rows + LANES), jnp.float32)] * NEAR
        scratch = [pltpu.VMEM(running, jnp.float32)]
    else:
        outs = [jax.ShapeDtypeStruct(running, jnp.float32)]
        scratch = []
    count = len(blocks) * SIDE * rows
    return pl.pallas_call(
        functools.partial(second_product, rows, starts, ending),
        in_specs=[INSIDE] * len(inputs),
        out_specs=[INSIDE] * len(outs),
        out_shape=outs,
        scratch_shapes=scratch + [pltpu.VMEM((len(blocks), 2 * cols, SIDE * rows), jnp.bfloat16)],
        compiler_params=pltpu.CompilerParams(vmem_limit_bytes=LIMIT),
        cost_estimate=pl.CostEstimate(
            flops=2 * count * width * 8 * cols,
            bytes_accessed=2 * count * width,
            transcendentals=0,
        ),
    )(*inputs)


def spread_lanes(items, shape):
    lane = lax.broadcasted_iota(jnp.int32, shape, 1)
    lanes = jnp.zeros(shape, jnp.float32)
    for k, rest in enumerate(items):
        for j in range(SPLITS):
            piece = rest.astype(jnp.bfloat16).astype(jnp.float32)
            lanes = jnp.where(lane == SPLITS * k + j, piece, lanes)
            rest = rest - piece
    return lanes.astype(jnp.bfloat16)


def collect_lanes(lanes, count):
    lane = lax.broadcasted_iota(jnp.int32, lanes.shape, 1)
    items = []
    for k in range(count):
        inside = (lane >= SPLITS * k) & (lane < SPLITS * (k + 1))
        items.append(jnp.sum(jnp.where(inside, lanes, 0.0), axis=1, keepdims=True))
    return items


def row_sum(value):
    return jnp.sum(value, axis=1, keepdims=True)


def pack(points_ref, rhs_ref, noise_ref, out_ref, keep_ref, noisy_ref, row_ref, line_ref, sems):
    rows, feats = points_ref.shape
    cols = rhs_ref.shape[0]
    first = pltpu.make_async_copy(points_ref, out_ref.at[pl.ds(0, rows), :], sems.at[0])
    second = pltpu.make_async_copy(rhs_ref, keep_ref, sems.at[1])
    third = pltpu.make_async_copy(noise_ref, line_ref, sems.at[2])
    second.start()
    third.start()
    first.start()
    second.wait()
    for k in range(rows // feats):
        part = keep_ref[:, pl.ds(k * feats, feats)]
        out_ref[pl.ds(rows + k * cols, cols), :] = part.astype(jnp.bfloat16)
    rhs = keep_ref[...]
    third.wait()
    noise = line_ref[...].reshape(1, rows)
    row_ref[...] = noise
    noisy = noise * rhs
    noisy_ref[...] = noisy
    lanes = spread_lanes((row_sum(rhs * rhs), row_sum(rhs * noisy)), (cols, LANES))
    out_ref[pl.ds(rows + cols * (rows // feats), cols), :] = lanes
    first.wait()


def outside(value):
    return pltpu.with_memory_space_constraint(value, pltpu.HBM)


def run_pack(points, rhs, noise):
    rows, feats = points.shape
    cols = rhs.shape[0]
    tall = rows + cols * (rows // feats) + cols
    place = pl.BlockSpec(memory_space=pltpu.HBM)
    return pl.pallas_call(
        pack,
        in_specs=[place] * 3,
        out_specs=[INSIDE] * 4,
        out_shape=[
            jax.ShapeDtypeStruct((tall, feats), points.dtype),
            jax.ShapeDtypeStruct(rhs.shape, rhs.dtype),
            jax.ShapeDtypeStruct(rhs.shape, rhs.dtype),
            jax.ShapeDtypeStruct((1, rows), noise.dtype),
        ],
        scratch_shapes=[pltpu.VMEM((rows,), noise.dtype), pltpu.SemaphoreType.DMA((3,))],
        compiler_params=pltpu.CompilerParams(vmem_limit_bytes=SMALL),
    )(outside(points), outside(rhs), outside(noise))


def run_bundle(side, near):
    place = pl.BlockSpec(memory_space=pl.ANY)
    return pl.pallas_call(
        bundle,
        in_specs=[INSIDE] * len(side) + [place] * len(near),
        out_specs=INSIDE,
        out_shape=jax.ShapeDtypeStruct((len(side),) + side[0].shape, side[0].dtype),
        compiler_params=pltpu.CompilerParams(vmem_limit_bytes=SMALL),
    )(*side, *near)


def bundle(*refs):
    for k, ref in enumerate(refs[:SIDE]):
        refs[-1][k] = ref[...]


def prepare(scale, *refs):
    near_ref, half_ref = refs[NEAR:]
    rows = refs[1].shape[0]
    for k, ref in enumerate(refs[:NEAR]):
        block = ref[:rows, :]
        part = pl.ds(k * rows, rows)
        near_ref[:, part] = block.astype(jnp.float32).T.astype(jnp.bfloat16)
        half_ref[:, part] = half_norms(scale, block)


def middle(*refs):
    noisy_ref, rhs_ref, image_ref, rest_ref, known_ref, packed_ref = refs[NEAR:]
    rhs = rhs_ref[...]
    rows = rhs.shape[1]
    total = refs[0][...]
    for ref in refs[1:NEAR]:
        total += ref[...]
    norm, noisy_norm = collect_lanes(total[:, rows:], 2)
    shift = 1.0 + noisy_norm / norm
    image = total[:, :rows] + noisy_ref[...]
    rest = image - shift * rhs
    image_ref[...] = image
    rest_ref[...] = rest
    lane = lax.broadcasted_iota(jnp.int32, known_ref.shape, 1)
    known_ref[...] = jnp.where(lane == 0, norm, shift)
    lanes = spread_lanes((row_sum(rhs * rest), row_sum(rest * rest)), known_ref.shape)
    high = rest.astype(jnp.bfloat16)
    low = (rest - high.astype(jnp.float32)).astype(jnp.bfloat16)
    packed_ref[...] = jnp.concatenate([high, low, lanes], axis=1)


def closing(*refs):
    noise_ref, rhs_ref, image_ref, rest_ref, known_ref = refs[NEAR : NEAR + 5]
    field_ref, residual_ref, direction_ref, image_dir_ref, norm_ref, curve_ref = refs[NEAR + 5 :]
    rhs = rhs_ref[...]
    image = image_ref[...]
    rows = rhs.shape[1]
    total = refs[0][...]
    for ref in refs[1:NEAR]:
        total += ref[...]
    rest_image = total[:, :rows] + noise_ref[...] * rest_ref[...]
    cross, square = collect_lanes(total[:, rows:], 2)
    norm, shift = known_ref[:, 0:1], known_ref[:, 1:2]
    extra = cross / norm
    alpha = 1.0 / (shift + extra)
    norm_next = alpha * alpha * jnp.maximum(square - extra * cross, 0.0)
    beta = norm_next / norm
    residual = rhs - alpha * image
    direction = residual + beta * rhs
    image_dir = (alpha * extra + beta) * image - alpha * rest_image
    curve_two = row_sum(direction * image_dir)
    field_ref[...] = alpha * rhs
    residual_ref[...] = residual
    direction_ref[...] = direction
    image_dir_ref[...] = image_dir
    norm_ref[...] = jnp.broadcast_to(norm_next, norm_ref.shape)
    curve_ref[...] = jnp.broadcast_to(curve_two, norm_ref.shape).T


def finish(curve_ref, norm_ref, field_ref, residual_ref, direction_ref, image_dir_ref, *outs):
    cols = curve_ref.shape[1]
    curve = jnp.sum(curve_ref[...], axis=0, keepdims=True)
    curve = jnp.concatenate([curve, jnp.ones((1, LANES - cols), jnp.float32)], axis=1)
    curve = jnp.broadcast_to(curve, (LANES, LANES)).T[:cols, 0:1]
    alpha = norm_ref[:, 0:1] / curve
    outs[0][...] = field_ref[...] + alpha * direction_ref[...]
    outs[1][...] = residual_ref[...] - alpha * image_dir_ref[...]


def per_device(points, noise_var, right_side):
    rows, feats = points.shape
    packed, rhs, noisy, noise = run_pack(points, right_side.T, noise_var)
    cols = rhs.shape[0]
    field_shape = ((cols, rows), jnp.float32)
    lanes_shape = ((cols, LANES), jnp.float32)
    side = [packed]
    for k in range(1, SIDE):
        side.append(partner(packed, reach(SIDE_MASKS, k), reach(LINE_MASKS, k)))
    near = exchange([points] * NEAR, NEAR_MASKS)
    own = run_bundle(side, near[1:])
    own_across = partner(own, CORE_MASK)
    first, second = [partner(own, *line_masks(turn)) for turn in (1, 2)]
    near, half = small_call(
        functools.partial(prepare, scale_of(feats)),
        [((feats, NEAR * rows), points.dtype), ((8, NEAR * rows), jnp.float32)],
        packed,
        *near[1:],
    )

    def first_call(far, last, ending=False):
        return run_first(far, near, half, last, rows, cols, ending)

    across = own_across
    half_a, total = first_call([own], None)
    half_b, total = first_call([across], total)
    first, second, total = lax.optimization_barrier((first, second, total))
    third = partner(second, *line_masks(1))
    across = [partner(item, CORE_MASK) for item in (first, second)]
    pair_a, total = first_call([first, across[0]], total)
    pair_b, total = first_call([second, across[1]], total)
    third, total = lax.optimization_barrier((third, total))
    across = partner(third, CORE_MASK)
    half_c, total = first_call([third], total)
    half_d, *parts = first_call([across], total, True)

    wide_shape = ((cols, 2 * rows + LANES), jnp.bfloat16)
    image, rest, known, packed = small_call(
        middle,
        [field_shape, field_shape, lanes_shape, wide_shape],
        *exchange(parts, NEAR_MASKS),
        noisy,
        rhs,
    )
    side = [packed]
    for k in range(1, SIDE):
        side.append(partner(packed, reach(SIDE_MASKS, k), reach(LINE_MASKS, k)))
    own = run_bundle(side, [])
    across = partner(own, CORE_MASK)
    first, second = [partner(own, *line_masks(turn)) for turn in (1, 2)]
    skip = SIDE * rows
    total = run_second([own], [(half_a, 0)], None, rows)[0]
    total = run_second([across], [(half_b, 0)], total, rows)[0]
    first, second, total = lax.optimization_barrier((first, second, total))
    third = partner(second, *line_masks(1))
    across = [partner(item, CORE_MASK) for item in (first, second)]
    total = run_second([first, second], [(pair_a, 0), (pair_b, 0)], total, rows)[0]
    total = run_second(across, [(pair_a, skip), (pair_b, skip)], total, rows)[0]
    third, total = lax.optimization_barrier((third, total))
    across = partner(third, CORE_MASK)
    total = run_second([third], [(half_c, 0)], total, rows)[0]
    parts = run_second([across], [(half_d, 0)], total, rows, True)
    field, residual, direction, image_dir, norm_next, curve = small_call(
        closing,
        [field_shape] * 4 + [lanes_shape, ((DEVICES, cols), jnp.float32)],
        *exchange(parts, NEAR_MASKS),
        noise,
        rhs,
        image,
        rest,
        known,
    )
    curve = lax.all_to_all(curve[:, None, :], "pts", 0, 0).reshape(DEVICES, cols)
    field, residual = small_call(
        finish, [field_shape] * 2, curve, norm_next, field, residual, direction, image_dir
    )
    return (field.T, residual.T)


def solution(mesh):
    return jax.shard_map(
        per_device,
        mesh=mesh,
        in_specs=(P("pts", None), P("pts"), P("pts", None)),
        out_specs=(P("pts", None), P("pts", None)),
        check_vma=False,
    )
```

```python
import functools
import math

import jax
import jax.numpy as jnp
from jax import lax
from jax.experimental import pallas as pl
from jax.experimental.pallas import tpu as pltpu
from jax.sharding import PartitionSpec as P

DEVICES = 128
NEAR_MASKS = (10, 2)
SIDE_MASKS = (6, 24)
LINE_MASKS = (32, 64)
CORE_MASK = 1
NEAR = 1 << len(NEAR_MASKS)
SIDE = 1 << len(SIDE_MASKS)
EVEN_LINES = (0, 1, 3, 2)
ODD_LINES = (0, 1, 2, 3)
TURNS = 4
CHIPS = SIDE * TURNS
PAIR = 2
UNROLL = 2
LANES = 128
CHUNK = 512
UNIT = 256
SPLITS = 3
SUMS = 3
LIMIT = 6 * 1024 * 1024
SMALL = 8 * 1024 * 1024
INSIDE = pl.BlockSpec(memory_space=pltpu.VMEM)


def scale_of(feats):
    return 2.0 / feats * math.log2(math.e)


def reach(masks, k):
    mask = 0
    for bit, step in enumerate(masks):
        if (k >> bit) & 1:
            mask ^= step
    return mask


def chip_groups():
    groups, seen = [], set()
    for base in range(DEVICES):
        if base not in seen:
            group = [base ^ reach(SIDE_MASKS + LINE_MASKS, k) for k in range(CHIPS)]
            groups.append(group)
            seen.update(group)
    return groups


def place_in_group(index):
    place = 0
    for bit, mask in enumerate(SIDE_MASKS + LINE_MASKS):
        place += lax.rem(lax.div(index, 1 << (mask.bit_length() - 1)), 2) << bit
    return place


def partner(value, even, odd=None):
    odd = even if odd is None else odd
    pairs = [(k, k ^ (odd if k & CORE_MASK else even)) for k in range(DEVICES)]
    return lax.ppermute(value, "pts", pairs)


def exchange(items, masks):
    return [items[0]] + [partner(items[k], reach(masks, k)) for k in range(1, len(items))]


def line_masks(turn):
    return reach(LINE_MASKS, EVEN_LINES[turn]), reach(SIDE_MASKS, ODD_LINES[turn])


def share(copies):
    return lax.all_to_all(copies, "pts", 0, 0, axis_index_groups=chip_groups())


def small_call(body, shapes, *args):
    return pl.pallas_call(
        body,
        in_specs=[INSIDE] * len(args),
        out_specs=[INSIDE] * len(shapes),
        out_shape=[jax.ShapeDtypeStruct(*shape) for shape in shapes],
        compiler_params=pltpu.CompilerParams(vmem_limit_bytes=SMALL),
    )(*args)


def half_norms(scale, block):
    ones = jnp.ones((8, block.shape[1]), jnp.bfloat16)
    dims = (((1,), (1,)), ((), ()))
    square = jnp.square(block.astype(jnp.float32))
    high = square.astype(jnp.bfloat16)
    low = (square - high.astype(jnp.float32)).astype(jnp.bfloat16)
    total = lax.dot_general(ones, high, dims, preferred_element_type=jnp.float32)
    total += lax.dot_general(ones, low, dims, preferred_element_type=jnp.float32)
    return total * (-0.5 * scale)


def first_product(scale, rows, count, opening, ending, *refs):
    far_refs = refs[:count]
    near_ref, half_ref = refs[count : count + 2]
    kern_ref, sum_ref, far_ref = refs[count + 2 + (0 if opening else 1) :][:1] + refs[-2:]
    sum_ref[...] = jnp.zeros_like(sum_ref) if opening else refs[count + 2][...]
    cols = sum_ref.shape[0]
    width = near_ref.shape[1]
    chunks = width // UNIT
    tall = rows + cols * (rows // near_ref.shape[0])
    for k, ref in enumerate(far_refs):
        far_ref[pl.ds(k * SIDE, SIDE)] = ref[...]
        for j in range(SIDE):
            sum_ref[:, width:] += ref[j, pl.ds(tall, cols), :].astype(jnp.float32)

    @pl.loop(0, far_ref.shape[0] // (PAIR * UNROLL))
    def _(step):
        units, far, vec, far_half, here = [], [], [], [], []
        for u in range(UNROLL):
            first = PAIR * (UNROLL * step + u)
            block = jnp.concatenate([far_ref[first + k, :rows, :] for k in range(PAIR)], axis=0)
            pieces = [
                far_ref[first + k, pl.ds(at, cols), :]
                for k in range(PAIR)
                for at in range(rows, tall, cols)
            ]
            block_f = block.astype(jnp.float32)
            far.append(block)
            vec.append(jnp.concatenate(pieces, axis=1))
            far_half.append(jnp.sum(block_f * block_f, axis=1, keepdims=True) * (-0.5 * scale))
            here.append(pl.ds(pl.multiple_of(first * rows, PAIR * rows), PAIR * rows))
            units += [(u, pl.ds(c * UNIT, UNIT)) for c in range(chunks)]
        cross, tile = {}, {}
        for c in range(len(units) + 2):
            if c < len(units):
                u, part = units[c]
                cross[c] = jnp.dot(far[u], near_ref[:, part], preferred_element_type=jnp.float32)
            if 0 <= c - 1 < len(units):
                u, part = units[c - 1]
                tile[c - 1] = jnp.exp2(
                    cross.pop(c - 1) * scale + far_half[u] + half_ref[0:1, part]
                ).astype(jnp.bfloat16)
                kern_ref[here[u], part] = tile[c - 1]
            if 0 <= c - 2 < len(units):
                u, part = units[c - 2]
                sum_ref[:, part] += jnp.dot(
                    vec[u], tile.pop(c - 2), preferred_element_type=jnp.float32
                )

    if ending:
        for k, ref in enumerate(refs[-2 - NEAR : -2]):
            ref[:, :rows] = sum_ref[:, pl.ds(k * rows, rows)]
            ref[:, rows:] = sum_ref[:, width:]


def second_product(rows, core, starts, *refs):
    kerns = refs[:TURNS]
    blocks_ref = refs[TURNS]
    vec_ref, total_ref = refs[-2:]
    cols = total_ref.shape[0]
    index = lax.axis_index("pts")
    place = place_in_group(index)
    odd = lax.rem(index, 2)
    for n in range(TURNS):
        for side in range(SIDE):
            even_slot = side + SIDE * EVEN_LINES[n]
            odd_slot = SIDE * side + ODD_LINES[n]
            slot = jnp.bitwise_xor(place, jnp.where(odd == core, even_slot, odd_slot))
            part = pl.ds(side * rows, rows)
            block = blocks_ref[slot].astype(jnp.float32)
            value = block[:, :rows] + collect_lanes(block[:, rows:], SUMS)[-1]
            high = value.astype(jnp.bfloat16)
            vec_ref[n, :cols, part] = high
            vec_ref[n, cols:, part] = (value - high.astype(jnp.float32)).astype(jnp.bfloat16)
    for c in range(total_ref.shape[1] // CHUNK):
        part = pl.ds(c * CHUNK, CHUNK)
        value = jnp.zeros((2 * cols, CHUNK), jnp.float32)
        for n, ref in enumerate(kerns):
            tile = ref[pl.ds(starts[n], SIDE * rows), part]
            value += jnp.dot(vec_ref[n], tile, preferred_element_type=jnp.float32)
        value = value[:cols] + value[cols:]
        if core == 1:
            value += refs[TURNS + 1][:, part]
        total_ref[:, part] = value
    if core == 0:
        refs[-3][...] = total_ref[...]
    else:
        other_ref = refs[TURNS + 2]
        lanes = jnp.zeros((total_ref.shape[0], LANES), jnp.float32)
        for k in range(CHIPS):
            lanes += blocks_ref[k, :, rows:].astype(jnp.float32)
            lanes += other_ref[k, :, rows:].astype(jnp.float32)
        for k, ref in enumerate(refs[TURNS + 3 : TURNS + 3 + NEAR]):
            ref[:, :rows] = total_ref[:, pl.ds(k * rows, rows)]
            ref[:, rows:] = lanes


def run_first(far, near, half, last, rows, cols, ending=False):
    feats, width = near.shape
    opening = last is None
    inputs = list(far) + [near, half] + ([] if opening else [last])
    count = len(far) * SIDE * rows
    running = (cols, width + LANES)
    if ending:
        outs = [jax.ShapeDtypeStruct((cols, rows + LANES), jnp.float32)] * NEAR
        scratch = [pltpu.VMEM(running, jnp.float32)]
    else:
        outs = [jax.ShapeDtypeStruct(running, jnp.float32)]
        scratch = []
    return pl.pallas_call(
        functools.partial(first_product, scale_of(feats), rows, len(far), opening, ending),
        in_specs=[INSIDE] * len(inputs),
        out_specs=[INSIDE] * (1 + len(outs)),
        out_shape=[pltpu.VMEM((count, width), jnp.bfloat16)] + outs,
        scratch_shapes=scratch + [pltpu.VMEM((len(far) * SIDE,) + far[0].shape[1:], jnp.bfloat16)],
        compiler_params=pltpu.CompilerParams(vmem_limit_bytes=LIMIT),
        cost_estimate=pl.CostEstimate(
            flops=4 * count * width * feats,
            bytes_accessed=2 * count * width,
            transcendentals=count * width,
        ),
    )(*inputs)


def run_second(core, pieces, blocks, rows, *others):
    width = pieces[0][0].shape[1]
    cols = blocks.shape[1]
    starts = [start for _, start in pieces]
    kerns = [pltpu.with_memory_space_constraint(kern, pltpu.VMEM) for kern, _ in pieces]
    inputs = kerns + [blocks] + list(others)
    if core == 0:
        outs = [jax.ShapeDtypeStruct((cols, width), jnp.float32)]
    else:
        outs = [jax.ShapeDtypeStruct((cols, rows + LANES), jnp.float32)] * NEAR
    return pl.pallas_call(
        functools.partial(second_product, rows, core, starts),
        in_specs=[INSIDE] * len(inputs),
        out_specs=[INSIDE] * len(outs),
        out_shape=outs,
        scratch_shapes=[
            pltpu.VMEM((TURNS, 2 * cols, SIDE * rows), jnp.bfloat16),
            pltpu.VMEM((cols, width), jnp.float32),
        ],
        compiler_params=pltpu.CompilerParams(vmem_limit_bytes=LIMIT),
        cost_estimate=pl.CostEstimate(
            flops=2 * TURNS * SIDE * rows * width * 8 * cols,
            bytes_accessed=2 * TURNS * SIDE * rows * width,
            transcendentals=0,
        ),
    )(*inputs)


def spread_lanes(items, shape):
    lane = lax.broadcasted_iota(jnp.int32, shape, 1)
    lanes = jnp.zeros(shape, jnp.float32)
    for k, rest in enumerate(items):
        for j in range(SPLITS):
            piece = rest.astype(jnp.bfloat16).astype(jnp.float32)
            lanes = jnp.where(lane == SPLITS * k + j, piece, lanes)
            rest = rest - piece
    return lanes.astype(jnp.bfloat16)


def collect_lanes(lanes, count):
    lane = lax.broadcasted_iota(jnp.int32, lanes.shape, 1)
    items = []
    for k in range(count):
        inside = (lane >= SPLITS * k) & (lane < SPLITS * (k + 1))
        items.append(jnp.sum(jnp.where(inside, lanes, 0.0), axis=1, keepdims=True))
    return items


def row_sum(value):
    return jnp.sum(value, axis=1, keepdims=True)


def pack(points_ref, rhs_ref, noise_ref, out_ref, keep_ref, noisy_ref, row_ref, line_ref, sems):
    rows, feats = points_ref.shape
    cols = rhs_ref.shape[0]
    first = pltpu.make_async_copy(points_ref, out_ref.at[pl.ds(0, rows), :], sems.at[0])
    second = pltpu.make_async_copy(rhs_ref, keep_ref, sems.at[1])
    third = pltpu.make_async_copy(noise_ref, line_ref, sems.at[2])
    second.start()
    third.start()
    first.start()
    second.wait()
    for k in range(rows // feats):
        part = keep_ref[:, pl.ds(k * feats, feats)]
        out_ref[pl.ds(rows + k * cols, cols), :] = part.astype(jnp.bfloat16)
    rhs = keep_ref[...]
    third.wait()
    noise = line_ref[...].reshape(1, rows)
    row_ref[...] = noise
    noisy = noise * rhs
    noisy_ref[...] = noisy
    lanes = spread_lanes((row_sum(rhs * rhs), row_sum(rhs * noisy)), (cols, LANES))
    out_ref[pl.ds(rows + cols * (rows // feats), cols), :] = lanes
    first.wait()


def outside(value):
    return pltpu.with_memory_space_constraint(value, pltpu.HBM)


def run_pack(points, rhs, noise):
    rows, feats = points.shape
    cols = rhs.shape[0]
    tall = rows + cols * (rows // feats) + cols
    place = pl.BlockSpec(memory_space=pltpu.HBM)
    return pl.pallas_call(
        pack,
        in_specs=[place] * 3,
        out_specs=[INSIDE] * 4,
        out_shape=[
            jax.ShapeDtypeStruct((tall, feats), points.dtype),
            jax.ShapeDtypeStruct(rhs.shape, rhs.dtype),
            jax.ShapeDtypeStruct(rhs.shape, rhs.dtype),
            jax.ShapeDtypeStruct((1, rows), noise.dtype),
        ],
        scratch_shapes=[pltpu.VMEM((rows,), noise.dtype), pltpu.SemaphoreType.DMA((3,))],
        compiler_params=pltpu.CompilerParams(vmem_limit_bytes=SMALL),
    )(outside(points), outside(rhs), outside(noise))


def run_bundle(side, near):
    place = pl.BlockSpec(memory_space=pl.ANY)
    return pl.pallas_call(
        bundle,
        in_specs=[INSIDE] * len(side) + [place] * len(near),
        out_specs=INSIDE,
        out_shape=jax.ShapeDtypeStruct((len(side),) + side[0].shape, side[0].dtype),
        compiler_params=pltpu.CompilerParams(vmem_limit_bytes=SMALL),
    )(*side, *near)


def bundle(*refs):
    for k, ref in enumerate(refs[:SIDE]):
        refs[-1][k] = ref[...]


def prepare(scale, *refs):
    near_ref, half_ref = refs[NEAR:]
    rows = refs[1].shape[0]
    for k, ref in enumerate(refs[:NEAR]):
        block = ref[:rows, :]
        part = pl.ds(k * rows, rows)
        near_ref[:, part] = block.astype(jnp.float32).T.astype(jnp.bfloat16)
        half_ref[:, part] = half_norms(scale, block)


def middle(*refs):
    noisy_ref, rhs_ref, image_ref, rest_ref, known_ref, copies_ref = refs[NEAR:]
    rhs = rhs_ref[...]
    rows = rhs.shape[1]
    total = refs[0][...]
    for ref in refs[1:NEAR]:
        total += ref[...]
    norm, noisy_norm = collect_lanes(total[:, rows:], 2)
    shift = 1.0 + noisy_norm / norm
    image = total[:, :rows] + noisy_ref[...]
    rest = image - shift * rhs
    image_ref[...] = image
    rest_ref[...] = rest
    lane = lax.broadcasted_iota(jnp.int32, known_ref.shape, 1)
    known_ref[...] = jnp.where(lane == 0, norm, shift)
    mean = row_sum(rest) * (1.0 / rows)
    lanes = spread_lanes((row_sum(rhs * rest), row_sum(rest * rest), mean), known_ref.shape)
    packed = jnp.concatenate([(rest - mean).astype(jnp.bfloat16), lanes], axis=1)
    for k in range(copies_ref.shape[0]):
        copies_ref[k] = packed


def closing(*refs):
    noise_ref, rhs_ref, image_ref, rest_ref, known_ref = refs[NEAR : NEAR + 5]
    field_ref, residual_ref, direction_ref, image_dir_ref, norm_ref, curve_ref = refs[NEAR + 5 :]
    rhs = rhs_ref[...]
    image = image_ref[...]
    rows = rhs.shape[1]
    total = refs[0][...]
    for ref in refs[1:NEAR]:
        total += ref[...]
    rest_image = total[:, :rows] + noise_ref[...] * rest_ref[...]
    cross, square = collect_lanes(total[:, rows:], 2)
    norm, shift = known_ref[:, 0:1], known_ref[:, 1:2]
    extra = cross / norm
    alpha = 1.0 / (shift + extra)
    norm_next = alpha * alpha * jnp.maximum(square - extra * cross, 0.0)
    beta = norm_next / norm
    residual = rhs - alpha * image
    direction = residual + beta * rhs
    image_dir = (alpha * extra + beta) * image - alpha * rest_image
    curve_two = row_sum(direction * image_dir)
    field_ref[...] = alpha * rhs
    residual_ref[...] = residual
    direction_ref[...] = direction
    image_dir_ref[...] = image_dir
    norm_ref[...] = jnp.broadcast_to(norm_next, norm_ref.shape)
    curve_ref[...] = jnp.broadcast_to(curve_two, norm_ref.shape).T


def finish(curve_ref, norm_ref, field_ref, residual_ref, direction_ref, image_dir_ref, *outs):
    cols = curve_ref.shape[1]
    curve = jnp.sum(curve_ref[...], axis=0, keepdims=True)
    curve = jnp.concatenate([curve, jnp.ones((1, LANES - cols), jnp.float32)], axis=1)
    curve = jnp.broadcast_to(curve, (LANES, LANES)).T[:cols, 0:1]
    alpha = norm_ref[:, 0:1] / curve
    outs[0][...] = field_ref[...] + alpha * direction_ref[...]
    outs[1][...] = residual_ref[...] - alpha * image_dir_ref[...]


def per_device(points, noise_var, right_side):
    rows, feats = points.shape
    packed, rhs, noisy, noise = run_pack(points, right_side.T, noise_var)
    cols = rhs.shape[0]
    field_shape = ((cols, rows), jnp.float32)
    lanes_shape = ((cols, LANES), jnp.float32)
    side = [packed]
    for k in range(1, SIDE):
        side.append(partner(packed, reach(SIDE_MASKS, k), reach(LINE_MASKS, k)))
    near = exchange([points] * NEAR, NEAR_MASKS)
    own = run_bundle(side, near[1:])
    own_across = partner(own, CORE_MASK)
    first, second = [partner(own, *line_masks(turn)) for turn in (1, 2)]
    near, half = small_call(
        functools.partial(prepare, scale_of(feats)),
        [((feats, NEAR * rows), points.dtype), ((8, NEAR * rows), jnp.float32)],
        packed,
        *near[1:],
    )

    def first_call(far, last, ending=False):
        return run_first(far, near, half, last, rows, cols, ending)

    across = own_across
    half_a, total = first_call([own], None)
    half_b, total = first_call([across], total)
    first, second, total = lax.optimization_barrier((first, second, total))
    third = partner(second, *line_masks(1))
    across = [partner(item, CORE_MASK) for item in (first, second)]
    pair_a, total = first_call([first, across[0]], total)
    pair_b, total = first_call([second, across[1]], total)
    third, total = lax.optimization_barrier((third, total))
    across = partner(third, CORE_MASK)
    half_c, total = first_call([third], total)
    half_d, *parts = first_call([across], total, True)
    skip = SIDE * rows
    own_pieces = [(half_a, 0), (pair_a, 0), (pair_b, 0), (half_c, 0)]
    other_pieces = [(half_b, 0), (pair_a, skip), (pair_b, skip), (half_d, 0)]

    image, rest, known, copies = small_call(
        middle,
        [field_shape, field_shape, lanes_shape, ((CHIPS, cols, rows + LANES), jnp.bfloat16)],
        *exchange(parts, NEAR_MASKS),
        noisy,
        rhs,
    )
    copies = share(copies)
    other = partner(copies, CORE_MASK)
    half_total = run_second(0, own_pieces, copies, rows)[0]
    parts = run_second(1, other_pieces, other, rows, half_total, copies)
    field, residual, direction, image_dir, norm_next, curve = small_call(
        closing,
        [field_shape] * 4 + [lanes_shape, ((DEVICES, cols), jnp.float32)],
        *exchange(parts, NEAR_MASKS),
        noise,
        rhs,
        image,
        rest,
        known,
    )
    curve = lax.all_to_all(curve[:, None, :], "pts", 0, 0).reshape(DEVICES, cols)
    field, residual = small_call(
        finish, [field_shape] * 2, curve, norm_next, field, residual, direction, image_dir
    )
    return (field.T, residual.T)


def solution(mesh):
    return jax.shard_map(
        per_device,
        mesh=mesh,
        in_specs=(P("pts", None), P("pts"), P("pts", None)),
        out_specs=(P("pts", None), P("pts", None)),
        check_vma=False,
    )
```

```python
import functools
import math

import jax
import jax.numpy as jnp
from jax import lax
from jax.experimental import pallas as pl
from jax.experimental.pallas import tpu as pltpu
from jax.sharding import PartitionSpec as P

DEVICES = 128
NEAR_MASKS = (10, 2)
SIDE_MASKS = (6, 24)
LINE_MASKS = (32, 64)
CORE_MASK = 1
NEAR = 1 << len(NEAR_MASKS)
SIDE = 1 << len(SIDE_MASKS)
EVEN_LINES = (0, 1, 3, 2)
ODD_LINES = (0, 1, 2, 3)
TURNS = 4
CHIPS = SIDE * TURNS
PAIR = 1
UNROLL = 4
LANES = 128
CHUNK = 512
UNIT = 256
SPLITS = 3
SUMS = 3
LIMIT = 6 * 1024 * 1024
SMALL = 8 * 1024 * 1024
INSIDE = pl.BlockSpec(memory_space=pltpu.VMEM)


def scale_of(feats):
    return 2.0 / feats * math.log2(math.e)


def reach(masks, k):
    mask = 0
    for bit, step in enumerate(masks):
        if (k >> bit) & 1:
            mask ^= step
    return mask


def chip_groups():
    groups, seen = [], set()
    for base in range(DEVICES):
        if base not in seen:
            group = [base ^ reach(SIDE_MASKS + LINE_MASKS, k) for k in range(CHIPS)]
            groups.append(group)
            seen.update(group)
    return groups


def place_in_group(index):
    place = 0
    for bit, mask in enumerate(SIDE_MASKS + LINE_MASKS):
        place += lax.rem(lax.div(index, 1 << (mask.bit_length() - 1)), 2) << bit
    return place


def partner(value, even, odd=None):
    odd = even if odd is None else odd
    pairs = [(k, k ^ (odd if k & CORE_MASK else even)) for k in range(DEVICES)]
    return lax.ppermute(value, "pts", pairs)


def exchange(items, masks):
    return [items[0]] + [partner(items[k], reach(masks, k)) for k in range(1, len(items))]


def line_masks(turn):
    return reach(LINE_MASKS, EVEN_LINES[turn]), reach(SIDE_MASKS, ODD_LINES[turn])


def share(copies):
    return lax.all_to_all(copies, "pts", 0, 0, axis_index_groups=chip_groups())


def small_call(body, shapes, *args):
    return pl.pallas_call(
        body,
        in_specs=[INSIDE] * len(args),
        out_specs=[INSIDE] * len(shapes),
        out_shape=[jax.ShapeDtypeStruct(*shape) for shape in shapes],
        compiler_params=pltpu.CompilerParams(vmem_limit_bytes=SMALL),
    )(*args)


def half_norms(scale, block):
    ones = jnp.ones((8, block.shape[1]), jnp.bfloat16)
    dims = (((1,), (1,)), ((), ()))
    square = jnp.square(block.astype(jnp.float32))
    high = square.astype(jnp.bfloat16)
    low = (square - high.astype(jnp.float32)).astype(jnp.bfloat16)
    total = lax.dot_general(ones, high, dims, preferred_element_type=jnp.float32)
    total += lax.dot_general(ones, low, dims, preferred_element_type=jnp.float32)
    return total * (-0.5 * scale)


def first_product(scale, rows, count, opening, ending, *refs):
    far_refs = refs[:count]
    near_ref, half_ref = refs[count : count + 2]
    kern_ref, sum_ref, far_ref = refs[count + 2 + (0 if opening else 1) :][:1] + refs[-2:]
    sum_ref[...] = jnp.zeros_like(sum_ref) if opening else refs[count + 2][...]
    cols = sum_ref.shape[0]
    width = near_ref.shape[1]
    chunks = width // UNIT
    tall = rows + cols * (rows // near_ref.shape[0])
    for k, ref in enumerate(far_refs):
        far_ref[pl.ds(k * SIDE, SIDE)] = ref[...]
        for j in range(SIDE):
            sum_ref[:, width:] += ref[j, pl.ds(tall, cols), :].astype(jnp.float32)

    @pl.loop(0, far_ref.shape[0] // (PAIR * UNROLL))
    def _(step):
        units, far, vec, far_half, here = [], [], [], [], []
        for u in range(UNROLL):
            first = PAIR * (UNROLL * step + u)
            block = jnp.concatenate([far_ref[first + k, :rows, :] for k in range(PAIR)], axis=0)
            pieces = [
                far_ref[first + k, pl.ds(at, cols), :]
                for k in range(PAIR)
                for at in range(rows, tall, cols)
            ]
            block_f = block.astype(jnp.float32)
            far.append(block)
            vec.append(jnp.concatenate(pieces, axis=1))
            far_half.append(jnp.sum(block_f * block_f, axis=1, keepdims=True) * (-0.5 * scale))
            here.append(pl.ds(pl.multiple_of(first * rows, PAIR * rows), PAIR * rows))
            units += [(u, pl.ds(c * UNIT, UNIT)) for c in range(chunks)]
        cross, tile = {}, {}
        for c in range(len(units) + 2):
            if c < len(units):
                u, part = units[c]
                cross[c] = jnp.dot(far[u], near_ref[:, part], preferred_element_type=jnp.float32)
            if 0 <= c - 1 < len(units):
                u, part = units[c - 1]
                tile[c - 1] = jnp.exp2(
                    cross.pop(c - 1) * scale + far_half[u] + half_ref[0:1, part]
                ).astype(jnp.bfloat16)
                kern_ref[here[u], part] = tile[c - 1]
            if 0 <= c - 2 < len(units):
                u, part = units[c - 2]
                sum_ref[:, part] += jnp.dot(
                    vec[u], tile.pop(c - 2), preferred_element_type=jnp.float32
                )

    if ending:
        for k, ref in enumerate(refs[-2 - NEAR : -2]):
            ref[:, :rows] = sum_ref[:, pl.ds(k * rows, rows)]
            ref[:, rows:] = sum_ref[:, width:]


def second_product(rows, core, starts, *refs):
    kerns = refs[:TURNS]
    blocks_ref = refs[TURNS]
    vec_ref, total_ref = refs[-2:]
    cols = total_ref.shape[0]
    index = lax.axis_index("pts")
    place = place_in_group(index)
    odd = lax.rem(index, 2)
    for n in range(TURNS):
        for side in range(SIDE):
            even_slot = side + SIDE * EVEN_LINES[n]
            odd_slot = SIDE * side + ODD_LINES[n]
            slot = jnp.bitwise_xor(place, jnp.where(odd == core, even_slot, odd_slot))
            part = pl.ds(side * rows, rows)
            block = blocks_ref[slot].astype(jnp.float32)
            value = block[:, :rows] + collect_lanes(block[:, rows:], SUMS)[-1]
            high = value.astype(jnp.bfloat16)
            vec_ref[n, :cols, part] = high
            vec_ref[n, cols:, part] = (value - high.astype(jnp.float32)).astype(jnp.bfloat16)
    for c in range(total_ref.shape[1] // CHUNK):
        part = pl.ds(c * CHUNK, CHUNK)
        value = jnp.zeros((2 * cols, CHUNK), jnp.float32)
        for n, ref in enumerate(kerns):
            tile = ref[pl.ds(starts[n], SIDE * rows), part]
            value += jnp.dot(vec_ref[n], tile, preferred_element_type=jnp.float32)
        value = value[:cols] + value[cols:]
        if core == 1:
            value += refs[TURNS + 1][:, part]
        total_ref[:, part] = value
    if core == 0:
        refs[-3][...] = total_ref[...]
    else:
        other_ref = refs[TURNS + 2]
        lanes = jnp.zeros((total_ref.shape[0], LANES), jnp.float32)
        for k in range(CHIPS):
            lanes += blocks_ref[k, :, rows:].astype(jnp.float32)
            lanes += other_ref[k, :, rows:].astype(jnp.float32)
        for k, ref in enumerate(refs[TURNS + 3 : TURNS + 3 + NEAR]):
            ref[:, :rows] = total_ref[:, pl.ds(k * rows, rows)]
            ref[:, rows:] = lanes


def run_first(far, near, half, last, rows, cols, ending=False):
    feats, width = near.shape
    opening = last is None
    inputs = list(far) + [near, half] + ([] if opening else [last])
    count = len(far) * SIDE * rows
    running = (cols, width + LANES)
    if ending:
        outs = [jax.ShapeDtypeStruct((cols, rows + LANES), jnp.float32)] * NEAR
        scratch = [pltpu.VMEM(running, jnp.float32)]
    else:
        outs = [jax.ShapeDtypeStruct(running, jnp.float32)]
        scratch = []
    return pl.pallas_call(
        functools.partial(first_product, scale_of(feats), rows, len(far), opening, ending),
        in_specs=[INSIDE] * len(inputs),
        out_specs=[INSIDE] * (1 + len(outs)),
        out_shape=[pltpu.VMEM((count, width), jnp.bfloat16)] + outs,
        scratch_shapes=scratch + [pltpu.VMEM((len(far) * SIDE,) + far[0].shape[1:], jnp.bfloat16)],
        compiler_params=pltpu.CompilerParams(vmem_limit_bytes=LIMIT),
        cost_estimate=pl.CostEstimate(
            flops=4 * count * width * feats,
            bytes_accessed=2 * count * width,
            transcendentals=count * width,
        ),
    )(*inputs)


def run_second(core, pieces, blocks, rows, *others):
    width = pieces[0][0].shape[1]
    cols = blocks.shape[1]
    starts = [start for _, start in pieces]
    kerns = [pltpu.with_memory_space_constraint(kern, pltpu.VMEM) for kern, _ in pieces]
    inputs = kerns + [blocks] + list(others)
    if core == 0:
        outs = [jax.ShapeDtypeStruct((cols, width), jnp.float32)]
    else:
        outs = [jax.ShapeDtypeStruct((cols, rows + LANES), jnp.float32)] * NEAR
    return pl.pallas_call(
        functools.partial(second_product, rows, core, starts),
        in_specs=[INSIDE] * len(inputs),
        out_specs=[INSIDE] * len(outs),
        out_shape=outs,
        scratch_shapes=[
            pltpu.VMEM((TURNS, 2 * cols, SIDE * rows), jnp.bfloat16),
            pltpu.VMEM((cols, width), jnp.float32),
        ],
        compiler_params=pltpu.CompilerParams(vmem_limit_bytes=LIMIT),
        cost_estimate=pl.CostEstimate(
            flops=2 * TURNS * SIDE * rows * width * 8 * cols,
            bytes_accessed=2 * TURNS * SIDE * rows * width,
            transcendentals=0,
        ),
    )(*inputs)


def spread_lanes(items, shape):
    lane = lax.broadcasted_iota(jnp.int32, shape, 1)
    lanes = jnp.zeros(shape, jnp.float32)
    for k, rest in enumerate(items):
        for j in range(SPLITS):
            piece = rest.astype(jnp.bfloat16).astype(jnp.float32)
            lanes = jnp.where(lane == SPLITS * k + j, piece, lanes)
            rest = rest - piece
    return lanes.astype(jnp.bfloat16)


def collect_lanes(lanes, count):
    lane = lax.broadcasted_iota(jnp.int32, lanes.shape, 1)
    items = []
    for k in range(count):
        inside = (lane >= SPLITS * k) & (lane < SPLITS * (k + 1))
        items.append(jnp.sum(jnp.where(inside, lanes, 0.0), axis=1, keepdims=True))
    return items


def row_sum(value):
    return jnp.sum(value, axis=1, keepdims=True)


def pack(points_ref, rhs_ref, noise_ref, out_ref, keep_ref, noisy_ref, row_ref, line_ref, sems):
    rows, feats = points_ref.shape
    cols = rhs_ref.shape[0]
    first = pltpu.make_async_copy(points_ref, out_ref.at[pl.ds(0, rows), :], sems.at[0])
    second = pltpu.make_async_copy(rhs_ref, keep_ref, sems.at[1])
    third = pltpu.make_async_copy(noise_ref, line_ref, sems.at[2])
    second.start()
    third.start()
    first.start()
    second.wait()
    for k in range(rows // feats):
        part = keep_ref[:, pl.ds(k * feats, feats)]
        out_ref[pl.ds(rows + k * cols, cols), :] = part.astype(jnp.bfloat16)
    rhs = keep_ref[...]
    third.wait()
    noise = line_ref[...].reshape(1, rows)
    row_ref[...] = noise
    noisy = noise * rhs
    noisy_ref[...] = noisy
    lanes = spread_lanes((row_sum(rhs * rhs), row_sum(rhs * noisy)), (cols, LANES))
    out_ref[pl.ds(rows + cols * (rows // feats), cols), :] = lanes
    first.wait()


def outside(value):
    return pltpu.with_memory_space_constraint(value, pltpu.HBM)


def run_pack(points, rhs, noise):
    rows, feats = points.shape
    cols = rhs.shape[0]
    tall = rows + cols * (rows // feats) + cols
    place = pl.BlockSpec(memory_space=pltpu.HBM)
    return pl.pallas_call(
        pack,
        in_specs=[place] * 3,
        out_specs=[INSIDE] * 4,
        out_shape=[
            jax.ShapeDtypeStruct((tall, feats), points.dtype),
            jax.ShapeDtypeStruct(rhs.shape, rhs.dtype),
            jax.ShapeDtypeStruct(rhs.shape, rhs.dtype),
            jax.ShapeDtypeStruct((1, rows), noise.dtype),
        ],
        scratch_shapes=[pltpu.VMEM((rows,), noise.dtype), pltpu.SemaphoreType.DMA((3,))],
        compiler_params=pltpu.CompilerParams(vmem_limit_bytes=SMALL),
    )(outside(points), outside(rhs), outside(noise))


def run_bundle(side, near):
    place = pl.BlockSpec(memory_space=pl.ANY)
    return pl.pallas_call(
        bundle,
        in_specs=[INSIDE] * len(side) + [place] * len(near),
        out_specs=INSIDE,
        out_shape=jax.ShapeDtypeStruct((len(side),) + side[0].shape, side[0].dtype),
        compiler_params=pltpu.CompilerParams(vmem_limit_bytes=SMALL),
    )(*side, *near)


def bundle(*refs):
    for k, ref in enumerate(refs[:SIDE]):
        refs[-1][k] = ref[...]


def prepare(scale, *refs):
    near_ref, half_ref = refs[NEAR:]
    rows = refs[1].shape[0]
    for k, ref in enumerate(refs[:NEAR]):
        block = ref[:rows, :]
        part = pl.ds(k * rows, rows)
        near_ref[:, part] = block.astype(jnp.float32).T.astype(jnp.bfloat16)
        half_ref[:, part] = half_norms(scale, block)


def middle(*refs):
    noisy_ref, rhs_ref, image_ref, rest_ref, known_ref, copies_ref = refs[NEAR:]
    rhs = rhs_ref[...]
    rows = rhs.shape[1]
    total = refs[0][...]
    for ref in refs[1:NEAR]:
        total += ref[...]
    norm, noisy_norm = collect_lanes(total[:, rows:], 2)
    shift = 1.0 + noisy_norm / norm
    image = total[:, :rows] + noisy_ref[...]
    rest = image - shift * rhs
    image_ref[...] = image
    rest_ref[...] = rest
    lane = lax.broadcasted_iota(jnp.int32, known_ref.shape, 1)
    known_ref[...] = jnp.where(lane == 0, norm, shift)
    mean = row_sum(rest) * (1.0 / rows)
    lanes = spread_lanes((row_sum(rhs * rest), row_sum(rest * rest), mean), known_ref.shape)
    packed = jnp.concatenate([(rest - mean).astype(jnp.bfloat16), lanes], axis=1)
    for k in range(copies_ref.shape[0]):
        copies_ref[k] = packed


def closing(*refs):
    noise_ref, rhs_ref, image_ref, rest_ref, known_ref = refs[NEAR : NEAR + 5]
    field_ref, residual_ref, direction_ref, image_dir_ref, norm_ref, curve_ref = refs[NEAR + 5 :]
    rhs = rhs_ref[...]
    image = image_ref[...]
    rows = rhs.shape[1]
    total = refs[0][...]
    for ref in refs[1:NEAR]:
        total += ref[...]
    rest_image = total[:, :rows] + noise_ref[...] * rest_ref[...]
    cross, square = collect_lanes(total[:, rows:], 2)
    norm, shift = known_ref[:, 0:1], known_ref[:, 1:2]
    extra = cross / norm
    alpha = 1.0 / (shift + extra)
    norm_next = alpha * alpha * jnp.maximum(square - extra * cross, 0.0)
    beta = norm_next / norm
    residual = rhs - alpha * image
    direction = residual + beta * rhs
    image_dir = (alpha * extra + beta) * image - alpha * rest_image
    curve_two = row_sum(direction * image_dir)
    field_ref[...] = alpha * rhs
    residual_ref[...] = residual
    direction_ref[...] = direction
    image_dir_ref[...] = image_dir
    norm_ref[...] = jnp.broadcast_to(norm_next, norm_ref.shape)
    curve_ref[...] = jnp.broadcast_to(curve_two, norm_ref.shape).T


def finish(curve_ref, norm_ref, field_ref, residual_ref, direction_ref, image_dir_ref, *outs):
    cols = curve_ref.shape[1]
    curve = jnp.sum(curve_ref[...], axis=0, keepdims=True)
    curve = jnp.concatenate([curve, jnp.ones((1, LANES - cols), jnp.float32)], axis=1)
    curve = jnp.broadcast_to(curve, (LANES, LANES)).T[:cols, 0:1]
    alpha = norm_ref[:, 0:1] / curve
    outs[0][...] = field_ref[...] + alpha * direction_ref[...]
    outs[1][...] = residual_ref[...] - alpha * image_dir_ref[...]


def per_device(points, noise_var, right_side):
    rows, feats = points.shape
    packed, rhs, noisy, noise = run_pack(points, right_side.T, noise_var)
    cols = rhs.shape[0]
    field_shape = ((cols, rows), jnp.float32)
    lanes_shape = ((cols, LANES), jnp.float32)
    side = [packed]
    for k in range(1, SIDE):
        side.append(partner(packed, reach(SIDE_MASKS, k), reach(LINE_MASKS, k)))
    near = exchange([points] * NEAR, NEAR_MASKS)
    near, half = small_call(
        functools.partial(prepare, scale_of(feats)),
        [((feats, NEAR * rows), points.dtype), ((8, NEAR * rows), jnp.float32)],
        packed,
        *near[1:],
    )
    own = run_bundle(side, [half])
    own_across = partner(own, CORE_MASK)
    first, second = [partner(own, *line_masks(turn)) for turn in (1, 2)]

    def first_call(far, last, ending=False):
        return run_first(far, near, half, last, rows, cols, ending)

    across = own_across
    half_a, total = first_call([own], None)
    half_b, total = first_call([across], total)
    first, second, total = lax.optimization_barrier((first, second, total))
    third = partner(second, *line_masks(1))
    across = [partner(item, CORE_MASK) for item in (first, second)]
    pair_a, total = first_call([first, across[0]], total)
    pair_b, total = first_call([second, across[1]], total)
    third, total = lax.optimization_barrier((third, total))
    across = partner(third, CORE_MASK)
    half_c, total = first_call([third], total)
    half_d, *parts = first_call([across], total, True)
    skip = SIDE * rows
    own_pieces = [(half_a, 0), (pair_a, 0), (pair_b, 0), (half_c, 0)]
    other_pieces = [(half_b, 0), (pair_a, skip), (pair_b, skip), (half_d, 0)]

    image, rest, known, copies = small_call(
        middle,
        [field_shape, field_shape, lanes_shape, ((CHIPS, cols, rows + LANES), jnp.bfloat16)],
        *exchange(parts, NEAR_MASKS),
        noisy,
        rhs,
    )
    copies = share(copies)
    other = partner(copies, CORE_MASK)
    half_total = run_second(0, own_pieces, copies, rows)[0]
    parts = run_second(1, other_pieces, other, rows, half_total, copies)
    field, residual, direction, image_dir, norm_next, curve = small_call(
        closing,
        [field_shape] * 4 + [lanes_shape, ((DEVICES, cols), jnp.float32)],
        *exchange(parts, NEAR_MASKS),
        noise,
        rhs,
        image,
        rest,
        known,
    )
    curve = lax.all_to_all(curve[:, None, :], "pts", 0, 0).reshape(DEVICES, cols)
    field, residual = small_call(
        finish, [field_shape] * 2, curve, norm_next, field, residual, direction, image_dir
    )
    return (field.T, residual.T)


def solution(mesh):
    return jax.shard_map(
        per_device,
        mesh=mesh,
        in_specs=(P("pts", None), P("pts"), P("pts", None)),
        out_specs=(P("pts", None), P("pts", None)),
        check_vma=False,
    )
```

```python
import functools
import math

import jax
import jax.numpy as jnp
from jax import lax
from jax.experimental import pallas as pl
from jax.experimental.pallas import tpu as pltpu
from jax.sharding import PartitionSpec as P

DEVICES = 128
NEAR_MASKS = (10, 2)
SIDE_MASKS = (6, 24)
LINE_MASKS = (32, 64)
CORE_MASK = 1
NEAR = 1 << len(NEAR_MASKS)
SIDE = 1 << len(SIDE_MASKS)
EVEN_LINES = (0, 1, 3, 2)
ODD_LINES = (0, 1, 2, 3)
TURNS = 4
CHIPS = SIDE * TURNS
LANES = 128
CHUNK = 512
UNIT = 256
SPLITS = 3
SUMS = 3
LIMIT = 6 * 1024 * 1024
SMALL = 8 * 1024 * 1024
INSIDE = pl.BlockSpec(memory_space=pltpu.VMEM)


def scale_of(feats):
    return 2.0 / feats * math.log2(math.e)


def reach(masks, k):
    mask = 0
    for bit, step in enumerate(masks):
        if (k >> bit) & 1:
            mask ^= step
    return mask


def chip_groups():
    groups, seen = [], set()
    for base in range(DEVICES):
        if base not in seen:
            group = [base ^ reach(SIDE_MASKS + LINE_MASKS, k) for k in range(CHIPS)]
            groups.append(group)
            seen.update(group)
    return groups


def place_in_group(index):
    place = 0
    for bit, mask in enumerate(SIDE_MASKS + LINE_MASKS):
        place += lax.rem(lax.div(index, 1 << (mask.bit_length() - 1)), 2) << bit
    return place


def partner(value, even, odd=None):
    odd = even if odd is None else odd
    pairs = [(k, k ^ (odd if k & CORE_MASK else even)) for k in range(DEVICES)]
    return lax.ppermute(value, "pts", pairs)


def exchange(items, masks):
    return [items[0]] + [partner(items[k], reach(masks, k)) for k in range(1, len(items))]


def line_masks(turn):
    return reach(LINE_MASKS, EVEN_LINES[turn]), reach(SIDE_MASKS, ODD_LINES[turn])


def share(copies):
    return lax.all_to_all(copies, "pts", 0, 0, axis_index_groups=chip_groups())


def small_call(body, shapes, *args):
    return pl.pallas_call(
        body,
        in_specs=[INSIDE] * len(args),
        out_specs=[INSIDE] * len(shapes),
        out_shape=[jax.ShapeDtypeStruct(*shape) for shape in shapes],
        compiler_params=pltpu.CompilerParams(vmem_limit_bytes=SMALL),
    )(*args)


def half_norms(scale, block):
    ones = jnp.ones((8, block.shape[1]), jnp.bfloat16)
    dims = (((1,), (1,)), ((), ()))
    square = jnp.square(block.astype(jnp.float32))
    high = square.astype(jnp.bfloat16)
    low = (square - high.astype(jnp.float32)).astype(jnp.bfloat16)
    total = lax.dot_general(ones, high, dims, preferred_element_type=jnp.float32)
    total += lax.dot_general(ones, low, dims, preferred_element_type=jnp.float32)
    return total * (-0.5 * scale)


def first_product(scale, rows, count, opening, ending, *refs):
    far_refs = refs[:count]
    near_ref, half_ref = refs[count : count + 2]
    kern_ref = refs[count + 2 + (0 if opening else 1)]
    sum_ref, far_ref, vec_ref = refs[-3:]
    sum_ref[...] = jnp.zeros_like(sum_ref) if opening else refs[count + 2][...]
    cols = sum_ref.shape[0]
    feats, width = near_ref.shape
    tall = rows + cols * (rows // feats)
    for k, ref in enumerate(far_refs):
        for j in range(SIDE):
            at = (k * SIDE + j) * rows
            far_ref[pl.ds(at, rows), :] = ref[j, :rows, :]
            for n in range(rows // feats):
                part = pl.ds(at + n * feats, feats)
                vec_ref[:, part] = ref[j, pl.ds(rows + n * cols, cols), :]
            sum_ref[:, width:] += ref[j, pl.ds(tall, cols), :].astype(jnp.float32)

    bundle_rows = SIDE * rows

    @pl.loop(0, count)
    def _(step):
        far, vec, far_half, here, units = [], [], [], [], []
        for r in range(bundle_rows // UNIT):
            at = pl.ds(pl.multiple_of(step * bundle_rows + r * UNIT, UNIT), UNIT)
            block = far_ref[at, :]
            block_f = block.astype(jnp.float32)
            far.append(block)
            vec.append(vec_ref[:, at])
            far_half.append(jnp.sum(block_f * block_f, axis=1, keepdims=True) * (-0.5 * scale))
            here.append(at)
        for c in range(width // UNIT):
            units += [(r, c) for r in range(len(far))]
        cross, tile, image = {}, {}, {}
        for n in range(len(units) + 2):
            if n < len(units):
                r, c = units[n]
                near = near_ref[:, pl.ds(c * UNIT, UNIT)]
                cross[n] = jnp.dot(far[r], near, preferred_element_type=jnp.float32)
            if 0 <= n - 1 < len(units):
                r, c = units[n - 1]
                part = pl.ds(c * UNIT, UNIT)
                tile[n - 1] = jnp.exp2(
                    cross.pop(n - 1) * scale + far_half[r] + half_ref[0:1, part]
                ).astype(jnp.bfloat16)
                kern_ref[here[r], part] = tile[n - 1]
            if 0 <= n - 2 < len(units):
                r, c = units[n - 2]
                value = jnp.dot(vec[r], tile.pop(n - 2), preferred_element_type=jnp.float32)
                image[c] = value if r == 0 else image[c] + value
                if r == len(far) - 1:
                    sum_ref[:, pl.ds(c * UNIT, UNIT)] += image.pop(c)

    if ending:
        write_parts(rows, width, sum_ref, refs[-3 - NEAR : -3])


def write_parts(rows, width, sum_ref, outs):
    for k, ref in enumerate(outs):
        ref[:, :rows] = sum_ref[:, pl.ds(k * rows, rows)]
        ref[:, rows:] = sum_ref[:, width:]


def second_product(rows, core, starts, *refs):
    kerns = refs[:TURNS]
    blocks_ref = refs[TURNS]
    vec_ref, total_ref = refs[-2:]
    cols = total_ref.shape[0]
    index = lax.axis_index("pts")
    place = place_in_group(index)
    odd = lax.rem(index, 2)
    for n in range(TURNS):
        for side in range(SIDE):
            even_slot = side + SIDE * EVEN_LINES[n]
            odd_slot = SIDE * side + ODD_LINES[n]
            slot = jnp.bitwise_xor(place, jnp.where(odd == core, even_slot, odd_slot))
            part = pl.ds(side * rows, rows)
            block = blocks_ref[slot].astype(jnp.float32)
            value = block[:, :rows] + collect_lanes(block[:, rows:], SUMS)[-1]
            high = value.astype(jnp.bfloat16)
            vec_ref[n, :cols, part] = high
            vec_ref[n, cols:, part] = (value - high.astype(jnp.float32)).astype(jnp.bfloat16)
    for c in range(total_ref.shape[1] // CHUNK):
        part = pl.ds(c * CHUNK, CHUNK)
        value = jnp.zeros((2 * cols, CHUNK), jnp.float32)
        for n, ref in enumerate(kerns):
            tile = ref[pl.ds(starts[n], SIDE * rows), part]
            value += jnp.dot(vec_ref[n], tile, preferred_element_type=jnp.float32)
        value = value[:cols] + value[cols:]
        if core == 1:
            value += refs[TURNS + 1][:, part]
        total_ref[:, part] = value
    if core == 0:
        refs[-3][...] = total_ref[...]
    else:
        other_ref = refs[TURNS + 2]
        lanes = jnp.zeros((total_ref.shape[0], LANES), jnp.float32)
        for k in range(CHIPS):
            lanes += blocks_ref[k, :, rows:].astype(jnp.float32)
            lanes += other_ref[k, :, rows:].astype(jnp.float32)
        for k, ref in enumerate(refs[TURNS + 3 : TURNS + 3 + NEAR]):
            ref[:, :rows] = total_ref[:, pl.ds(k * rows, rows)]
            ref[:, rows:] = lanes


def run_first(far, near, half, last, rows, cols, ending=False):
    feats, width = near.shape
    opening = last is None
    inputs = list(far) + [near, half] + ([] if opening else [last])
    count = len(far) * SIDE * rows
    running = (cols, width + LANES)
    if ending:
        outs = [jax.ShapeDtypeStruct((cols, rows + LANES), jnp.float32)] * NEAR
        scratch = [pltpu.VMEM(running, jnp.float32)]
    else:
        outs = [jax.ShapeDtypeStruct(running, jnp.float32)]
        scratch = []
    return pl.pallas_call(
        functools.partial(first_product, scale_of(feats), rows, len(far), opening, ending),
        in_specs=[INSIDE] * len(inputs),
        out_specs=[INSIDE] * (1 + len(outs)),
        out_shape=[pltpu.VMEM((count, width), jnp.bfloat16)] + outs,
        scratch_shapes=scratch
        + [pltpu.VMEM((count, feats), jnp.bfloat16), pltpu.VMEM((cols, count), jnp.bfloat16)],
        compiler_params=pltpu.CompilerParams(vmem_limit_bytes=LIMIT),
        cost_estimate=pl.CostEstimate(
            flops=4 * count * width * feats,
            bytes_accessed=2 * count * width,
            transcendentals=count * width,
        ),
    )(*inputs)


def run_second(core, pieces, blocks, rows, *others):
    width = pieces[0][0].shape[1]
    cols = blocks.shape[1]
    starts = [start for _, start in pieces]
    kerns = [pltpu.with_memory_space_constraint(kern, pltpu.VMEM) for kern, _ in pieces]
    inputs = kerns + [blocks] + list(others)
    if core == 0:
        outs = [jax.ShapeDtypeStruct((cols, width), jnp.float32)]
    else:
        outs = [jax.ShapeDtypeStruct((cols, rows + LANES), jnp.float32)] * NEAR
    return pl.pallas_call(
        functools.partial(second_product, rows, core, starts),
        in_specs=[INSIDE] * len(inputs),
        out_specs=[INSIDE] * len(outs),
        out_shape=outs,
        scratch_shapes=[
            pltpu.VMEM((TURNS, 2 * cols, SIDE * rows), jnp.bfloat16),
            pltpu.VMEM((cols, width), jnp.float32),
        ],
        compiler_params=pltpu.CompilerParams(vmem_limit_bytes=LIMIT),
        cost_estimate=pl.CostEstimate(
            flops=2 * TURNS * SIDE * rows * width * 8 * cols,
            bytes_accessed=2 * TURNS * SIDE * rows * width,
            transcendentals=0,
        ),
    )(*inputs)


def spread_lanes(items, shape):
    lane = lax.broadcasted_iota(jnp.int32, shape, 1)
    lanes = jnp.zeros(shape, jnp.float32)
    for k, rest in enumerate(items):
        for j in range(SPLITS):
            piece = rest.astype(jnp.bfloat16).astype(jnp.float32)
            lanes = jnp.where(lane == SPLITS * k + j, piece, lanes)
            rest = rest - piece
    return lanes.astype(jnp.bfloat16)


def collect_lanes(lanes, count):
    lane = lax.broadcasted_iota(jnp.int32, lanes.shape, 1)
    items = []
    for k in range(count):
        inside = (lane >= SPLITS * k) & (lane < SPLITS * (k + 1))
        items.append(jnp.sum(jnp.where(inside, lanes, 0.0), axis=1, keepdims=True))
    return items


def row_sum(value):
    return jnp.sum(value, axis=1, keepdims=True)


def pack(points_ref, rhs_ref, noise_ref, out_ref, keep_ref, noisy_ref, row_ref, line_ref, sems):
    rows, feats = points_ref.shape
    cols = rhs_ref.shape[0]
    first = pltpu.make_async_copy(points_ref, out_ref.at[pl.ds(0, rows), :], sems.at[0])
    second = pltpu.make_async_copy(rhs_ref, keep_ref, sems.at[1])
    third = pltpu.make_async_copy(noise_ref, line_ref, sems.at[2])
    second.start()
    third.start()
    first.start()
    second.wait()
    for k in range(rows // feats):
        part = keep_ref[:, pl.ds(k * feats, feats)]
        out_ref[pl.ds(rows + k * cols, cols), :] = part.astype(jnp.bfloat16)
    rhs = keep_ref[...]
    third.wait()
    noise = line_ref[...].reshape(1, rows)
    row_ref[...] = noise
    noisy = noise * rhs
    noisy_ref[...] = noisy
    lanes = spread_lanes((row_sum(rhs * rhs), row_sum(rhs * noisy)), (cols, LANES))
    out_ref[pl.ds(rows + cols * (rows // feats), cols), :] = lanes
    first.wait()


def outside(value):
    return pltpu.with_memory_space_constraint(value, pltpu.HBM)


def run_pack(points, rhs, noise):
    rows, feats = points.shape
    cols = rhs.shape[0]
    tall = rows + cols * (rows // feats) + cols
    place = pl.BlockSpec(memory_space=pltpu.HBM)
    return pl.pallas_call(
        pack,
        in_specs=[place] * 3,
        out_specs=[INSIDE] * 4,
        out_shape=[
            jax.ShapeDtypeStruct((tall, feats), points.dtype),
            jax.ShapeDtypeStruct(rhs.shape, rhs.dtype),
            jax.ShapeDtypeStruct(rhs.shape, rhs.dtype),
            jax.ShapeDtypeStruct((1, rows), noise.dtype),
        ],
        scratch_shapes=[pltpu.VMEM((rows,), noise.dtype), pltpu.SemaphoreType.DMA((3,))],
        compiler_params=pltpu.CompilerParams(vmem_limit_bytes=SMALL),
    )(outside(points), outside(rhs), outside(noise))


def run_bundle(side, near):
    place = pl.BlockSpec(memory_space=pl.ANY)
    return pl.pallas_call(
        bundle,
        in_specs=[INSIDE] * len(side) + [place] * len(near),
        out_specs=INSIDE,
        out_shape=jax.ShapeDtypeStruct((len(side),) + side[0].shape, side[0].dtype),
        compiler_params=pltpu.CompilerParams(vmem_limit_bytes=SMALL),
    )(*side, *near)


def bundle(*refs):
    for k, ref in enumerate(refs[:SIDE]):
        refs[-1][k] = ref[...]


def prepare(scale, *refs):
    near_ref, half_ref = refs[NEAR:]
    rows = refs[1].shape[0]
    for k, ref in enumerate(refs[:NEAR]):
        block = ref[:rows, :]
        part = pl.ds(k * rows, rows)
        near_ref[:, part] = block.astype(jnp.float32).T.astype(jnp.bfloat16)
        half_ref[:, part] = half_norms(scale, block)


def middle(*refs):
    noisy_ref, rhs_ref, image_ref, rest_ref, known_ref, copies_ref = refs[NEAR:]
    rhs = rhs_ref[...]
    rows = rhs.shape[1]
    total = refs[0][...]
    for ref in refs[1:NEAR]:
        total += ref[...]
    norm, noisy_norm = collect_lanes(total[:, rows:], 2)
    shift = 1.0 + noisy_norm / norm
    image = total[:, :rows] + noisy_ref[...]
    rest = image - shift * rhs
    image_ref[...] = image
    rest_ref[...] = rest
    lane = lax.broadcasted_iota(jnp.int32, known_ref.shape, 1)
    known_ref[...] = jnp.where(lane == 0, norm, shift)
    mean = row_sum(rest) * (1.0 / rows)
    lanes = spread_lanes((row_sum(rhs * rest), row_sum(rest * rest), mean), known_ref.shape)
    packed = jnp.concatenate([(rest - mean).astype(jnp.bfloat16), lanes], axis=1)
    for k in range(copies_ref.shape[0]):
        copies_ref[k] = packed


def closing(*refs):
    noise_ref, rhs_ref, image_ref, rest_ref, known_ref = refs[NEAR : NEAR + 5]
    field_ref, residual_ref, direction_ref, image_dir_ref, norm_ref, curve_ref = refs[NEAR + 5 :]
    rhs = rhs_ref[...]
    image = image_ref[...]
    rows = rhs.shape[1]
    total = refs[0][...]
    for ref in refs[1:NEAR]:
        total += ref[...]
    rest_image = total[:, :rows] + noise_ref[...] * rest_ref[...]
    cross, square = collect_lanes(total[:, rows:], 2)
    norm, shift = known_ref[:, 0:1], known_ref[:, 1:2]
    extra = cross / norm
    alpha = 1.0 / (shift + extra)
    norm_next = alpha * alpha * jnp.maximum(square - extra * cross, 0.0)
    beta = norm_next / norm
    residual = rhs - alpha * image
    direction = residual + beta * rhs
    image_dir = (alpha * extra + beta) * image - alpha * rest_image
    curve_two = row_sum(direction * image_dir)
    field_ref[...] = alpha * rhs
    residual_ref[...] = residual
    direction_ref[...] = direction
    image_dir_ref[...] = image_dir
    norm_ref[...] = jnp.broadcast_to(norm_next, norm_ref.shape)
    curve_ref[...] = jnp.broadcast_to(curve_two, norm_ref.shape).T


def finish(curve_ref, norm_ref, field_ref, residual_ref, direction_ref, image_dir_ref, *outs):
    cols = curve_ref.shape[1]
    curve = jnp.sum(curve_ref[...], axis=0, keepdims=True)
    curve = jnp.concatenate([curve, jnp.ones((1, LANES - cols), jnp.float32)], axis=1)
    curve = jnp.broadcast_to(curve, (LANES, LANES)).T[:cols, 0:1]
    alpha = norm_ref[:, 0:1] / curve
    outs[0][...] = field_ref[...] + alpha * direction_ref[...]
    outs[1][...] = residual_ref[...] - alpha * image_dir_ref[...]


def per_device(points, noise_var, right_side):
    rows, feats = points.shape
    packed, rhs, noisy, noise = run_pack(points, right_side.T, noise_var)
    cols = rhs.shape[0]
    field_shape = ((cols, rows), jnp.float32)
    lanes_shape = ((cols, LANES), jnp.float32)
    side = [packed]
    for k in range(1, SIDE):
        side.append(partner(packed, reach(SIDE_MASKS, k), reach(LINE_MASKS, k)))
    near = exchange([points] * NEAR, NEAR_MASKS)
    own = run_bundle(side, near[1:])
    own_across = partner(own, CORE_MASK)
    first, second = [partner(own, *line_masks(turn)) for turn in (1, 2)]
    near, half = small_call(
        functools.partial(prepare, scale_of(feats)),
        [((feats, NEAR * rows), points.dtype), ((8, NEAR * rows), jnp.float32)],
        packed,
        *near[1:],
    )

    def first_call(far, last, ending=False):
        return run_first(far, near, half, last, rows, cols, ending)

    across = own_across
    half_a, total = first_call([own], None)
    half_b, total = first_call([across], total)
    first, second, total = lax.optimization_barrier((first, second, total))
    third = partner(second, *line_masks(1))
    across = [partner(item, CORE_MASK) for item in (first, second)]
    pair_a, total = first_call([first, across[0]], total)
    pair_b, total = first_call([second, across[1]], total)
    third, total = lax.optimization_barrier((third, total))
    across = partner(third, CORE_MASK)
    half_c, total = first_call([third], total)
    half_d, *parts = first_call([across], total, True)
    skip = SIDE * rows
    own_pieces = [(half_a, 0), (pair_a, 0), (pair_b, 0), (half_c, 0)]
    other_pieces = [(half_b, 0), (pair_a, skip), (pair_b, skip), (half_d, 0)]

    image, rest, known, copies = small_call(
        middle,
        [field_shape, field_shape, lanes_shape, ((CHIPS, cols, rows + LANES), jnp.bfloat16)],
        *exchange(parts, NEAR_MASKS),
        noisy,
        rhs,
    )
    copies = share(copies)
    other = partner(copies, CORE_MASK)
    half_total = run_second(0, own_pieces, copies, rows)[0]
    parts = run_second(1, other_pieces, other, rows, half_total, copies)
    field, residual, direction, image_dir, norm_next, curve = small_call(
        closing,
        [field_shape] * 4 + [lanes_shape, ((DEVICES, cols), jnp.float32)],
        *exchange(parts, NEAR_MASKS),
        noise,
        rhs,
        image,
        rest,
        known,
    )
    curve = lax.all_to_all(curve[:, None, :], "pts", 0, 0).reshape(DEVICES, cols)
    field, residual = small_call(
        finish, [field_shape] * 2, curve, norm_next, field, residual, direction, image_dir
    )
    return (field.T, residual.T)


def solution(mesh):
    return jax.shard_map(
        per_device,
        mesh=mesh,
        in_specs=(P("pts", None), P("pts"), P("pts", None)),
        out_specs=(P("pts", None), P("pts", None)),
        check_vma=False,
    )
```

```python
import functools
import math

import jax
import jax.numpy as jnp
from jax import lax
from jax.experimental import pallas as pl
from jax.experimental.pallas import tpu as pltpu
from jax.sharding import PartitionSpec as P

DEVICES = 128
NEAR_MASKS = (10, 2)
SIDE_MASKS = (6, 24)
LINE_MASKS = (32, 64)
CORE_MASK = 1
NEAR = 1 << len(NEAR_MASKS)
SIDE = 1 << len(SIDE_MASKS)
EVEN_LINES = (0, 1, 3, 2)
ODD_LINES = (0, 1, 2, 3)
TURNS = 4
CHIPS = SIDE * TURNS
PAIR = 2
UNROLL = 2
LANES = 128
CHUNK = 256
UNIT = 256
SPLITS = 3
SUMS = 3
LIMIT = 6 * 1024 * 1024
SMALL = 8 * 1024 * 1024
INSIDE = pl.BlockSpec(memory_space=pltpu.VMEM)


def scale_of(feats):
    return 2.0 / feats * math.log2(math.e)


def reach(masks, k):
    mask = 0
    for bit, step in enumerate(masks):
        if (k >> bit) & 1:
            mask ^= step
    return mask


def core_groups():
    return [[k for k in range(DEVICES) if k % 2 == odd] for odd in range(2)]


def chip_groups():
    groups, seen = [], set()
    for base in range(DEVICES):
        if base not in seen:
            group = [base ^ reach(SIDE_MASKS + LINE_MASKS, k) for k in range(CHIPS)]
            groups.append(group)
            seen.update(group)
    return groups


def place_in_group(index):
    place = 0
    for bit, mask in enumerate(SIDE_MASKS + LINE_MASKS):
        place += lax.rem(lax.div(index, 1 << (mask.bit_length() - 1)), 2) << bit
    return place


def partner(value, even, odd=None):
    odd = even if odd is None else odd
    pairs = [(k, k ^ (odd if k & CORE_MASK else even)) for k in range(DEVICES)]
    return lax.ppermute(value, "pts", pairs)


def exchange(items, masks):
    return [items[0]] + [partner(items[k], reach(masks, k)) for k in range(1, len(items))]


def line_masks(turn):
    return reach(LINE_MASKS, EVEN_LINES[turn]), reach(SIDE_MASKS, ODD_LINES[turn])


def share(copies):
    return lax.all_to_all(copies, "pts", 0, 0, axis_index_groups=chip_groups())


def small_call(body, shapes, *args):
    return pl.pallas_call(
        body,
        in_specs=[INSIDE] * len(args),
        out_specs=[INSIDE] * len(shapes),
        out_shape=[jax.ShapeDtypeStruct(*shape) for shape in shapes],
        compiler_params=pltpu.CompilerParams(vmem_limit_bytes=SMALL),
    )(*args)


def half_norms(scale, block):
    ones = jnp.ones((8, block.shape[1]), jnp.bfloat16)
    dims = (((1,), (1,)), ((), ()))
    square = jnp.square(block.astype(jnp.float32))
    high = square.astype(jnp.bfloat16)
    low = (square - high.astype(jnp.float32)).astype(jnp.bfloat16)
    total = lax.dot_general(ones, high, dims, preferred_element_type=jnp.float32)
    total += lax.dot_general(ones, low, dims, preferred_element_type=jnp.float32)
    return total * (-0.5 * scale)


def first_product(scale, rows, count, opening, ending, *refs):
    far_refs = refs[:count]
    near_ref, half_ref = refs[count : count + 2]
    kern_ref, sum_ref, far_ref = refs[count + 2 + (0 if opening else 1) :][:1] + refs[-2:]
    sum_ref[...] = jnp.zeros_like(sum_ref) if opening else refs[count + 2][...]
    cols = sum_ref.shape[0]
    width = near_ref.shape[1]
    chunks = width // UNIT
    tall = rows + cols * (rows // near_ref.shape[0])
    for k, ref in enumerate(far_refs):
        far_ref[pl.ds(k * SIDE, SIDE)] = ref[...]
        for j in range(SIDE):
            sum_ref[:, width:] += ref[j, pl.ds(tall, cols), :].astype(jnp.float32)

    @pl.loop(0, far_ref.shape[0] // (PAIR * UNROLL))
    def _(step):
        units, far, vec, far_half, here = [], [], [], [], []
        for u in range(UNROLL):
            first = PAIR * (UNROLL * step + u)
            block = jnp.concatenate([far_ref[first + k, :rows, :] for k in range(PAIR)], axis=0)
            pieces = [
                far_ref[first + k, pl.ds(at, cols), :]
                for k in range(PAIR)
                for at in range(rows, tall, cols)
            ]
            block_f = block.astype(jnp.float32)
            far.append(block)
            vec.append(jnp.concatenate(pieces, axis=1))
            far_half.append(jnp.sum(block_f * block_f, axis=1, keepdims=True) * (-0.5 * scale))
            here.append(pl.ds(pl.multiple_of(first * rows, PAIR * rows), PAIR * rows))
            units += [(u, pl.ds(c * UNIT, UNIT)) for c in range(chunks)]
        cross, tile = {}, {}
        for c in range(len(units) + 2):
            if c < len(units):
                u, part = units[c]
                cross[c] = jnp.dot(far[u], near_ref[:, part], preferred_element_type=jnp.float32)
            if 0 <= c - 1 < len(units):
                u, part = units[c - 1]
                tile[c - 1] = jnp.exp2(
                    cross.pop(c - 1) * scale + far_half[u] + half_ref[0:1, part]
                ).astype(jnp.bfloat16)
                kern_ref[here[u], part] = tile[c - 1]
            if 0 <= c - 2 < len(units):
                u, part = units[c - 2]
                sum_ref[:, part] += jnp.dot(
                    vec[u], tile.pop(c - 2), preferred_element_type=jnp.float32
                )

    if ending:
        for k, ref in enumerate(refs[-2 - NEAR : -2]):
            ref[:, :rows] = sum_ref[:, pl.ds(k * rows, rows)]
            ref[:, rows:] = sum_ref[:, width:]


def second_product(rows, core, starts, *refs):
    kerns = refs[:TURNS]
    blocks_ref = refs[TURNS]
    vec_ref, total_ref = refs[-2:]
    cols = total_ref.shape[0]
    index = lax.axis_index("pts")
    place = place_in_group(index)
    odd = lax.rem(index, 2)
    for n in range(TURNS):
        for side in range(SIDE):
            even_slot = side + SIDE * EVEN_LINES[n]
            odd_slot = SIDE * side + ODD_LINES[n]
            slot = jnp.bitwise_xor(place, jnp.where(odd == core, even_slot, odd_slot))
            part = pl.ds(side * rows, rows)
            block = blocks_ref[slot].astype(jnp.float32)
            value = block[:, :rows] + collect_lanes(block[:, rows:], SUMS)[-1]
            high = value.astype(jnp.bfloat16)
            vec_ref[n, :cols, part] = high
            vec_ref[n, cols:, part] = (value - high.astype(jnp.float32)).astype(jnp.bfloat16)
    for c in range(total_ref.shape[1] // CHUNK):
        part = pl.ds(c * CHUNK, CHUNK)
        value = jnp.zeros((2 * cols, CHUNK), jnp.float32)
        for n, ref in enumerate(kerns):
            tile = ref[pl.ds(starts[n], SIDE * rows), part]
            value += jnp.dot(vec_ref[n], tile, preferred_element_type=jnp.float32)
        value = value[:cols] + value[cols:]
        if core == 1:
            value += refs[TURNS + 1][:, part]
        total_ref[:, part] = value
    if core == 0:
        refs[-3][...] = total_ref[...]
    else:
        other_ref = refs[TURNS + 2]
        lanes = jnp.zeros((total_ref.shape[0], LANES), jnp.float32)
        for k in range(CHIPS):
            lanes += blocks_ref[k, :, rows:].astype(jnp.float32)
            lanes += other_ref[k, :, rows:].astype(jnp.float32)
        for k, ref in enumerate(refs[TURNS + 3 : TURNS + 3 + NEAR]):
            ref[:, :rows] = total_ref[:, pl.ds(k * rows, rows)]
            ref[:, rows:] = lanes


def run_first(far, near, half, last, rows, cols, ending=False):
    feats, width = near.shape
    opening = last is None
    inputs = list(far) + [near, half] + ([] if opening else [last])
    count = len(far) * SIDE * rows
    running = (cols, width + LANES)
    if ending:
        outs = [jax.ShapeDtypeStruct((cols, rows + LANES), jnp.float32)] * NEAR
        scratch = [pltpu.VMEM(running, jnp.float32)]
    else:
        outs = [jax.ShapeDtypeStruct(running, jnp.float32)]
        scratch = []
    return pl.pallas_call(
        functools.partial(first_product, scale_of(feats), rows, len(far), opening, ending),
        in_specs=[INSIDE] * len(inputs),
        out_specs=[INSIDE] * (1 + len(outs)),
        out_shape=[pltpu.VMEM((count, width), jnp.bfloat16)] + outs,
        scratch_shapes=scratch + [pltpu.VMEM((len(far) * SIDE,) + far[0].shape[1:], jnp.bfloat16)],
        compiler_params=pltpu.CompilerParams(vmem_limit_bytes=LIMIT),
        cost_estimate=pl.CostEstimate(
            flops=4 * count * width * feats,
            bytes_accessed=2 * count * width,
            transcendentals=count * width,
        ),
    )(*inputs)


def run_second(core, pieces, blocks, rows, *others):
    width = pieces[0][0].shape[1]
    cols = blocks.shape[1]
    starts = [start for _, start in pieces]
    kerns = [pltpu.with_memory_space_constraint(kern, pltpu.VMEM) for kern, _ in pieces]
    inputs = kerns + [blocks] + list(others)
    if core == 0:
        outs = [jax.ShapeDtypeStruct((cols, width), jnp.float32)]
    else:
        outs = [jax.ShapeDtypeStruct((cols, rows + LANES), jnp.float32)] * NEAR
    return pl.pallas_call(
        functools.partial(second_product, rows, core, starts),
        in_specs=[INSIDE] * len(inputs),
        out_specs=[INSIDE] * len(outs),
        out_shape=outs,
        scratch_shapes=[
            pltpu.VMEM((TURNS, 2 * cols, SIDE * rows), jnp.bfloat16),
            pltpu.VMEM((cols, width), jnp.float32),
        ],
        compiler_params=pltpu.CompilerParams(vmem_limit_bytes=LIMIT),
        cost_estimate=pl.CostEstimate(
            flops=2 * TURNS * SIDE * rows * width * 8 * cols,
            bytes_accessed=2 * TURNS * SIDE * rows * width,
            transcendentals=0,
        ),
    )(*inputs)


def spread_lanes(items, shape):
    lane = lax.broadcasted_iota(jnp.int32, shape, 1)
    lanes = jnp.zeros(shape, jnp.float32)
    for k, rest in enumerate(items):
        for j in range(SPLITS):
            piece = rest.astype(jnp.bfloat16).astype(jnp.float32)
            lanes = jnp.where(lane == SPLITS * k + j, piece, lanes)
            rest = rest - piece
    return lanes.astype(jnp.bfloat16)


def collect_lanes(lanes, count):
    lane = lax.broadcasted_iota(jnp.int32, lanes.shape, 1)
    items = []
    for k in range(count):
        inside = (lane >= SPLITS * k) & (lane < SPLITS * (k + 1))
        items.append(jnp.sum(jnp.where(inside, lanes, 0.0), axis=1, keepdims=True))
    return items


def row_sum(value):
    return jnp.sum(value, axis=1, keepdims=True)


def pack(points_ref, rhs_ref, noise_ref, out_ref, keep_ref, noisy_ref, row_ref, line_ref, sems):
    rows, feats = points_ref.shape
    cols = rhs_ref.shape[0]
    first = pltpu.make_async_copy(points_ref, out_ref.at[pl.ds(0, rows), :], sems.at[0])
    second = pltpu.make_async_copy(rhs_ref, keep_ref, sems.at[1])
    third = pltpu.make_async_copy(noise_ref, line_ref, sems.at[2])
    second.start()
    third.start()
    first.start()
    second.wait()
    for k in range(rows // feats):
        part = keep_ref[:, pl.ds(k * feats, feats)]
        out_ref[pl.ds(rows + k * cols, cols), :] = part.astype(jnp.bfloat16)
    rhs = keep_ref[...]
    third.wait()
    noise = line_ref[...].reshape(1, rows)
    row_ref[...] = noise
    noisy = noise * rhs
    noisy_ref[...] = noisy
    lanes = spread_lanes((row_sum(rhs * rhs), row_sum(rhs * noisy)), (cols, LANES))
    out_ref[pl.ds(rows + cols * (rows // feats), cols), :] = lanes
    first.wait()


def outside(value):
    return pltpu.with_memory_space_constraint(value, pltpu.HBM)


def run_pack(points, rhs, noise):
    rows, feats = points.shape
    cols = rhs.shape[0]
    tall = rows + cols * (rows // feats) + cols
    place = pl.BlockSpec(memory_space=pltpu.HBM)
    return pl.pallas_call(
        pack,
        in_specs=[place] * 3,
        out_specs=[INSIDE] * 4,
        out_shape=[
            jax.ShapeDtypeStruct((tall, feats), points.dtype),
            jax.ShapeDtypeStruct(rhs.shape, rhs.dtype),
            jax.ShapeDtypeStruct(rhs.shape, rhs.dtype),
            jax.ShapeDtypeStruct((1, rows), noise.dtype),
        ],
        scratch_shapes=[pltpu.VMEM((rows,), noise.dtype), pltpu.SemaphoreType.DMA((3,))],
        compiler_params=pltpu.CompilerParams(vmem_limit_bytes=SMALL),
    )(outside(points), outside(rhs), outside(noise))


def run_bundle(side, near):
    place = pl.BlockSpec(memory_space=pl.ANY)
    return pl.pallas_call(
        bundle,
        in_specs=[INSIDE] * len(side) + [place] * len(near),
        out_specs=INSIDE,
        out_shape=jax.ShapeDtypeStruct((len(side),) + side[0].shape, side[0].dtype),
        compiler_params=pltpu.CompilerParams(vmem_limit_bytes=SMALL),
    )(*side, *near)


def bundle(*refs):
    for k, ref in enumerate(refs[:SIDE]):
        refs[-1][k] = ref[...]


def prepare(scale, *refs):
    near_ref, half_ref = refs[NEAR:]
    rows = refs[1].shape[0]
    for k, ref in enumerate(refs[:NEAR]):
        block = ref[:rows, :]
        part = pl.ds(k * rows, rows)
        near_ref[:, part] = block.astype(jnp.float32).T.astype(jnp.bfloat16)
        half_ref[:, part] = half_norms(scale, block)


def middle(*refs):
    noisy_ref, rhs_ref, image_ref, rest_ref, known_ref, copies_ref = refs[NEAR:]
    rhs = rhs_ref[...]
    rows = rhs.shape[1]
    total = refs[0][...]
    for ref in refs[1:NEAR]:
        total += ref[...]
    norm, noisy_norm = collect_lanes(total[:, rows:], 2)
    shift = 1.0 + noisy_norm / norm
    image = total[:, :rows] + noisy_ref[...]
    rest = image - shift * rhs
    image_ref[...] = image
    rest_ref[...] = rest
    lane = lax.broadcasted_iota(jnp.int32, known_ref.shape, 1)
    known_ref[...] = jnp.where(lane == 0, norm, shift)
    mean = row_sum(rest) * (1.0 / rows)
    lanes = spread_lanes((row_sum(rhs * rest), row_sum(rest * rest), mean), known_ref.shape)
    packed = jnp.concatenate([(rest - mean).astype(jnp.bfloat16), lanes], axis=1)
    for k in range(copies_ref.shape[0]):
        copies_ref[k] = packed


def closing(*refs):
    noise_ref, rhs_ref, image_ref, rest_ref, known_ref = refs[NEAR : NEAR + 5]
    field_ref, residual_ref, direction_ref, image_dir_ref, norm_ref, curve_ref = refs[NEAR + 5 :]
    rhs = rhs_ref[...]
    image = image_ref[...]
    rows = rhs.shape[1]
    total = refs[0][...]
    for ref in refs[1:NEAR]:
        total += ref[...]
    rest_image = total[:, :rows] + noise_ref[...] * rest_ref[...]
    cross, square = collect_lanes(total[:, rows:], 2)
    norm, shift = known_ref[:, 0:1], known_ref[:, 1:2]
    extra = cross / norm
    alpha = 1.0 / (shift + extra)
    norm_next = alpha * alpha * jnp.maximum(square - extra * cross, 0.0)
    beta = norm_next / norm
    residual = rhs - alpha * image
    direction = residual + beta * rhs
    image_dir = (alpha * extra + beta) * image - alpha * rest_image
    curve_two = row_sum(direction * image_dir)
    field_ref[...] = alpha * rhs
    residual_ref[...] = residual
    direction_ref[...] = direction
    image_dir_ref[...] = image_dir
    norm_ref[...] = jnp.broadcast_to(norm_next, norm_ref.shape)
    curve_ref[...] = jnp.broadcast_to(curve_two, norm_ref.shape).T[: curve_ref.shape[0]]


def finish(curve_ref, other_ref, norm_ref, field_ref, residual_ref, direction_ref, image_dir_ref, *outs):
    cols = curve_ref.shape[1]
    curve = jnp.sum(curve_ref[...] + other_ref[...], axis=0, keepdims=True)
    curve = jnp.concatenate([curve, jnp.ones((1, LANES - cols), jnp.float32)], axis=1)
    curve = jnp.broadcast_to(curve, (LANES, LANES)).T[:cols, 0:1]
    alpha = norm_ref[:, 0:1] / curve
    outs[0][...] = field_ref[...] + alpha * direction_ref[...]
    outs[1][...] = residual_ref[...] - alpha * image_dir_ref[...]


def per_device(points, noise_var, right_side):
    rows, feats = points.shape
    packed, rhs, noisy, noise = run_pack(points, right_side.T, noise_var)
    cols = rhs.shape[0]
    field_shape = ((cols, rows), jnp.float32)
    lanes_shape = ((cols, LANES), jnp.float32)
    side = [packed]
    for k in range(1, SIDE):
        side.append(partner(packed, reach(SIDE_MASKS, k), reach(LINE_MASKS, k)))
    near = exchange([points] * NEAR, NEAR_MASKS)
    own = run_bundle(side, near[1:])
    own_across = partner(own, CORE_MASK)
    first, second = [partner(own, *line_masks(turn)) for turn in (1, 2)]
    near, half = small_call(
        functools.partial(prepare, scale_of(feats)),
        [((feats, NEAR * rows), points.dtype), ((8, NEAR * rows), jnp.float32)],
        packed,
        *near[1:],
    )

    def first_call(far, last, ending=False):
        return run_first(far, near, half, last, rows, cols, ending)

    across = own_across
    half_a, total = first_call([own], None)
    half_b, total = first_call([across], total)
    first, second, total = lax.optimization_barrier((first, second, total))
    third = partner(second, *line_masks(1))
    across = [partner(item, CORE_MASK) for item in (first, second)]
    pair_a, total = first_call([first, across[0]], total)
    pair_b, total = first_call([second, across[1]], total)
    third, total = lax.optimization_barrier((third, total))
    across = partner(third, CORE_MASK)
    half_c, total = first_call([third], total)
    half_d, *parts = first_call([across], total, True)
    skip = SIDE * rows
    own_pieces = [(half_a, 0), (pair_a, 0), (pair_b, 0), (half_c, 0)]
    other_pieces = [(half_b, 0), (pair_a, skip), (pair_b, skip), (half_d, 0)]

    image, rest, known, copies = small_call(
        middle,
        [field_shape, field_shape, lanes_shape, ((CHIPS, cols, rows + LANES), jnp.bfloat16)],
        *exchange(parts, NEAR_MASKS),
        noisy,
        rhs,
    )
    copies = share(copies)
    other = partner(copies, CORE_MASK)
    half_total = run_second(0, own_pieces, copies, rows)[0]
    parts = run_second(1, other_pieces, other, rows, half_total, copies)
    field, residual, direction, image_dir, norm_next, curve = small_call(
        closing,
        [field_shape] * 4 + [lanes_shape, ((DEVICES // 2, cols), jnp.float32)],
        *exchange(parts, NEAR_MASKS),
        noise,
        rhs,
        image,
        rest,
        known,
    )
    curve = lax.all_to_all(curve[:, None, :], "pts", 0, 0, axis_index_groups=core_groups())
    curves = [item.reshape(DEVICES // 2, cols) for item in (curve, partner(curve, CORE_MASK))]
    field, residual = small_call(
        finish, [field_shape] * 2, *curves, norm_next, field, residual, direction, image_dir
    )
    return (field.T, residual.T)


def solution(mesh):
    return jax.shard_map(
        per_device,
        mesh=mesh,
        in_specs=(P("pts", None), P("pts"), P("pts", None)),
        out_specs=(P("pts", None), P("pts", None)),
        check_vma=False,
    )
```

```python
import functools
import math

import jax
import jax.numpy as jnp
from jax import lax
from jax.experimental import pallas as pl
from jax.experimental.pallas import tpu as pltpu
from jax.sharding import PartitionSpec as P

DEVICES = 128
NEAR_MASKS = (10, 2)
SIDE_MASKS = (6, 24)
LINE_MASKS = (32, 64)
CORE_MASK = 1
NEAR = 1 << len(NEAR_MASKS)
SIDE = 1 << len(SIDE_MASKS)
EVEN_LINES = (0, 1, 3, 2)
ODD_LINES = (0, 1, 2, 3)
TURNS = 4
CHIPS = SIDE * TURNS
PAIR = 2
LANES = 128
CHUNK = 512
UNIT = 256
SPLITS = 3
SUMS = 3
LIMIT = 6 * 1024 * 1024
SMALL = 8 * 1024 * 1024
INSIDE = pl.BlockSpec(memory_space=pltpu.VMEM)


def scale_of(feats):
    return 2.0 / feats * math.log2(math.e)


def reach(masks, k):
    mask = 0
    for bit, step in enumerate(masks):
        if (k >> bit) & 1:
            mask ^= step
    return mask


def chip_groups():
    groups, seen = [], set()
    for base in range(DEVICES):
        if base not in seen:
            group = [base ^ reach(SIDE_MASKS + LINE_MASKS, k) for k in range(CHIPS)]
            groups.append(group)
            seen.update(group)
    return groups


def place_in_group(index):
    place = 0
    for bit, mask in enumerate(SIDE_MASKS + LINE_MASKS):
        place += lax.rem(lax.div(index, 1 << (mask.bit_length() - 1)), 2) << bit
    return place


def partner(value, even, odd=None):
    odd = even if odd is None else odd
    pairs = [(k, k ^ (odd if k & CORE_MASK else even)) for k in range(DEVICES)]
    return lax.ppermute(value, "pts", pairs)


def exchange(items, masks):
    return [items[0]] + [partner(items[k], reach(masks, k)) for k in range(1, len(items))]


def line_masks(turn):
    return reach(LINE_MASKS, EVEN_LINES[turn]), reach(SIDE_MASKS, ODD_LINES[turn])


def share(copies):
    return lax.all_to_all(copies, "pts", 0, 0, axis_index_groups=chip_groups())


def small_call(body, shapes, *args):
    return pl.pallas_call(
        body,
        in_specs=[INSIDE] * len(args),
        out_specs=[INSIDE] * len(shapes),
        out_shape=[jax.ShapeDtypeStruct(*shape) for shape in shapes],
        compiler_params=pltpu.CompilerParams(vmem_limit_bytes=SMALL),
    )(*args)


def half_norms(scale, block):
    ones = jnp.ones((8, block.shape[1]), jnp.bfloat16)
    dims = (((1,), (1,)), ((), ()))
    square = jnp.square(block.astype(jnp.float32))
    high = square.astype(jnp.bfloat16)
    low = (square - high.astype(jnp.float32)).astype(jnp.bfloat16)
    total = lax.dot_general(ones, high, dims, preferred_element_type=jnp.float32)
    total += lax.dot_general(ones, low, dims, preferred_element_type=jnp.float32)
    return total * (-0.5 * scale)


def first_product(scale, rows, count, opening, ending, *refs):
    far_refs = refs[:count]
    near_ref, half_ref = refs[count : count + 2]
    kern_ref = refs[count + 2 + (0 if opening else 1)]
    sum_ref = refs[-1]
    sum_ref[...] = jnp.zeros_like(sum_ref) if opening else refs[count + 2][...]
    cols = sum_ref.shape[0]
    width = near_ref.shape[1]
    tall = rows + cols * (rows // near_ref.shape[0])
    units, far, vec, far_half, here = [], [], [], [], []
    for k, ref in enumerate(far_refs):
        for j in range(SIDE):
            sum_ref[:, width:] += ref[j, pl.ds(tall, cols), :].astype(jnp.float32)
        for first in range(0, SIDE, PAIR):
            blocks = range(first, first + PAIR)
            block = jnp.concatenate([ref[j, :rows, :] for j in blocks], axis=0)
            pieces = [ref[j, pl.ds(at, cols), :] for j in blocks for at in range(rows, tall, cols)]
            block_f = block.astype(jnp.float32)
            units += [(len(far), pl.ds(at, UNIT)) for at in range(0, width, UNIT)]
            far.append(block)
            vec.append(jnp.concatenate(pieces, axis=1))
            far_half.append(jnp.sum(block_f * block_f, axis=1, keepdims=True) * (-0.5 * scale))
            here.append(pl.ds((k * SIDE + first) * rows, PAIR * rows))
    cross, tile = {}, {}
    for c in range(len(units) + 2):
        if c < len(units):
            u, part = units[c]
            cross[c] = jnp.dot(far[u], near_ref[:, part], preferred_element_type=jnp.float32)
        if 0 <= c - 1 < len(units):
            u, part = units[c - 1]
            tile[c - 1] = jnp.exp2(
                cross.pop(c - 1) * scale + far_half[u] + half_ref[0:1, part]
            ).astype(jnp.bfloat16)
            kern_ref[here[u], part] = tile[c - 1]
        if 0 <= c - 2 < len(units):
            u, part = units[c - 2]
            sum_ref[:, part] += jnp.dot(
                vec[u], tile.pop(c - 2), preferred_element_type=jnp.float32
            )

    if ending:
        for k, ref in enumerate(refs[-1 - NEAR : -1]):
            ref[:, :rows] = sum_ref[:, pl.ds(k * rows, rows)]
            ref[:, rows:] = sum_ref[:, width:]


def second_product(rows, core, starts, *refs):
    kerns = refs[:TURNS]
    blocks_ref = refs[TURNS]
    vec_ref, total_ref = refs[-2:]
    cols = total_ref.shape[0]
    index = lax.axis_index("pts")
    place = place_in_group(index)
    odd = lax.rem(index, 2)
    for n in range(TURNS):
        for side in range(SIDE):
            even_slot = side + SIDE * EVEN_LINES[n]
            odd_slot = SIDE * side + ODD_LINES[n]
            slot = jnp.bitwise_xor(place, jnp.where(odd == core, even_slot, odd_slot))
            part = pl.ds(side * rows, rows)
            block = blocks_ref[slot].astype(jnp.float32)
            value = block[:, :rows] + collect_lanes(block[:, rows:], SUMS)[-1]
            high = value.astype(jnp.bfloat16)
            vec_ref[n, :cols, part] = high
            vec_ref[n, cols:, part] = (value - high.astype(jnp.float32)).astype(jnp.bfloat16)
    for c in range(total_ref.shape[1] // CHUNK):
        part = pl.ds(c * CHUNK, CHUNK)
        value = jnp.zeros((2 * cols, CHUNK), jnp.float32)
        for n, ref in enumerate(kerns):
            tile = ref[pl.ds(starts[n], SIDE * rows), part]
            value += jnp.dot(vec_ref[n], tile, preferred_element_type=jnp.float32)
        value = value[:cols] + value[cols:]
        if core == 1:
            value += refs[TURNS + 1][:, part]
        total_ref[:, part] = value
    if core == 0:
        refs[-3][...] = total_ref[...]
    else:
        other_ref = refs[TURNS + 2]
        lanes = jnp.zeros((total_ref.shape[0], LANES), jnp.float32)
        for k in range(CHIPS):
            lanes += blocks_ref[k, :, rows:].astype(jnp.float32)
            lanes += other_ref[k, :, rows:].astype(jnp.float32)
        for k, ref in enumerate(refs[TURNS + 3 : TURNS + 3 + NEAR]):
            ref[:, :rows] = total_ref[:, pl.ds(k * rows, rows)]
            ref[:, rows:] = lanes


def run_first(far, near, half, last, rows, cols, ending=False):
    feats, width = near.shape
    opening = last is None
    inputs = list(far) + [near, half] + ([] if opening else [last])
    count = len(far) * SIDE * rows
    running = (cols, width + LANES)
    if ending:
        outs = [jax.ShapeDtypeStruct((cols, rows + LANES), jnp.float32)] * NEAR
        scratch = [pltpu.VMEM(running, jnp.float32)]
    else:
        outs = [jax.ShapeDtypeStruct(running, jnp.float32)]
        scratch = []
    return pl.pallas_call(
        functools.partial(first_product, scale_of(feats), rows, len(far), opening, ending),
        in_specs=[INSIDE] * len(inputs),
        out_specs=[INSIDE] * (1 + len(outs)),
        out_shape=[pltpu.VMEM((count, width), jnp.bfloat16)] + outs,
        scratch_shapes=scratch,
        compiler_params=pltpu.CompilerParams(vmem_limit_bytes=LIMIT),
        cost_estimate=pl.CostEstimate(
            flops=4 * count * width * feats,
            bytes_accessed=2 * count * width,
            transcendentals=count * width,
        ),
    )(*inputs)


def run_second(core, pieces, blocks, rows, *others):
    width = pieces[0][0].shape[1]
    cols = blocks.shape[1]
    starts = [start for _, start in pieces]
    kerns = [pltpu.with_memory_space_constraint(kern, pltpu.VMEM) for kern, _ in pieces]
    inputs = kerns + [blocks] + list(others)
    if core == 0:
        outs = [jax.ShapeDtypeStruct((cols, width), jnp.float32)]
    else:
        outs = [jax.ShapeDtypeStruct((cols, rows + LANES), jnp.float32)] * NEAR
    return pl.pallas_call(
        functools.partial(second_product, rows, core, starts),
        in_specs=[INSIDE] * len(inputs),
        out_specs=[INSIDE] * len(outs),
        out_shape=outs,
        scratch_shapes=[
            pltpu.VMEM((TURNS, 2 * cols, SIDE * rows), jnp.bfloat16),
            pltpu.VMEM((cols, width), jnp.float32),
        ],
        compiler_params=pltpu.CompilerParams(vmem_limit_bytes=LIMIT),
        cost_estimate=pl.CostEstimate(
            flops=2 * TURNS * SIDE * rows * width * 8 * cols,
            bytes_accessed=2 * TURNS * SIDE * rows * width,
            transcendentals=0,
        ),
    )(*inputs)


def spread_lanes(items, shape):
    lane = lax.broadcasted_iota(jnp.int32, shape, 1)
    lanes = jnp.zeros(shape, jnp.float32)
    for k, rest in enumerate(items):
        for j in range(SPLITS):
            piece = rest.astype(jnp.bfloat16).astype(jnp.float32)
            lanes = jnp.where(lane == SPLITS * k + j, piece, lanes)
            rest = rest - piece
    return lanes.astype(jnp.bfloat16)


def collect_lanes(lanes, count):
    lane = lax.broadcasted_iota(jnp.int32, lanes.shape, 1)
    items = []
    for k in range(count):
        inside = (lane >= SPLITS * k) & (lane < SPLITS * (k + 1))
        items.append(jnp.sum(jnp.where(inside, lanes, 0.0), axis=1, keepdims=True))
    return items


def row_sum(value):
    return jnp.sum(value, axis=1, keepdims=True)


def pack(points_ref, rhs_ref, noise_ref, out_ref, keep_ref, noisy_ref, row_ref, line_ref, sems):
    rows, feats = points_ref.shape
    cols = rhs_ref.shape[0]
    first = pltpu.make_async_copy(points_ref, out_ref.at[pl.ds(0, rows), :], sems.at[0])
    second = pltpu.make_async_copy(rhs_ref, keep_ref, sems.at[1])
    third = pltpu.make_async_copy(noise_ref, line_ref, sems.at[2])
    second.start()
    third.start()
    first.start()
    second.wait()
    for k in range(rows // feats):
        part = keep_ref[:, pl.ds(k * feats, feats)]
        out_ref[pl.ds(rows + k * cols, cols), :] = part.astype(jnp.bfloat16)
    rhs = keep_ref[...]
    third.wait()
    noise = line_ref[...].reshape(1, rows)
    row_ref[...] = noise
    noisy = noise * rhs
    noisy_ref[...] = noisy
    lanes = spread_lanes((row_sum(rhs * rhs), row_sum(rhs * noisy)), (cols, LANES))
    out_ref[pl.ds(rows + cols * (rows // feats), cols), :] = lanes
    first.wait()


def outside(value):
    return pltpu.with_memory_space_constraint(value, pltpu.HBM)


def run_pack(points, rhs, noise):
    rows, feats = points.shape
    cols = rhs.shape[0]
    tall = rows + cols * (rows // feats) + cols
    place = pl.BlockSpec(memory_space=pltpu.HBM)
    return pl.pallas_call(
        pack,
        in_specs=[place] * 3,
        out_specs=[INSIDE] * 4,
        out_shape=[
            jax.ShapeDtypeStruct((tall, feats), points.dtype),
            jax.ShapeDtypeStruct(rhs.shape, rhs.dtype),
            jax.ShapeDtypeStruct(rhs.shape, rhs.dtype),
            jax.ShapeDtypeStruct((1, rows), noise.dtype),
        ],
        scratch_shapes=[pltpu.VMEM((rows,), noise.dtype), pltpu.SemaphoreType.DMA((3,))],
        compiler_params=pltpu.CompilerParams(vmem_limit_bytes=SMALL),
    )(outside(points), outside(rhs), outside(noise))


def run_bundle(side, near):
    place = pl.BlockSpec(memory_space=pl.ANY)
    return pl.pallas_call(
        bundle,
        in_specs=[INSIDE] * len(side) + [place] * len(near),
        out_specs=INSIDE,
        out_shape=jax.ShapeDtypeStruct((len(side),) + side[0].shape, side[0].dtype),
        compiler_params=pltpu.CompilerParams(vmem_limit_bytes=SMALL),
    )(*side, *near)


def bundle(*refs):
    for k, ref in enumerate(refs[:SIDE]):
        refs[-1][k] = ref[...]


def prepare(scale, *refs):
    near_ref, half_ref = refs[NEAR:]
    rows = refs[1].shape[0]
    for k, ref in enumerate(refs[:NEAR]):
        block = ref[:rows, :]
        part = pl.ds(k * rows, rows)
        near_ref[:, part] = block.astype(jnp.float32).T.astype(jnp.bfloat16)
        half_ref[:, part] = half_norms(scale, block)


def middle(*refs):
    noisy_ref, rhs_ref, image_ref, rest_ref, known_ref, copies_ref = refs[NEAR:]
    rhs = rhs_ref[...]
    rows = rhs.shape[1]
    total = refs[0][...]
    for ref in refs[1:NEAR]:
        total += ref[...]
    norm, noisy_norm = collect_lanes(total[:, rows:], 2)
    shift = 1.0 + noisy_norm / norm
    image = total[:, :rows] + noisy_ref[...]
    rest = image - shift * rhs
    image_ref[...] = image
    rest_ref[...] = rest
    lane = lax.broadcasted_iota(jnp.int32, known_ref.shape, 1)
    known_ref[...] = jnp.where(lane == 0, norm, shift)
    mean = row_sum(rest) * (1.0 / rows)
    lanes = spread_lanes((row_sum(rhs * rest), row_sum(rest * rest), mean), known_ref.shape)
    packed = jnp.concatenate([(rest - mean).astype(jnp.bfloat16), lanes], axis=1)
    for k in range(copies_ref.shape[0]):
        copies_ref[k] = packed


def closing(*refs):
    noise_ref, rhs_ref, image_ref, rest_ref, known_ref = refs[NEAR : NEAR + 5]
    field_ref, residual_ref, direction_ref, image_dir_ref, norm_ref, curve_ref = refs[NEAR + 5 :]
    rhs = rhs_ref[...]
    image = image_ref[...]
    rows = rhs.shape[1]
    total = refs[0][...]
    for ref in refs[1:NEAR]:
        total += ref[...]
    rest_image = total[:, :rows] + noise_ref[...] * rest_ref[...]
    cross, square = collect_lanes(total[:, rows:], 2)
    norm, shift = known_ref[:, 0:1], known_ref[:, 1:2]
    extra = cross / norm
    alpha = 1.0 / (shift + extra)
    norm_next = alpha * alpha * jnp.maximum(square - extra * cross, 0.0)
    beta = norm_next / norm
    residual = rhs - alpha * image
    direction = residual + beta * rhs
    image_dir = (alpha * extra + beta) * image - alpha * rest_image
    curve_two = row_sum(direction * image_dir)
    field_ref[...] = alpha * rhs
    residual_ref[...] = residual
    direction_ref[...] = direction
    image_dir_ref[...] = image_dir
    norm_ref[...] = jnp.broadcast_to(norm_next, norm_ref.shape)
    curve_ref[...] = jnp.broadcast_to(curve_two, norm_ref.shape).T


def finish(curve_ref, norm_ref, field_ref, residual_ref, direction_ref, image_dir_ref, *outs):
    cols = curve_ref.shape[1]
    curve = jnp.sum(curve_ref[...], axis=0, keepdims=True)
    curve = jnp.concatenate([curve, jnp.ones((1, LANES - cols), jnp.float32)], axis=1)
    curve = jnp.broadcast_to(curve, (LANES, LANES)).T[:cols, 0:1]
    alpha = norm_ref[:, 0:1] / curve
    outs[0][...] = field_ref[...] + alpha * direction_ref[...]
    outs[1][...] = residual_ref[...] - alpha * image_dir_ref[...]


def per_device(points, noise_var, right_side):
    rows, feats = points.shape
    packed, rhs, noisy, noise = run_pack(points, right_side.T, noise_var)
    cols = rhs.shape[0]
    field_shape = ((cols, rows), jnp.float32)
    lanes_shape = ((cols, LANES), jnp.float32)
    side = [packed]
    for k in range(1, SIDE):
        side.append(partner(packed, reach(SIDE_MASKS, k), reach(LINE_MASKS, k)))
    near = exchange([points] * NEAR, NEAR_MASKS)
    own = run_bundle(side, near[1:])
    own_across = partner(own, CORE_MASK)
    first, second = [partner(own, *line_masks(turn)) for turn in (1, 2)]
    near, half = small_call(
        functools.partial(prepare, scale_of(feats)),
        [((feats, NEAR * rows), points.dtype), ((8, NEAR * rows), jnp.float32)],
        packed,
        *near[1:],
    )

    def first_call(far, last, ending=False):
        return run_first(far, near, half, last, rows, cols, ending)

    across = own_across
    half_a, total = first_call([own], None)
    half_b, total = first_call([across], total)
    first, second, total = lax.optimization_barrier((first, second, total))
    third = partner(second, *line_masks(1))
    across = [partner(item, CORE_MASK) for item in (first, second)]
    pair_a, total = first_call([first, across[0]], total)
    pair_b, total = first_call([second, across[1]], total)
    third, total = lax.optimization_barrier((third, total))
    across = partner(third, CORE_MASK)
    half_c, total = first_call([third], total)
    half_d, *parts = first_call([across], total, True)
    skip = SIDE * rows
    own_pieces = [(half_a, 0), (pair_a, 0), (pair_b, 0), (half_c, 0)]
    other_pieces = [(half_b, 0), (pair_a, skip), (pair_b, skip), (half_d, 0)]

    image, rest, known, copies = small_call(
        middle,
        [field_shape, field_shape, lanes_shape, ((CHIPS, cols, rows + LANES), jnp.bfloat16)],
        *exchange(parts, NEAR_MASKS),
        noisy,
        rhs,
    )
    copies = share(copies)
    other = partner(copies, CORE_MASK)
    half_total = run_second(0, own_pieces, copies, rows)[0]
    parts = run_second(1, other_pieces, other, rows, half_total, copies)
    field, residual, direction, image_dir, norm_next, curve = small_call(
        closing,
        [field_shape] * 4 + [lanes_shape, ((DEVICES, cols), jnp.float32)],
        *exchange(parts, NEAR_MASKS),
        noise,
        rhs,
        image,
        rest,
        known,
    )
    curve = lax.all_to_all(curve[:, None, :], "pts", 0, 0).reshape(DEVICES, cols)
    field, residual = small_call(
        finish, [field_shape] * 2, curve, norm_next, field, residual, direction, image_dir
    )
    return (field.T, residual.T)


def solution(mesh):
    return jax.shard_map(
        per_device,
        mesh=mesh,
        in_specs=(P("pts", None), P("pts"), P("pts", None)),
        out_specs=(P("pts", None), P("pts", None)),
        check_vma=False,
    )
```

```python
import functools
import math

import jax
import jax.numpy as jnp
from jax import lax
from jax.experimental import pallas as pl
from jax.experimental.pallas import tpu as pltpu
from jax.sharding import PartitionSpec as P

DEVICES = 128
NEAR_MASKS = (10, 2)
SIDE_MASKS = (6, 24)
LINE_MASKS = (32, 64)
CORE_MASK = 1
NEAR = 1 << len(NEAR_MASKS)
SIDE = 1 << len(SIDE_MASKS)
EVEN_LINES = (0, 1, 3, 2)
ODD_LINES = (0, 1, 2, 3)
TURNS = 4
CHIPS = SIDE * TURNS
PAIR = 2
LANES = 128
CHUNK = 512
UNIT = 256
SPLITS = 3
SUMS = 3
LIMIT = 6 * 1024 * 1024
SMALL = 8 * 1024 * 1024
INSIDE = pl.BlockSpec(memory_space=pltpu.VMEM)


def scale_of(feats):
    return 2.0 / feats * math.log2(math.e)


def reach(masks, k):
    mask = 0
    for bit, step in enumerate(masks):
        if (k >> bit) & 1:
            mask ^= step
    return mask


def chip_groups():
    groups, seen = [], set()
    for base in range(DEVICES):
        if base not in seen:
            group = [base ^ reach(SIDE_MASKS + LINE_MASKS, k) for k in range(CHIPS)]
            groups.append(group)
            seen.update(group)
    return groups


def place_in_group(index):
    place = 0
    for bit, mask in enumerate(SIDE_MASKS + LINE_MASKS):
        place += lax.rem(lax.div(index, 1 << (mask.bit_length() - 1)), 2) << bit
    return place


def partner(value, even, odd=None):
    odd = even if odd is None else odd
    pairs = [(k, k ^ (odd if k & CORE_MASK else even)) for k in range(DEVICES)]
    return lax.ppermute(value, "pts", pairs)


def exchange(items, masks):
    return [items[0]] + [partner(items[k], reach(masks, k)) for k in range(1, len(items))]


def line_masks(turn):
    return reach(LINE_MASKS, EVEN_LINES[turn]), reach(SIDE_MASKS, ODD_LINES[turn])


def share(copies):
    return lax.all_to_all(copies, "pts", 0, 0, axis_index_groups=chip_groups())


def small_call(body, shapes, *args):
    return pl.pallas_call(
        body,
        in_specs=[INSIDE] * len(args),
        out_specs=[INSIDE] * len(shapes),
        out_shape=[jax.ShapeDtypeStruct(*shape) for shape in shapes],
        compiler_params=pltpu.CompilerParams(vmem_limit_bytes=SMALL),
    )(*args)


def half_norms(scale, block):
    ones = jnp.ones((8, block.shape[1]), jnp.bfloat16)
    dims = (((1,), (1,)), ((), ()))
    square = jnp.square(block.astype(jnp.float32))
    high = square.astype(jnp.bfloat16)
    low = (square - high.astype(jnp.float32)).astype(jnp.bfloat16)
    total = lax.dot_general(ones, high, dims, preferred_element_type=jnp.float32)
    total += lax.dot_general(ones, low, dims, preferred_element_type=jnp.float32)
    return total * (-0.5 * scale)


def first_product(scale, rows, count, opening, ending, *refs):
    far_refs = refs[:count]
    near_ref, half_ref = refs[count : count + 2]
    kern_ref = refs[count + 2 + (0 if opening else 1)]
    sum_ref = refs[-1]
    sum_ref[...] = jnp.zeros_like(sum_ref) if opening else refs[count + 2][...]
    cols = sum_ref.shape[0]
    width = near_ref.shape[1]
    tall = rows + cols * (rows // near_ref.shape[0])
    units, far, vec, far_half, here = [], [], [], [], []
    for k, ref in enumerate(far_refs):
        for j in range(SIDE):
            sum_ref[:, width:] += ref[j, pl.ds(tall, cols), :].astype(jnp.float32)
        for first in range(0, SIDE, PAIR):
            blocks = range(first, first + PAIR)
            block = jnp.concatenate([ref[j, :rows, :] for j in blocks], axis=0)
            pieces = [ref[j, pl.ds(at, cols), :] for j in blocks for at in range(rows, tall, cols)]
            block_f = block.astype(jnp.float32)
            units += [(len(far), pl.ds(at, UNIT)) for at in range(0, width, UNIT)]
            far.append(block)
            vec.append(jnp.concatenate(pieces, axis=1))
            far_half.append(jnp.sum(block_f * block_f, axis=1, keepdims=True) * (-0.5 * scale))
            here.append(pl.ds((k * SIDE + first) * rows, PAIR * rows))
    cross, tile = {}, {}
    for c in range(len(units) + 2):
        if c < len(units):
            u, part = units[c]
            cross[c] = jnp.dot(far[u], near_ref[:, part], preferred_element_type=jnp.float32)
        if 0 <= c - 1 < len(units):
            u, part = units[c - 1]
            tile[c - 1] = jnp.exp2(
                cross.pop(c - 1) * scale + far_half[u] + half_ref[0:1, part]
            ).astype(jnp.bfloat16)
            kern_ref[here[u], part] = tile[c - 1]
        if 0 <= c - 2 < len(units):
            u, part = units[c - 2]
            sum_ref[:, part] += jnp.dot(
                vec[u], tile.pop(c - 2), preferred_element_type=jnp.float32
            )

    if ending:
        for k, ref in enumerate(refs[-1 - NEAR : -1]):
            ref[:, :rows] = sum_ref[:, pl.ds(k * rows, rows)]
            ref[:, rows:] = sum_ref[:, width:]


def second_product(rows, core, starts, *refs):
    kerns = refs[:TURNS]
    blocks_ref = refs[TURNS]
    vec_ref, total_ref = refs[-2:]
    cols = total_ref.shape[0]
    index = lax.axis_index("pts")
    place = place_in_group(index)
    odd = lax.rem(index, 2)
    for n in range(TURNS):
        for side in range(SIDE):
            even_slot = side + SIDE * EVEN_LINES[n]
            odd_slot = SIDE * side + ODD_LINES[n]
            slot = jnp.bitwise_xor(place, jnp.where(odd == core, even_slot, odd_slot))
            part = pl.ds(side * rows, rows)
            block = blocks_ref[slot].astype(jnp.float32)
            value = block[:, :rows] + collect_lanes(block[:, rows:], SUMS)[-1]
            high = value.astype(jnp.bfloat16)
            vec_ref[n, :cols, part] = high
            vec_ref[n, cols:, part] = (value - high.astype(jnp.float32)).astype(jnp.bfloat16)
    for c in range(total_ref.shape[1] // CHUNK):
        part = pl.ds(c * CHUNK, CHUNK)
        value = jnp.zeros((2 * cols, CHUNK), jnp.float32)
        for n, ref in enumerate(kerns):
            tile = ref[pl.ds(starts[n], SIDE * rows), part]
            value += jnp.dot(vec_ref[n], tile, preferred_element_type=jnp.float32)
        value = value[:cols] + value[cols:]
        if core == 1:
            value += refs[TURNS + 1][:, part]
        total_ref[:, part] = value
    if core == 0:
        refs[-3][...] = total_ref[...]
    else:
        other_ref = refs[TURNS + 2]
        lanes = jnp.zeros((total_ref.shape[0], LANES), jnp.float32)
        for k in range(CHIPS):
            lanes += blocks_ref[k, :, rows:].astype(jnp.float32)
            lanes += other_ref[k, :, rows:].astype(jnp.float32)
        for k, ref in enumerate(refs[TURNS + 3 : TURNS + 3 + NEAR]):
            ref[:, :rows] = total_ref[:, pl.ds(k * rows, rows)]
            ref[:, rows:] = lanes


def run_first(far, near, half, last, rows, cols, ending=False):
    feats, width = near.shape
    opening = last is None
    inputs = list(far) + [near, half] + ([] if opening else [last])
    count = len(far) * SIDE * rows
    running = (cols, width + LANES)
    if ending:
        outs = [jax.ShapeDtypeStruct((cols, rows + LANES), jnp.float32)] * NEAR
        scratch = [pltpu.VMEM(running, jnp.float32)]
    else:
        outs = [jax.ShapeDtypeStruct(running, jnp.float32)]
        scratch = []
    return pl.pallas_call(
        functools.partial(first_product, scale_of(feats), rows, len(far), opening, ending),
        in_specs=[INSIDE] * len(inputs),
        out_specs=[INSIDE] * (1 + len(outs)),
        out_shape=[pltpu.VMEM((count, width), jnp.bfloat16)] + outs,
        scratch_shapes=scratch,
        compiler_params=pltpu.CompilerParams(vmem_limit_bytes=LIMIT),
        cost_estimate=pl.CostEstimate(
            flops=4 * count * width * feats,
            bytes_accessed=2 * count * width,
            transcendentals=count * width,
        ),
    )(*inputs)


def run_second(core, pieces, blocks, rows, *others):
    width = pieces[0][0].shape[1]
    cols = blocks.shape[1]
    starts = [start for _, start in pieces]
    kerns = [pltpu.with_memory_space_constraint(kern, pltpu.VMEM) for kern, _ in pieces]
    inputs = kerns + [blocks] + list(others)
    if core == 0:
        outs = [jax.ShapeDtypeStruct((cols, width), jnp.float32)]
    else:
        outs = [jax.ShapeDtypeStruct((cols, rows + LANES), jnp.float32)] * NEAR
    return pl.pallas_call(
        functools.partial(second_product, rows, core, starts),
        in_specs=[INSIDE] * len(inputs),
        out_specs=[INSIDE] * len(outs),
        out_shape=outs,
        scratch_shapes=[
            pltpu.VMEM((TURNS, 2 * cols, SIDE * rows), jnp.bfloat16),
            pltpu.VMEM((cols, width), jnp.float32),
        ],
        compiler_params=pltpu.CompilerParams(vmem_limit_bytes=LIMIT),
        cost_estimate=pl.CostEstimate(
            flops=2 * TURNS * SIDE * rows * width * 8 * cols,
            bytes_accessed=2 * TURNS * SIDE * rows * width,
            transcendentals=0,
        ),
    )(*inputs)


def spread_lanes(items, shape):
    lane = lax.broadcasted_iota(jnp.int32, shape, 1)
    lanes = jnp.zeros(shape, jnp.float32)
    for k, rest in enumerate(items):
        for j in range(SPLITS):
            piece = rest.astype(jnp.bfloat16).astype(jnp.float32)
            lanes = jnp.where(lane == SPLITS * k + j, piece, lanes)
            rest = rest - piece
    return lanes.astype(jnp.bfloat16)


def collect_lanes(lanes, count):
    lane = lax.broadcasted_iota(jnp.int32, lanes.shape, 1)
    items = []
    for k in range(count):
        inside = (lane >= SPLITS * k) & (lane < SPLITS * (k + 1))
        items.append(jnp.sum(jnp.where(inside, lanes, 0.0), axis=1, keepdims=True))
    return items


def row_sum(value):
    return jnp.sum(value, axis=1, keepdims=True)


def pack(points_ref, rhs_ref, noise_ref, out_ref, keep_ref, noisy_ref, row_ref, line_ref, sems):
    rows, feats = points_ref.shape
    cols = rhs_ref.shape[0]
    first = pltpu.make_async_copy(points_ref, out_ref.at[pl.ds(0, rows), :], sems.at[0])
    second = pltpu.make_async_copy(rhs_ref, keep_ref, sems.at[1])
    third = pltpu.make_async_copy(noise_ref, line_ref, sems.at[2])
    second.start()
    third.start()
    first.start()
    second.wait()
    for k in range(rows // feats):
        part = keep_ref[:, pl.ds(k * feats, feats)]
        out_ref[pl.ds(rows + k * cols, cols), :] = part.astype(jnp.bfloat16)
    rhs = keep_ref[...]
    third.wait()
    noise = line_ref[...].reshape(1, rows)
    row_ref[...] = noise
    noisy = noise * rhs
    noisy_ref[...] = noisy
    lanes = spread_lanes((row_sum(rhs * rhs), row_sum(rhs * noisy)), (cols, LANES))
    out_ref[pl.ds(rows + cols * (rows // feats), cols), :] = lanes
    first.wait()


def outside(value):
    return pltpu.with_memory_space_constraint(value, pltpu.HBM)


def run_pack(points, rhs, noise):
    rows, feats = points.shape
    cols = rhs.shape[0]
    tall = rows + cols * (rows // feats) + cols
    place = pl.BlockSpec(memory_space=pltpu.HBM)
    return pl.pallas_call(
        pack,
        in_specs=[place] * 3,
        out_specs=[INSIDE] * 4,
        out_shape=[
            jax.ShapeDtypeStruct((tall, feats), points.dtype),
            jax.ShapeDtypeStruct(rhs.shape, rhs.dtype),
            jax.ShapeDtypeStruct(rhs.shape, rhs.dtype),
            jax.ShapeDtypeStruct((1, rows), noise.dtype),
        ],
        scratch_shapes=[pltpu.VMEM((rows,), noise.dtype), pltpu.SemaphoreType.DMA((3,))],
        compiler_params=pltpu.CompilerParams(vmem_limit_bytes=SMALL),
    )(outside(points), outside(rhs), outside(noise))


def run_bundle(side, near):
    place = pl.BlockSpec(memory_space=pl.ANY)
    return pl.pallas_call(
        bundle,
        in_specs=[INSIDE] * len(side) + [place] * len(near),
        out_specs=INSIDE,
        out_shape=jax.ShapeDtypeStruct((len(side),) + side[0].shape, side[0].dtype),
        compiler_params=pltpu.CompilerParams(vmem_limit_bytes=SMALL),
    )(*side, *near)


def bundle(*refs):
    for k, ref in enumerate(refs[:SIDE]):
        refs[-1][k] = ref[...]


def prepare(scale, *refs):
    near_ref, half_ref = refs[NEAR:]
    rows = refs[1].shape[0]
    for k, ref in enumerate(refs[:NEAR]):
        block = ref[:rows, :]
        part = pl.ds(k * rows, rows)
        near_ref[:, part] = block.astype(jnp.float32).T.astype(jnp.bfloat16)
        half_ref[:, part] = half_norms(scale, block)


def middle(*refs):
    noisy_ref, rhs_ref, image_ref, rest_ref, known_ref, copies_ref = refs[NEAR:]
    rhs = rhs_ref[...]
    rows = rhs.shape[1]
    total = refs[0][...]
    for ref in refs[1:NEAR]:
        total += ref[...]
    norm, noisy_norm = collect_lanes(total[:, rows:], 2)
    shift = 1.0 + noisy_norm / norm
    image = total[:, :rows] + noisy_ref[...]
    rest = image - shift * rhs
    image_ref[...] = image
    rest_ref[...] = rest
    lane = lax.broadcasted_iota(jnp.int32, known_ref.shape, 1)
    known_ref[...] = jnp.where(lane == 0, norm, shift)
    mean = row_sum(rest) * (1.0 / rows)
    lanes = spread_lanes((row_sum(rhs * rest), row_sum(rest * rest), mean), known_ref.shape)
    packed = jnp.concatenate([(rest - mean).astype(jnp.bfloat16), lanes], axis=1)
    for k in range(copies_ref.shape[0]):
        copies_ref[k] = packed


def closing(*refs):
    noise_ref, rhs_ref, image_ref, rest_ref, known_ref = refs[NEAR : NEAR + 5]
    field_ref, residual_ref, direction_ref, image_dir_ref, norm_ref, curve_ref = refs[NEAR + 5 :]
    rhs = rhs_ref[...]
    image = image_ref[...]
    rows = rhs.shape[1]
    total = refs[0][...]
    for ref in refs[1:NEAR]:
        total += ref[...]
    rest_image = total[:, :rows] + noise_ref[...] * rest_ref[...]
    cross, square = collect_lanes(total[:, rows:], 2)
    norm, shift = known_ref[:, 0:1], known_ref[:, 1:2]
    extra = cross / norm
    alpha = 1.0 / (shift + extra)
    norm_next = alpha * alpha * jnp.maximum(square - extra * cross, 0.0)
    beta = norm_next / norm
    residual = rhs - alpha * image
    direction = residual + beta * rhs
    image_dir = (alpha * extra + beta) * image - alpha * rest_image
    curve_two = row_sum(direction * image_dir)
    field_ref[...] = alpha * rhs
    residual_ref[...] = residual
    direction_ref[...] = direction
    image_dir_ref[...] = image_dir
    norm_ref[...] = jnp.broadcast_to(norm_next, norm_ref.shape)
    curve_ref[...] = jnp.broadcast_to(curve_two, norm_ref.shape).T


def finish(curve_ref, norm_ref, field_ref, residual_ref, direction_ref, image_dir_ref, *outs):
    cols = curve_ref.shape[1]
    curve = jnp.sum(curve_ref[...], axis=0, keepdims=True)
    curve = jnp.concatenate([curve, jnp.ones((1, LANES - cols), jnp.float32)], axis=1)
    curve = jnp.broadcast_to(curve, (LANES, LANES)).T[:cols, 0:1]
    alpha = norm_ref[:, 0:1] / curve
    outs[0][...] = field_ref[...] + alpha * direction_ref[...]
    outs[1][...] = residual_ref[...] - alpha * image_dir_ref[...]


def per_device(points, noise_var, right_side):
    rows, feats = points.shape
    packed, rhs, noisy, noise = run_pack(points, right_side.T, noise_var)
    cols = rhs.shape[0]
    field_shape = ((cols, rows), jnp.float32)
    lanes_shape = ((cols, LANES), jnp.float32)
    side = [packed]
    for k in range(1, SIDE):
        side.append(partner(packed, reach(SIDE_MASKS, k), reach(LINE_MASKS, k)))
    near = exchange([points] * NEAR, NEAR_MASKS)
    own = run_bundle(side, near[1:2])
    own_across = partner(own, CORE_MASK)
    first, second = [partner(own, *line_masks(turn)) for turn in (1, 2)]
    near, half = small_call(
        functools.partial(prepare, scale_of(feats)),
        [((feats, NEAR * rows), points.dtype), ((8, NEAR * rows), jnp.float32)],
        packed,
        *near[1:],
    )

    def first_call(far, last, ending=False):
        return run_first(far, near, half, last, rows, cols, ending)

    across = own_across
    half_a, total = first_call([own], None)
    half_b, total = first_call([across], total)
    first, second, total = lax.optimization_barrier((first, second, total))
    third = partner(second, *line_masks(1))
    across = [partner(item, CORE_MASK) for item in (first, second)]
    pair_a, total = first_call([first, across[0]], total)
    pair_b, total = first_call([second, across[1]], total)
    third, total = lax.optimization_barrier((third, total))
    across = partner(third, CORE_MASK)
    half_c, total = first_call([third], total)
    half_d, *parts = first_call([across], total, True)
    skip = SIDE * rows
    own_pieces = [(half_a, 0), (pair_a, 0), (pair_b, 0), (half_c, 0)]
    other_pieces = [(half_b, 0), (pair_a, skip), (pair_b, skip), (half_d, 0)]

    image, rest, known, copies = small_call(
        middle,
        [field_shape, field_shape, lanes_shape, ((CHIPS, cols, rows + LANES), jnp.bfloat16)],
        *exchange(parts, NEAR_MASKS),
        noisy,
        rhs,
    )
    copies = share(copies)
    other = partner(copies, CORE_MASK)
    half_total = run_second(0, own_pieces, copies, rows)[0]
    parts = run_second(1, other_pieces, other, rows, half_total, copies)
    field, residual, direction, image_dir, norm_next, curve = small_call(
        closing,
        [field_shape] * 4 + [lanes_shape, ((DEVICES, cols), jnp.float32)],
        *exchange(parts, NEAR_MASKS),
        noise,
        rhs,
        image,
        rest,
        known,
    )
    curve = lax.all_to_all(curve[:, None, :], "pts", 0, 0).reshape(DEVICES, cols)
    field, residual = small_call(
        finish, [field_shape] * 2, curve, norm_next, field, residual, direction, image_dir
    )
    return (field.T, residual.T)


def solution(mesh):
    return jax.shard_map(
        per_device,
        mesh=mesh,
        in_specs=(P("pts", None), P("pts"), P("pts", None)),
        out_specs=(P("pts", None), P("pts", None)),
        check_vma=False,
    )
```
